32 devices in a mesh: fsdp: 32 (over z, y, x, core).
Axes of the slice: x: 2, y: 2, z: 4, core: 2. Of those that a mesh axis runs over, the one named last changes fastest.
Arguments:
- tokens: bfloat16 [4096, 2048], P('fsdp'), may hold values from -6 to 6
- segments: int32 [4096], P('fsdp'), may hold values from 0 to 3, as said below
- positions: int32 [4096], P('fsdp'), may hold values from 0 to 2047
- gain_attn: bfloat16 [2048], P('fsdp'), may hold values from 0.5 to 1.5
- w_query: bfloat16 [2048, 2048], P('fsdp'), may hold values from -0.125 to 0.125
- w_key: bfloat16 [2048, 2048], P('fsdp'), may hold values from -0.125 to 0.125
- w_value: bfloat16 [2048, 2048], P('fsdp'), may hold values from -0.125 to 0.125
- w_out: bfloat16 [2048, 2048], P('fsdp'), may hold values from -0.75 to 0.75
- gain_mlp: bfloat16 [2048], P('fsdp'), may hold values from 0.5 to 1.5
- w_gate: bfloat16 [2048, 8192], P('fsdp'), may hold values from -0.125 to 0.125
- w_up: bfloat16 [2048, 8192], P('fsdp'), may hold values from -0.125 to 0.125
- w_down: bfloat16 [8192, 2048], P('fsdp'), may hold values from -0.0625 to 0.0625
- cotangent: bfloat16 [4096, 2048], P('fsdp'), may hold values from -6 to 6
Outputs:
- result: bfloat16 [4096, 2048], P('fsdp')
- grad_tokens: float32 [4096, 2048], P('fsdp')
- grad_gain_attn: float32 [2048], P('fsdp')
- grad_w_query: float32 [2048, 2048], P('fsdp')
- grad_w_key: float32 [2048, 2048], P('fsdp')
- grad_w_value: float32 [2048, 2048], P('fsdp')
- grad_w_out: float32 [2048, 2048], P('fsdp')
- grad_gain_mlp: float32 [2048], P('fsdp')
- grad_w_gate: float32 [2048, 8192], P('fsdp')
- grad_w_up: float32 [2048, 8192], P('fsdp')
- grad_w_down: float32 [8192, 2048], P('fsdp')
The draws below stay inside these ranges and needn't reach their ends.
Inputs may be any that keep to these rules, and one draw needn't show every extreme that they name: `segments`: segment numbers never fall along the token rows and never continue across a sequence boundary; each document has 1 to 1984 tokens and one has exactly 1984.
All inputs are finite; a program needn't handle non-finite values.
Results may differ from the reference program's by a relative error of at most 0.014.
Values may be sent and summed in bfloat16 or wider, within the bound.
No kernel may reach another device: no remote copies, remote signals or barrier semaphores. Data moves between devices by JAX's collectives and lax.ppermute only.
A program may use at most 704 MiB of HBM per device.

```python
import jax
import jax.numpy as jnp
from jax import lax

D = 2048
HEADS = 32
HEAD_DIM = 64
FF = 8192
TOK_DEV = 128
SEQ = 2048
TOKENS = 4096
SEQS = 2


def draw_segments(key, part):
    key = jax.random.fold_in(key, 11)
    key_first, key_pick = jax.random.split(key)
    first = jax.random.randint(key_first, (SEQS,), TOK_DEV // 2, TOK_DEV)
    picked = jax.random.randint(key_pick, (), 0, SEQS)
    order = jnp.arange(SEQS, dtype=jnp.int32)
    first = jnp.where(order == picked, TOK_DEV // 2, first)
    place = jnp.arange(SEQ, dtype=jnp.int32)
    later = (place[None, :] >= first[:, None]).astype(jnp.int32)
    return (2 * order[:, None] + later).reshape(TOKENS).astype(jnp.int32)


def set_ends(array, stream_key, smallest, high):
    spot = [jax.random.randint(jax.random.fold_in(stream_key, axis), (), 0, length) for axis, length in enumerate(array.shape)]
    longest = array.shape.index(max(array.shape))
    beside = spot[:longest] + [(spot[longest] + 1) % array.shape[longest]] + spot[longest + 1:]
    return array.at[tuple(spot)].set(smallest).at[tuple(beside)].set(high)


def raised(array, stream_key, source, target, shards_of, factor):
    owner, partner = [(jnp.arange(array.shape[axis_at]) // (array.shape[axis_at] // shards_of)).reshape([-1 if axis == axis_at else 1 for axis in range(array.ndim)]) for axis_at in (source, target)]
    chosen = jax.random.permutation(stream_key, shards_of)[partner]
    strong = (owner == chosen) | (owner == (partner + shards_of // 2) % shards_of)
    return jnp.where(strong, factor * array, array)


def shard_levels(key, dims, cuts, low, largest):
    level = 1.0
    for dim, blocks in cuts:
        draws = jax.random.uniform(jax.random.fold_in(jax.random.fold_in(key, 6), dim), (blocks,), jnp.float32, low / len(cuts), largest / len(cuts))
        level = level * jnp.repeat(jnp.exp(draws), dims[dim] // blocks).reshape((-1,) + (1,) * (len(dims) - 1 - dim))
    return level


def centred(stream_key, shape, spread, bound, shards=(), held_as=jnp.bfloat16):
    drawn = spread * jax.random.normal(stream_key, shape, jnp.float32)
    if shards:
        drawn = drawn * shard_levels(stream_key, shape, shards, -0.22, 0.18)
    return jnp.clip(drawn, -bound, bound).astype(held_as)


def bell_draw_with(key, extent, width, reach, pieces, heavy, kind=jnp.bfloat16):
    entries = width * jax.random.normal(key, extent, jnp.float32)
    if pieces:
        entries = entries * shard_levels(key, extent, pieces, -0.22, 0.18)
    return jnp.clip(raised(entries, jax.random.fold_in(key, 3), *heavy), -reach, reach).astype(kind)


def setup_inputs(seed: int = 0) -> dict:
    splits = jax.random.split(jax.random.key(seed), 14)
    tokens = bell_draw_with(splits[0], (TOKENS, D), 1.0, 6.0, ((0, 32),), (0, 1, 32, 2.75))
    segments = draw_segments(jax.random.fold_in(splits[13], 71), 0)
    positions = set_ends(jax.random.randint(splits[2], (TOKENS,), 0, SEQ), jax.random.fold_in(splits[2], 1), 0, SEQ - 1).astype(jnp.int32)
    gain_attn = jnp.clip(1.0 + 0.1 * jax.random.normal(splits[3], (D,), jnp.float32), 0.5, 1.5).astype(jnp.bfloat16)
    w_query = centred(splits[4], (D, D), D ** -0.5, 0.125, ((0, 32),))
    w_key = centred(splits[5], (D, D), D ** -0.5, 0.125, ((0, 32),))
    w_value = centred(splits[6], (D, D), D ** -0.5, 0.125, ((0, 32),))
    w_out = centred(splits[7], (D, D), (D // 32) ** -0.5, 0.75, ((0, 32),))
    gain_mlp = jnp.clip(1.0 + 0.1 * jax.random.normal(splits[8], (D,), jnp.float32), 0.5, 1.5).astype(jnp.bfloat16)
    w_gate = centred(splits[9], (D, FF), D ** -0.5, 0.125, ((0, 32),))
    w_up = centred(splits[10], (D, FF), D ** -0.5, 0.125, ((0, 32),))
    w_down = centred(splits[11], (FF, D), FF ** -0.5, 0.0625, ((0, 32),))
    cotangent = centred(splits[12], (TOKENS, D), 1.0, 6.0, ((0, 32),))
    return {"tokens": tokens, "segments": segments, "positions": positions, "gain_attn": gain_attn, "w_query": w_query, "w_key": w_key, "w_value": w_value, "w_out": w_out, "gain_mlp": gain_mlp, "w_gate": w_gate, "w_up": w_up, "w_down": w_down, "cotangent": cotangent}


EPS = 1e-05
THETA = 130000.0
NEG = -1e+30
HIGH = lax.Precision.HIGHEST

@jax.custom_vjp
def low(v):
    return lax.optimization_barrier(v.astype(jnp.bfloat16)).astype(jnp.float32)

@jax.custom_vjp
def low_back(v):
    return v

def low_keep(v):
    return (low(v), None)

def low_pass(kept, grad):
    return (grad,)

def back_keep(v):
    return (v, None)

def back_low(kept, grad):
    return (low(grad),)
low.defvjp(low_keep, low_pass)
low_back.defvjp(back_keep, back_low)

def norm_rows(v, gain):
    scale = lax.rsqrt(lax.optimization_barrier(jnp.mean(v * v, axis=-1, keepdims=True)) + EPS)
    return v * scale * gain

def rotate(v, positions):
    half = v.shape[-1] // 2
    freqs = THETA ** (-jnp.arange(half, dtype=jnp.float32) * 2.0 / v.shape[-1])
    angles = positions.astype(jnp.float32)[:, None] * freqs[None, :]
    cosine = jnp.cos(angles)[:, None, :]
    sine = jnp.sin(angles)[:, None, :]
    first = v[..., :half]
    second = v[..., half:]
    return jnp.concatenate([first * cosine - second * sine, second * cosine + first * sine], axis=-1)

def attend_block(query, keys, values, valid):
    scale = query.shape[-1] ** (-0.5)
    scores = low_back(jnp.einsum('qhd,khd->hqk', query, keys, precision=HIGH) * scale)
    scores = jnp.where(valid[None], scores, NEG)
    top = lax.optimization_barrier(jnp.max(scores, axis=-1, keepdims=True))
    expd = jnp.where(valid[None], jnp.exp(scores - top), 0.0)
    probs = expd / lax.optimization_barrier(jnp.sum(expd, axis=-1, keepdims=True))
    return jnp.einsum('hqk,khd->qhd', low(probs), values, precision=HIGH)

def attend_sequence(query, keys, values, docs):
    length = query.shape[0]
    order = jnp.arange(length, dtype=jnp.int32)
    valid = (docs[:, None] == docs[None, :]) & (order[:, None] >= order[None, :])
    group = min(8, HEADS)
    count = HEADS // group

    def split(v):
        return v.reshape(length, count, group, HEAD_DIM).transpose(1, 0, 2, 3)

    def one_group(item):
        return attend_block(item[0], item[1], item[2], valid)
    out = lax.map(jax.checkpoint(one_group), (split(query), split(keys), split(values)))
    return out.transpose(1, 0, 2, 3).reshape(length, HEADS * HEAD_DIM)

def attention(query, keys, values, segments):

    def one_sequence(item):
        return attend_sequence(item[0], item[1], item[2], item[3])
    shaped = (query.reshape(SEQS, SEQ, HEADS, HEAD_DIM), keys.reshape(SEQS, SEQ, HEADS, HEAD_DIM), values.reshape(SEQS, SEQ, HEADS, HEAD_DIM), segments.reshape(SEQS, SEQ))
    out = lax.map(jax.checkpoint(one_sequence), shaped)
    return out.reshape(TOKENS, D)

def reference(tokens, segments, positions, gain_attn, w_query, w_key, w_value, w_out, gain_mlp, w_gate, w_up, w_down, cotangent):

    def layer(x, gain_one, wq, wk, wv, wo, gain_two, wg, wu, wd):
        h1 = low(norm_rows(x, gain_one))
        qp = low_back(jnp.dot(h1, wq, precision=HIGH)).reshape(TOKENS, HEADS, HEAD_DIM)
        kp = low_back(jnp.dot(h1, wk, precision=HIGH)).reshape(TOKENS, HEADS, HEAD_DIM)
        query = low(rotate(qp, positions))
        keys = low(rotate(kp, positions))
        values = low(low_back(jnp.dot(h1, wv, precision=HIGH))).reshape(TOKENS, HEADS, HEAD_DIM)
        out = low(low_back(attention(query, keys, values, segments)))
        x2 = x + low_back(jnp.dot(out, wo, precision=HIGH))
        h2 = low(norm_rows(x2, gain_two))
        gate = low_back(jnp.dot(h2, wg, precision=HIGH))
        up = low_back(jnp.dot(h2, wu, precision=HIGH))
        mixed = low(jax.nn.silu(gate) * up)
        return x2 + low_back(jnp.dot(mixed, wd, precision=HIGH))
    primals = (tokens.astype(jnp.float32), gain_attn.astype(jnp.float32), w_query.astype(jnp.float32), w_key.astype(jnp.float32), w_value.astype(jnp.float32), w_out.astype(jnp.float32), gain_mlp.astype(jnp.float32), w_gate.astype(jnp.float32), w_up.astype(jnp.float32), w_down.astype(jnp.float32))
    output, pullback = jax.vjp(layer, *primals)
    grads = pullback(cotangent.astype(jnp.float32))
    return (output.astype(jnp.bfloat16), grads[0], grads[1], grads[2], grads[3], grads[4], grads[5], grads[6], grads[7], grads[8], grads[9])
```

```python
import jax
import jax.numpy as jnp
from jax import lax
from jax.sharding import PartitionSpec as P

HEADS = 32
HEAD_DIM = 64
SEQ = 2048


EPS = 1e-05
THETA = 130000.0
NEG = -1e30
BF = jnp.bfloat16


def norm_rows(v, gain):
    scale = lax.rsqrt(jnp.mean(v * v, axis=-1, keepdims=True) + EPS)
    return v * scale * gain


def norm_back(v, gain, grad):
    scale = lax.rsqrt(jnp.mean(v * v, axis=-1, keepdims=True) + EPS)
    hat = v * scale
    weighted = gain * grad
    back = scale * (weighted - hat * jnp.mean(hat * weighted, axis=-1, keepdims=True))
    return back, jnp.sum(grad * hat, axis=0)


def matmul(left, right):
    return jnp.dot(left, right, preferred_element_type=jnp.float32)


def times_t(left, right):
    return lax.dot_general(
        left, right, (((1,), (1,)), ((), ())), preferred_element_type=jnp.float32
    )


def t_times(left, right):
    return lax.dot_general(
        left, right, (((0,), (0,)), ((), ())), preferred_element_type=jnp.float32
    )


def rotate(v, cosine, sine):
    rows, width = v.shape
    v = v.reshape(rows, width // HEAD_DIM, 2, HEAD_DIM // 2)
    first, second = v[:, :, 0], v[:, :, 1]
    cosine, sine = cosine[:, None], sine[:, None]
    turned = jnp.stack([first * cosine - second * sine, second * cosine + first * sine], axis=2)
    return turned.reshape(rows, width)


def heads_first(v):
    return v.reshape(v.shape[0], -1, HEAD_DIM).transpose(1, 0, 2)


def heads_last(v):
    return v.transpose(1, 0, 2).reshape(v.shape[1], -1)


def attend_forward(query, keys, values, valid):
    query, keys, values = heads_first(query), heads_first(keys), heads_first(values)
    scores = jnp.einsum("hqd,hkd->hqk", query, keys, preferred_element_type=jnp.float32)
    scores = jnp.where(valid[None], scores * HEAD_DIM**-0.5, NEG)
    top = jnp.max(scores, axis=-1, keepdims=True)
    expd = jnp.exp(scores - top)
    total = jnp.sum(expd, axis=-1, keepdims=True)
    probs = (expd / total).astype(BF)
    out = jnp.einsum("hqk,hkd->hqd", probs, values, preferred_element_type=jnp.float32)
    return heads_last(out), top + jnp.log(total)


def attend_backward(query, keys, values, grad_out, logsum, valid):
    query, keys, values, grad_out = (heads_first(v) for v in (query, keys, values, grad_out))
    scale = HEAD_DIM**-0.5
    scores = jnp.einsum("hqd,hkd->hqk", query, keys, preferred_element_type=jnp.float32)
    probs = jnp.where(valid[None], jnp.exp(scores * scale - logsum), 0.0)
    dprob = jnp.einsum("hqd,hkd->hqk", grad_out, values, preferred_element_type=jnp.float32)
    delta = jnp.sum(probs * dprob, axis=-1, keepdims=True)
    dscore = (probs * (dprob - delta)).astype(BF)
    dquery = jnp.einsum("hqk,hkd->hqd", dscore, keys, preferred_element_type=jnp.float32) * scale
    dkeys = jnp.einsum("hqk,hqd->hkd", dscore, query, preferred_element_type=jnp.float32) * scale
    dvalues = jnp.einsum(
        "hqk,hqd->hkd", probs.astype(BF), grad_out, preferred_element_type=jnp.float32
    )
    return heads_last(dquery), heads_last(dkeys), heads_last(dvalues)


def local(
    tokens,
    segments,
    positions,
    gain_attn,
    w_query,
    w_key,
    w_value,
    w_out,
    gain_mlp,
    w_gate,
    w_up,
    w_down,
    cotangent,
):
    rows, width = tokens.shape
    team = SEQ // rows
    count = lax.axis_size("fsdp")
    teams = count // team
    index = lax.axis_index("fsdp")
    mine = index // team
    place = index % team
    groups = [[t * team + p for p in range(team)] for t in range(teams)]
    own = w_query.shape[0]
    head_cuts = teams if own % HEAD_DIM == 0 else 1
    ff_own = w_down.shape[0]

    def gather(v):
        return lax.all_gather(v, "fsdp", axis=0, tiled=True, axis_index_groups=groups)

    def scatter(v):
        return lax.psum_scatter(
            v, "fsdp", scatter_dimension=0, tiled=True, axis_index_groups=groups
        )

    def exchange(v):
        return lax.all_to_all(v, "fsdp", 0, 0, tiled=True, axis_index_groups=groups)

    def to_team(v, ahead):
        return lax.ppermute(
            v, "fsdp", [(i, (i + ahead * team) % count) for i in range(count)]
        )

    def across(v):
        held = jnp.zeros((teams,) + v.shape, v.dtype)
        held = lax.dynamic_update_index_in_dim(held, v, mine, 0)
        for ahead in range(1, teams):
            held = lax.dynamic_update_index_in_dim(
                held, to_team(v, ahead), (mine - ahead) % teams, 0
            )
        return held

    def sum_across(v):
        total = lax.dynamic_index_in_dim(v, mine, 0, keepdims=False)
        for ahead in range(1, teams):
            sent = lax.dynamic_index_in_dim(v, (mine + ahead) % teams, 0, keepdims=False)
            total = total + to_team(sent.astype(BF), ahead).astype(jnp.float32)
        return total

    def cut_columns(w, cuts):
        r, c = w.shape
        return w.reshape(r, cuts, team, -1).transpose(2, 0, 1, 3).reshape(team, r, c // team)

    def join_columns(v, cuts):
        _, r, c = v.shape
        return v.reshape(team, r, cuts, -1).transpose(1, 2, 0, 3).reshape(r, c * team)

    def columns_of(weights, cuts):
        cut = jnp.concatenate([cut_columns(w, cuts) for w in weights], axis=2)
        block = exchange(cut)
        full = across(block.reshape(-1, block.shape[2]))
        return full.reshape(-1, block.shape[2])

    def rows_of(grad, parts, cuts):
        grad = sum_across(grad.reshape(teams, -1, grad.shape[1])).astype(BF)
        got = exchange(grad.reshape(team, -1, grad.shape[1]))
        each = got.shape[2] // parts
        return [
            join_columns(got[:, :, i * each : (i + 1) * each], cuts).astype(jnp.float32)
            for i in range(parts)
        ]

    small = jnp.concatenate(
        [v.astype(jnp.float32) for v in (gain_attn, gain_mlp, segments, positions)]
    )
    small = lax.all_gather(small, "fsdp", axis=0)
    gain_one = small[:, :own].reshape(1, -1)
    gain_two = small[:, own : 2 * own].reshape(1, -1)
    small = lax.dynamic_slice_in_dim(small, mine * team, team, 0)
    docs = small[:, 2 * own : 2 * own + rows].reshape(-1)
    places = small[:, 2 * own + rows :].reshape(-1)

    x_all = gather(tokens)
    w_qkv = columns_of([w_query, w_key, w_value], head_cuts)
    dy_all = gather(cotangent)
    w_gu = columns_of([w_gate, w_up], teams)
    if head_cuts == teams:
        out_rows = across(w_out).reshape(-1, width)
    else:
        out_rows = lax.dynamic_slice_in_dim(
            lax.all_gather(w_out, "fsdp", axis=0, tiled=True), place * (width // team), width // team
        )
    down_rows = across(w_down).reshape(-1, width)

    freqs = THETA ** (-jnp.arange(HEAD_DIM // 2, dtype=jnp.float32) * 2.0 / HEAD_DIM)
    angles = places[:, None] * freqs[None, :]
    cosine, sine = jnp.cos(angles), jnp.sin(angles)
    order = jnp.arange(SEQ, dtype=jnp.int32)
    valid = (docs[:, None] == docs[None, :]) & (order[:, None] >= order[None, :])

    h1 = norm_rows(x_all.astype(jnp.float32), gain_one).astype(BF)
    qkv = matmul(h1, w_qkv)
    each = qkv.shape[1] // 3
    query = rotate(qkv[:, :each], cosine, sine).astype(BF)
    keys = rotate(qkv[:, each : 2 * each], cosine, sine).astype(BF)
    values = qkv[:, 2 * each :].astype(BF)
    out, logsum = attend_forward(query, keys, values, valid)
    out = out.astype(BF)
    x = tokens.astype(jnp.float32)
    x2 = x + scatter(matmul(out, out_rows).astype(BF)).astype(jnp.float32)
    h2 = gather(norm_rows(x2, gain_two).astype(BF))
    gu = matmul(h2, w_gu)
    hidden = gu.shape[1] // 2
    gate, up = gu[:, :hidden], gu[:, hidden:]
    sig = jax.nn.sigmoid(gate)
    silu = gate * sig
    mixed = (silu * up).astype(BF)
    dm = times_t(dy_all, down_rows)
    dgate = (dm * up * (sig + silu * (1.0 - sig))).astype(BF)
    dup = (dm * silu).astype(BF)
    dgu = jnp.concatenate([dgate, dup], axis=1)
    dh2 = scatter(times_t(dgu, w_gu).astype(BF)).astype(jnp.float32)
    result = (x2 + scatter(matmul(mixed, down_rows).astype(BF)).astype(jnp.float32)).astype(BF)
    grad_down = sum_across(t_times(mixed, dy_all).reshape(teams, ff_own, width))
    grad_gate, grad_up = rows_of(t_times(h2, dgu), 2, teams)

    back, gain_two_part = norm_back(x2, gain_two, dh2)
    dx2 = cotangent.astype(jnp.float32) + back
    da = gather(dx2.astype(BF))
    dout = times_t(da, out_rows).astype(BF)
    grad_out = t_times(out, da)
    if head_cuts == teams:
        grad_out = sum_across(grad_out.reshape(teams, own, width))
    else:
        grad_out = lax.psum(grad_out, "fsdp", axis_index_groups=[list(t) for t in zip(*groups)])
        grad_out = lax.dynamic_slice_in_dim(gather(grad_out), index * own, own)
    dquery, dkeys, dvalues = attend_backward(query, keys, values, dout, logsum, valid)
    dqkv = jnp.concatenate(
        [
            rotate(dquery, cosine, -sine).astype(BF),
            rotate(dkeys, cosine, -sine).astype(BF),
            dvalues.astype(BF),
        ],
        axis=1,
    )
    dh1 = scatter(times_t(dqkv, w_qkv).astype(BF)).astype(jnp.float32)
    grad_query, grad_key, grad_value = rows_of(t_times(h1, dqkv), 3, head_cuts)
    back, gain_one_part = norm_back(x, gain_one, dh1)
    grad_tokens = dx2 + back
    gains = jnp.stack([gain_one_part, gain_two_part]).reshape(2, count, own).transpose(1, 0, 2)
    gains = jnp.sum(lax.all_to_all(gains, "fsdp", 0, 0, tiled=True), axis=0)
    return (
        result,
        grad_tokens,
        gains[0],
        grad_query,
        grad_key,
        grad_value,
        grad_out,
        gains[1],
        grad_gate,
        grad_up,
        grad_down,
    )


def solution(mesh):
    flat = P("fsdp")
    wide = P("fsdp", None)
    return jax.shard_map(
        local,
        mesh=mesh,
        in_specs=(wide, flat, flat, flat, wide, wide, wide, wide, flat, wide, wide, wide, wide),
        out_specs=(wide, wide, flat, wide, wide, wide, wide, flat, wide, wide, wide),
        check_vma=False,
    )
```

```python
import functools

import jax
import jax.numpy as jnp
from jax import lax
from jax.experimental import pallas as pl
from jax.experimental.pallas import tpu as pltpu
from jax.sharding import PartitionSpec as P

HEADS = 32
HEAD_DIM = 64
SEQ = 2048
DOCS = 16


EPS = 1e-05
THETA = 130000.0
HIDE = -1e30
BF = jnp.bfloat16
F32 = jnp.float32
LANES = 2 * HEAD_DIM
HALF = HEAD_DIM // 2
BLOCK = 512
VMEM = 56 * 2**20


def barrier(*values):
    return lax.optimization_barrier(values)


def norm_rows(v, gain):
    scale = lax.rsqrt(jnp.mean(v * v, axis=-1, keepdims=True) + EPS)
    return v * scale * gain


def norm_back(v, gain, grad):
    scale = lax.rsqrt(jnp.mean(v * v, axis=-1, keepdims=True) + EPS)
    hat = v * scale
    weighted = gain * grad
    back = scale * (weighted - hat * jnp.mean(hat * weighted, axis=-1, keepdims=True))
    return back, jnp.sum(grad * hat, axis=0)


def matmul(left, right):
    return jnp.dot(left, right, preferred_element_type=F32)


def times_t(left, right):
    return lax.dot_general(left, right, (((1,), (1,)), ((), ())), preferred_element_type=F32)


def t_times(left, right):
    return lax.dot_general(left, right, (((0,), (0,)), ((), ())), preferred_element_type=F32)


def lane_index(shape):
    return lax.broadcasted_iota(jnp.int32, shape, len(shape) - 1)


def of_head(head, shape):
    return lane_index(shape) // HALF % 2 == head


def value_of_head(head, shape):
    return lane_index(shape) // HEAD_DIM == head


def parts_of(v):
    high = v.astype(BF)
    rest = v - high.astype(F32)
    mid = rest.astype(BF)
    return high, mid, (rest - mid.astype(F32)).astype(BF)


def in_lanes(columns, first, shape):
    lane = lane_index(shape)
    out = jnp.zeros(shape, BF)
    for c, column in enumerate(columns):
        out = jnp.where(lane == first + c, column, out)
    return out


def forward_kernel(subs, offsets, qkv, cosine, sine, q_mask, k_mask, qe, ke, vs, out, out32):
    rows = sum(subs)
    blocks = SEQ // rows
    full = (SEQ, LANES)

    def place_block(b, carry):
        start = 0
        for r, sub in enumerate(subs):
            here = pl.ds(pl.multiple_of(offsets[r * blocks + b], 16), sub)
            there = pl.ds(pl.multiple_of(b * rows + start, 16), sub)
            start += sub
            c, s = cosine[there, :], sine[there, :]
            for at, ends in ((0, qe), (1, ke)):
                v = qkv[here, at * LANES : (at + 1) * LANES]
                turned = (v * c + pltpu.roll(v, HEAD_DIM, 1) * s).astype(BF)
                if at == 0:
                    turned = turned * (HEAD_DIM**-0.5)
                mask = (q_mask, k_mask)[at][there, :]
                for head in range(2):
                    ends[head, there, :] = jnp.where(of_head(head, turned.shape), turned, mask)
            vs[there, :] = qkv[here, 2 * LANES :].astype(BF)
        return carry

    lax.fori_loop(0, blocks, place_block, 0)
    diagonal = lax.broadcasted_iota(jnp.int32, (BLOCK, BLOCK), 0) >= lane_index((BLOCK, BLOCK))
    shape = (BLOCK, LANES)
    for i in range(SEQ // BLOCK):
        mine = slice(i * BLOCK, (i + 1) * BLOCK)
        outs = []
        for head in range(2):
            query = qe[head, mine, :]
            scores = []
            for j in range(i + 1):
                s = times_t(query, ke[head, j * BLOCK : (j + 1) * BLOCK, :])
                scores.append(jnp.where(diagonal, s, HIDE) if j == i else s)
            top = functools.reduce(jnp.maximum, scores)
            top = jnp.max(top, axis=1, keepdims=True)
            total = jnp.zeros(shape, F32)
            for j, s in enumerate(scores):
                probs = jnp.exp(s - top).astype(BF)
                value = vs[j * BLOCK : (j + 1) * BLOCK, :]
                value = jnp.where(value_of_head(head, shape), value, jnp.ones((), BF))
                total += matmul(probs, value)
            spare = (1 - head) * HEAD_DIM
            weight = total[:, spare : spare + 1]
            outs.append(total / weight)
            logsum = top + jnp.log(weight)
            first = HEAD_DIM + (1 - head) * HALF
            extra = in_lanes(parts_of(-logsum), first, shape)
            qe[head, mine, :] = query + extra
        out32[mine, :] = jnp.where(value_of_head(0, shape), outs[0], outs[1])

    def send_block(b, carry):
        start = 0
        for r, sub in enumerate(subs):
            here = pl.ds(pl.multiple_of(offsets[r * blocks + b], 16), sub)
            there = pl.ds(pl.multiple_of(b * rows + start, 16), sub)
            start += sub
            out[here, :] = out32[there, :].astype(BF)
        return carry

    lax.fori_loop(0, blocks, send_block, 0)


def backward_kernel(subs, offsets, qe, ke, vs, out32, dout, cosine, sine, grads, de, dq, dk, dv):
    rows = sum(subs)
    blocks = SEQ // rows

    def place_block(b, carry):
        start = 0
        for r, sub in enumerate(subs):
            here = pl.ds(pl.multiple_of(offsets[r * blocks + b], 16), sub)
            there = pl.ds(pl.multiple_of(b * rows + start, 16), sub)
            start += sub
            grad = dout[here, :]
            weighted = grad.astype(F32) * out32[there, :]
            shape = grad.shape
            for head in range(2):
                own = value_of_head(head, shape)
                delta = jnp.sum(jnp.where(own, weighted, 0.0), axis=1, keepdims=True)
                extra = in_lanes(parts_of(-delta), (1 - head) * HEAD_DIM, shape)
                de[head, there, :] = jnp.where(own, grad, extra)
        return carry

    lax.fori_loop(0, blocks, place_block, 0)
    shape = (BLOCK, LANES)
    diagonal = lax.broadcasted_iota(jnp.int32, (BLOCK, BLOCK), 0) <= lane_index((BLOCK, BLOCK))
    lane = lane_index(shape)
    for head in range(2):
        spare = (1 - head) * HEAD_DIM
        ones = jnp.where((lane >= spare) & (lane < spare + 3), jnp.ones((), BF), jnp.zeros((), BF))
        for j in range(SEQ // BLOCK):
            theirs = slice(j * BLOCK, (j + 1) * BLOCK)
            key = ke[head, theirs, :]
            value = jnp.where(value_of_head(head, shape), vs[theirs, :], ones)
            dkey = jnp.zeros(shape, F32)
            dvalue = jnp.zeros(shape, F32)
            for i in range(j, SEQ // BLOCK):
                mine = slice(i * BLOCK, (i + 1) * BLOCK)
                query = qe[head, mine, :]
                grad = de[head, mine, :]
                probs = jnp.exp(times_t(key, query))
                if i == j:
                    probs = jnp.where(diagonal, probs, 0.0)
                dscore = (probs * times_t(value, grad)).astype(BF)
                dvalue += matmul(probs.astype(BF), grad)
                dkey += matmul(dscore, query)
                dquery = t_times(dscore, key)
                if j > 0:
                    dquery += dq[head, mine, :]
                dq[head, mine, :] = dquery
            dk[head, theirs, :] = dkey
            dv[head, theirs, :] = dvalue

    def send_block(b, carry):
        start = 0
        for r, sub in enumerate(subs):
            here = pl.ds(pl.multiple_of(offsets[r * blocks + b], 16), sub)
            there = pl.ds(pl.multiple_of(b * rows + start, 16), sub)
            start += sub
            c, s = cosine[there, :], sine[there, :]
            first = of_head(0, (sub, LANES))
            query = jnp.where(first, dq[0, there, :], dq[1, there, :]) * (HEAD_DIM**-0.5)
            key = jnp.where(first, dk[0, there, :], dk[1, there, :])
            for at, v in ((0, query), (1, key)):
                turned = v * c - pltpu.roll(v, HEAD_DIM, 1) * s
                grads[here, at * LANES : (at + 1) * LANES] = turned.astype(BF)
            value = jnp.where(value_of_head(0, (sub, LANES)), dv[0, there, :], dv[1, there, :])
            grads[here, 2 * LANES :] = value.astype(BF)
        return carry

    lax.fori_loop(0, blocks, send_block, 0)


def attend_forward(subs, offsets, qkv, cosine, sine, q_mask, k_mask):
    like = jax.ShapeDtypeStruct
    smem = pl.BlockSpec(memory_space=pltpu.SMEM)
    vmem = pl.BlockSpec(memory_space=pltpu.VMEM)
    return pl.pallas_call(
        functools.partial(forward_kernel, subs),
        out_shape=[
            like((2, SEQ, LANES), BF),
            like((2, SEQ, LANES), BF),
            like((SEQ, LANES), BF),
            like((SEQ, LANES), BF),
            like((SEQ, LANES), F32),
        ],
        in_specs=[smem] + [vmem] * 5,
        out_specs=[vmem] * 5,
        compiler_params=pltpu.CompilerParams(vmem_limit_bytes=VMEM),
        cost_estimate=pl.CostEstimate(
            flops=8 * SEQ * SEQ * LANES, bytes_accessed=12 * 2**20, transcendentals=SEQ * SEQ
        ),
    )(offsets, qkv, cosine, sine, q_mask, k_mask)


def attend_backward(subs, offsets, qe, ke, vs, out32, dout, cosine, sine):
    smem = pl.BlockSpec(memory_space=pltpu.SMEM)
    vmem = pl.BlockSpec(memory_space=pltpu.VMEM)
    return pl.pallas_call(
        functools.partial(backward_kernel, subs),
        out_shape=jax.ShapeDtypeStruct((SEQ, 3 * LANES), BF),
        in_specs=[smem] + [vmem] * 7,
        out_specs=vmem,
        scratch_shapes=[
            pltpu.VMEM((2, SEQ, LANES), BF),
            pltpu.VMEM((2, SEQ, LANES), F32),
            pltpu.VMEM((2, SEQ, LANES), F32),
            pltpu.VMEM((2, SEQ, LANES), F32),
        ],
        compiler_params=pltpu.CompilerParams(vmem_limit_bytes=VMEM),
        cost_estimate=pl.CostEstimate(
            flops=20 * SEQ * SEQ * LANES, bytes_accessed=12 * 2**20, transcendentals=SEQ * SEQ
        ),
    )(offsets, qe, ke, vs, out32, dout, cosine, sine)


class Team:
    def __init__(self, rows, count):
        self.rows, self.count = rows, count
        self.size = SEQ // rows
        self.teams = count // self.size
        axes = [2 << k for k in range(self.size.bit_length() - 2)]
        self.rails = [tuple(axes[r:] + axes[:r]) for r in range(len(axes))]
        share = rows // (8 * 16) * 16
        self.subs = [2 * share] + [3 * share] * (len(axes) - 1)
        self.subs[-1] += rows - sum(self.subs)

    def flip(self, v, mask):
        return lax.ppermute(v, "fsdp", [(i, i ^ mask) for i in range(self.count)])

    def ahead(self, v, teams):
        step = teams * self.size
        return lax.ppermute(v, "fsdp", [(i, (i + step) % self.count) for i in range(self.count)])

    def cut(self, v, times=1):
        out, start = [], 0
        for sub in self.subs:
            out.append(v[start : start + times * sub])
            start += times * sub
        return out

    def offsets(self, place):
        away = jnp.arange(self.size, dtype=jnp.int32) ^ place
        out, start = [], 0
        for rail, sub in zip(self.rails, self.subs):
            at = (away & 1) * (SEQ // 2) + start * (self.size // 2)
            for k, mask in enumerate(rail):
                at = at + jnp.where(away & mask != 0, sub << k, 0)
            out.append(at)
            start += sub
        return jnp.concatenate(out).astype(jnp.int32)

    def gather(self, v):
        held = self.cut(v)
        steps = len(self.rails[0])
        for s in range(steps - 1):
            got = barrier(*[self.flip(h, rail[s]) for h, rail in zip(held, self.rails)])
            held = barrier(*[jnp.concatenate([h, g]) for h, g in zip(held, got)])
        last = [self.flip(h, rail[-1]) for h, rail in zip(held, self.rails)]
        low = [self.flip(h, 1) for h in held]
        got = barrier(*last, *low)
        last, low = got[: len(last)], got[len(last) :]
        high = [self.flip(h, 1) for h in last]
        out = []
        for pair in zip(held, last):
            out.extend(pair)
        for pair in zip(low, high):
            out.extend(pair)
        return out

    def scatter(self, left, times):
        half = SEQ // 2
        chips = self.size // 2
        sent = [self.flip(times(c).astype(BF), 1) for c in self.cut(left[half:], chips)]
        kept = [times(c) for c in self.cut(left[:half], chips)]
        held = [k + s.astype(F32) for k, s in zip(kept, sent)]
        for step in reversed(range(len(self.rails[0]))):
            upper = barrier(*[h[h.shape[0] // 2 :].astype(BF) for h in held])
            got = barrier(*[self.flip(u, rail[step]) for u, rail in zip(upper, self.rails)])
            held = [h[: h.shape[0] // 2] + g.astype(F32) for h, g in zip(held, got)]
        return jnp.concatenate(held)


def local(
    tokens,
    segments,
    positions,
    gain_attn,
    w_query,
    w_key,
    w_value,
    w_out,
    gain_mlp,
    w_gate,
    w_up,
    w_down,
    cotangent,
):
    rows, width = tokens.shape
    count = lax.axis_size("fsdp")
    team = Team(rows, count)
    size, teams = team.size, team.teams
    index = lax.axis_index("fsdp")
    mine = index // size
    place = index % size
    groups = [[t * size + p for p in range(size)] for t in range(teams)]
    own = w_query.shape[0]
    whole_heads = own % HEAD_DIM == 0
    ff_own = w_down.shape[0]

    def exchange(v):
        return lax.all_to_all(v, "fsdp", 0, 0, tiled=True, axis_index_groups=groups)

    def across(v):
        held = jnp.zeros((teams,) + v.shape, v.dtype)
        held = lax.dynamic_update_index_in_dim(held, v, mine, 0)
        for step in range(1, teams):
            held = lax.dynamic_update_index_in_dim(
                held, team.ahead(v, step), (mine - step) % teams, 0
            )
        return held

    def sum_across(v):
        total = lax.dynamic_index_in_dim(v, mine, 0, keepdims=False)
        for step in range(1, teams):
            sent = lax.dynamic_index_in_dim(v, (mine + step) % teams, 0, keepdims=False)
            total = total + team.ahead(sent.astype(BF), step).astype(F32)
        return total

    def cut_ff(w):
        r, c = w.shape
        return w.reshape(r, teams, size, -1).transpose(2, 0, 1, 3).reshape(size, r, c // size)

    def join_ff(v):
        _, r, c = v.shape
        return v.reshape(size, r, teams, -1).transpose(1, 2, 0, 3).reshape(r, c * size)

    def cut_values(w):
        r, c = w.shape
        w = w.reshape((r, 2, size, -1) if whole_heads else (r, size, 2, -1))
        return w.transpose((2, 0, 1, 3) if whole_heads else (1, 0, 2, 3)).reshape(size, r, -1)

    def join_values(v):
        _, r, c = v.shape
        v = v.reshape(size, r, 2, -1)
        return v.transpose((1, 2, 0, 3) if whole_heads else (1, 0, 2, 3)).reshape(r, -1)

    def cut_turned(w):
        v = cut_values(w).reshape(size, -1, 2, 2, HALF)
        return v.transpose(0, 1, 3, 2, 4).reshape(size, -1, LANES)

    def join_turned(v):
        v = v.reshape(size, -1, 2, 2, HALF).transpose(0, 1, 3, 2, 4)
        return join_values(v.reshape(size, -1, LANES))

    def columns_of(cut):
        block = exchange(jnp.concatenate(cut, axis=2))
        return across(block.reshape(-1, block.shape[2])).reshape(-1, block.shape[2])

    def rows_of(grad, joins):
        grad = sum_across(grad.reshape(teams, -1, grad.shape[1])).astype(BF)
        got = exchange(grad.reshape(size, -1, grad.shape[1]))
        each = got.shape[2] // len(joins)
        return [
            join(got[:, :, i * each : (i + 1) * each]).astype(F32) for i, join in enumerate(joins)
        ]

    x_pieces = team.gather(tokens)
    small = jnp.concatenate([v.astype(F32) for v in (gain_attn, gain_mlp, segments, positions)])
    small = jnp.broadcast_to(small[None], (count, small.shape[0]))
    small = lax.all_to_all(small, "fsdp", 0, 0, tiled=True)
    gain_one = small[:, :own].reshape(1, -1)
    gain_two = small[:, own : 2 * own].reshape(1, -1)
    small = lax.dynamic_slice_in_dim(small, mine * size, size, 0)
    docs = small[:, 2 * own : 2 * own + rows].reshape(SEQ, 1)
    places = small[:, 2 * own + rows :].reshape(SEQ, 1)

    if whole_heads:
        out_rows = across(w_out).reshape(-1, width)
    else:
        out_rows = lax.dynamic_slice_in_dim(
            lax.all_gather(w_out, "fsdp", axis=0, tiled=True), place * LANES, LANES
        )
    w_qkv = columns_of([cut_turned(w_query), cut_turned(w_key), cut_values(w_value)])

    freqs = THETA ** (-jnp.arange(HALF, dtype=F32) * 2.0 / HEAD_DIM)
    angles = places * freqs[None, :]
    cosine, sine = jnp.cos(angles), jnp.sin(angles)
    cosine = jnp.concatenate([cosine] * 4, axis=1)
    sine = jnp.concatenate([-sine, -sine, sine, sine], axis=1)
    lane = jnp.arange(LANES)[None, :]
    number = (lane % HALF).astype(F32)
    carries = (lane < HEAD_DIM) & (lane % HALF < DOCS)
    q_mask = jnp.where(carries & (docs != number), HIDE, 0.0).astype(BF)
    tail = (lane >= HEAD_DIM) & (lane % HALF < 3)
    k_mask = jnp.where((carries & (docs == number)) | tail, 1.0, 0.0).astype(BF)
    offsets = team.offsets(place)
    subs = tuple(team.subs)

    h1 = jnp.concatenate([norm_rows(p.astype(F32), gain_one).astype(BF) for p in x_pieces])
    qkv = matmul(h1, w_qkv)
    qe, ke, vs, out, out32 = attend_forward(subs, offsets, qkv, cosine, sine, q_mask, k_mask)
    w_gu = columns_of([cut_ff(w_gate), cut_ff(w_up)])
    dy = jnp.concatenate(team.gather(cotangent))
    down_rows = across(w_down).reshape(-1, width)
    x = tokens.astype(F32)
    x2 = x + team.scatter(out, lambda v: matmul(v, out_rows))
    h2 = jnp.concatenate(team.gather(norm_rows(x2, gain_two).astype(BF)))
    gu = matmul(h2, w_gu)
    hidden = gu.shape[1] // 2
    gate, up = gu[:, :hidden], gu[:, hidden:]
    sig = jax.nn.sigmoid(gate)
    silu = gate * sig
    mixed = (silu * up).astype(BF)
    dm = times_t(dy, down_rows)
    dgate = (dm * up * (sig + silu * (1.0 - sig))).astype(BF)
    dup = (dm * silu).astype(BF)
    dgu = jnp.concatenate([dgate, dup], axis=1)
    dh2 = team.scatter(dgu, lambda v: times_t(v, w_gu))
    result = (x2 + team.scatter(mixed, lambda v: matmul(v, down_rows))).astype(BF)
    grad_gate, grad_up = rows_of(t_times(h2, dgu), [join_ff, join_ff])
    grad_down = sum_across(t_times(mixed, dy).reshape(teams, ff_own, width))

    back, gain_two_part = norm_back(x2, gain_two, dh2)
    dx2 = cotangent.astype(F32) + back
    da = jnp.concatenate(team.gather(dx2.astype(BF)))
    dout = times_t(da, out_rows).astype(BF)
    grad_out = t_times(out, da)
    if whole_heads:
        grad_out = sum_across(grad_out.reshape(teams, own, width))
    else:
        grad_out = lax.psum(grad_out, "fsdp", axis_index_groups=[list(t) for t in zip(*groups)])
        grad_out = lax.all_gather(grad_out, "fsdp", axis=0, tiled=True, axis_index_groups=groups)
        grad_out = lax.dynamic_slice_in_dim(grad_out, index * own, own)
    dqkv = attend_backward(subs, offsets, qe, ke, vs, out32, dout, cosine, sine)
    dh1 = team.scatter(dqkv, lambda v: times_t(v, w_qkv))
    grad_query, grad_key, grad_value = rows_of(
        t_times(h1, dqkv), [join_turned, join_turned, join_values]
    )
    back, gain_one_part = norm_back(x, gain_one, dh1)
    grad_tokens = dx2 + back
    gains = jnp.stack([gain_one_part, gain_two_part]).reshape(2, count, own).transpose(1, 0, 2)
    gains = jnp.sum(lax.all_to_all(gains, "fsdp", 0, 0, tiled=True), axis=0)
    return (
        result,
        grad_tokens,
        gains[0],
        grad_query,
        grad_key,
        grad_value,
        grad_out,
        gains[1],
        grad_gate,
        grad_up,
        grad_down,
    )


def solution(mesh):
    flat = P("fsdp")
    wide = P("fsdp", None)
    return jax.shard_map(
        local,
        mesh=mesh,
        in_specs=(wide, flat, flat, flat, wide, wide, wide, wide, flat, wide, wide, wide, wide),
        out_specs=(wide, wide, flat, wide, wide, wide, wide, flat, wide, wide, wide),
        check_vma=False,
    )
```

```python
import functools

import jax
import jax.numpy as jnp
from jax import lax
from jax.experimental import pallas as pl
from jax.experimental.pallas import tpu as pltpu
from jax.sharding import PartitionSpec as P

HEADS = 32
HEAD_DIM = 64
SEQ = 2048
DOCS = 16


EPS = 1e-05
THETA = 130000.0
HIDE = -1e30
BF = jnp.bfloat16
F32 = jnp.float32
LANES = 2 * HEAD_DIM
HALF = HEAD_DIM // 2
BLOCK = 512
VMEM = 56 * 2**20


def barrier(*values):
    return lax.optimization_barrier(values)


def norm_rows(v, gain):
    scale = lax.rsqrt(jnp.mean(v * v, axis=-1, keepdims=True) + EPS)
    return v * scale * gain


def norm_back(v, gain, grad):
    scale = lax.rsqrt(jnp.mean(v * v, axis=-1, keepdims=True) + EPS)
    hat = v * scale
    weighted = gain * grad
    back = scale * (weighted - hat * jnp.mean(hat * weighted, axis=-1, keepdims=True))
    return back, jnp.sum(grad * hat, axis=0)


def matmul(left, right):
    return jnp.dot(left, right, preferred_element_type=F32)


def times_t(left, right):
    return lax.dot_general(left, right, (((1,), (1,)), ((), ())), preferred_element_type=F32)


def t_times(left, right):
    return lax.dot_general(left, right, (((0,), (0,)), ((), ())), preferred_element_type=F32)


def call(kernel, out_shape, in_specs, out_specs, flops, moved, grid=(), scratch=()):
    return pl.pallas_call(
        kernel,
        grid=grid,
        out_shape=out_shape,
        in_specs=in_specs,
        out_specs=out_specs,
        scratch_shapes=list(scratch),
        compiler_params=pltpu.CompilerParams(vmem_limit_bytes=VMEM),
        cost_estimate=pl.CostEstimate(
            flops=int(flops) // 16, bytes_accessed=int(moved) // 16, transcendentals=0
        ),
    )


LIKE = jax.ShapeDtypeStruct
IN_SMEM = pl.BlockSpec(memory_space=pltpu.SMEM)
IN_VMEM = pl.BlockSpec(memory_space=pltpu.VMEM)


def lane_index(shape):
    return lax.broadcasted_iota(jnp.int32, shape, len(shape) - 1)


def of_head(head, shape):
    return lane_index(shape) // HEAD_DIM == head


def swapped(v):
    first = lane_index(v.shape) % HEAD_DIM < HALF
    return jnp.where(first, pltpu.roll(v, LANES - HALF, 1), pltpu.roll(v, HALF, 1))


def parts_of(v):
    high = v.astype(BF)
    rest = v - high.astype(F32)
    mid = rest.astype(BF)
    return high, mid, (rest - mid.astype(F32)).astype(BF)


def in_lanes(columns, first, shape):
    lane = lane_index(shape)
    out = jnp.zeros(shape, BF)
    for c, column in enumerate(columns):
        out = jnp.where(lane == first + c, column, out)
    return out


def send_rows(subs, offsets, give):
    rows = sum(subs)
    blocks = SEQ // rows

    def one(b, carry):
        start = 0
        for r, sub in enumerate(subs):
            there = pl.ds(pl.multiple_of(offsets[r * blocks + b], 16), sub)
            here = pl.ds(pl.multiple_of(b * rows + start, 16), sub)
            start += sub
            give(here, there)
        return carry

    lax.fori_loop(0, blocks, one, 0)


def forward_kernel(
    subs, offsets, qkv, cosine, sine, q_mask, k_mask, qe, ke, vs, out, out32, railed
):
    shape = (BLOCK, LANES)
    for i in range(SEQ // BLOCK):
        mine = slice(i * BLOCK, (i + 1) * BLOCK)
        c, s = cosine[mine, :], sine[mine, :]
        for at, ends, mask in ((0, qe, q_mask), (1, ke, k_mask)):
            v = qkv[mine, at * LANES : (at + 1) * LANES]
            turned = (v * c + swapped(v) * s).astype(BF)
            if at == 0:
                turned = turned * (HEAD_DIM**-0.5)
            for head in range(2):
                ends[head, mine, :] = jnp.where(of_head(head, shape), turned, mask[mine, :])
        vs[mine, :] = qkv[mine, 2 * LANES :].astype(BF)
    diagonal = lax.broadcasted_iota(jnp.int32, (BLOCK, BLOCK), 0) >= lane_index((BLOCK, BLOCK))
    for i in range(SEQ // BLOCK):
        mine = slice(i * BLOCK, (i + 1) * BLOCK)
        outs = []
        for head in range(2):
            spare = (1 - head) * HEAD_DIM
            query = qe[head, mine, :]
            scores = []
            for j in range(i + 1):
                s = times_t(query, ke[head, j * BLOCK : (j + 1) * BLOCK, :])
                scores.append(jnp.where(diagonal, s, HIDE) if j == i else s)
            top = functools.reduce(jnp.maximum, scores)
            top = jnp.max(top, axis=1, keepdims=True)
            total = jnp.zeros(shape, F32)
            for j, s in enumerate(scores):
                probs = jnp.exp(s - top).astype(BF)
                value = vs[j * BLOCK : (j + 1) * BLOCK, :]
                value = jnp.where(of_head(head, shape), value, jnp.ones((), BF))
                total += matmul(probs, value)
            weight = total[:, spare : spare + 1]
            outs.append(total / weight)
            logsum = top + jnp.log(weight)
            qe[head, mine, :] = query + in_lanes(parts_of(-logsum), spare + HALF, shape)
        both = jnp.where(of_head(0, shape), outs[0], outs[1])
        out32[mine, :] = both
        out[mine, :] = both.astype(BF)

    def give(here, there):
        railed[there, :] = out[here, :]

    send_rows(subs, offsets, give)


def backward_kernel(
    subs, offsets, qe, ke, vs, out32, dout, cosine, sine, grads, railed, de, dq, dk, dv
):
    shape = (BLOCK, LANES)
    for i in range(SEQ // BLOCK):
        mine = slice(i * BLOCK, (i + 1) * BLOCK)
        grad = dout[mine, :]
        weighted = grad.astype(F32) * out32[mine, :]
        for head in range(2):
            own = of_head(head, shape)
            delta = jnp.sum(jnp.where(own, weighted, 0.0), axis=1, keepdims=True)
            extra = in_lanes(parts_of(-delta), (1 - head) * HEAD_DIM, shape)
            de[head, mine, :] = jnp.where(own, grad, extra)
    diagonal = lax.broadcasted_iota(jnp.int32, (BLOCK, BLOCK), 0) <= lane_index((BLOCK, BLOCK))
    lane = lane_index(shape)
    for head in range(2):
        spare = (1 - head) * HEAD_DIM
        ones = jnp.where((lane >= spare) & (lane < spare + 3), jnp.ones((), BF), jnp.zeros((), BF))
        for j in range(SEQ // BLOCK):
            theirs = slice(j * BLOCK, (j + 1) * BLOCK)
            key = ke[head, theirs, :]
            value = jnp.where(of_head(head, shape), vs[theirs, :], ones)
            dkey = jnp.zeros(shape, F32)
            dvalue = jnp.zeros(shape, F32)
            for i in range(j, SEQ // BLOCK):
                mine = slice(i * BLOCK, (i + 1) * BLOCK)
                query = qe[head, mine, :]
                grad = de[head, mine, :]
                probs = jnp.exp(times_t(key, query))
                if i == j:
                    probs = jnp.where(diagonal, probs, 0.0)
                dscore = (probs * times_t(value, grad)).astype(BF)
                dvalue += matmul(probs.astype(BF), grad)
                dkey += matmul(dscore, query)
                dquery = t_times(dscore, key)
                if j > 0:
                    dquery += dq[head, mine, :]
                dq[head, mine, :] = dquery
            dk[head, theirs, :] = dkey
            dv[head, theirs, :] = dvalue
    for i in range(SEQ // BLOCK):
        mine = slice(i * BLOCK, (i + 1) * BLOCK)
        c, s = cosine[mine, :], sine[mine, :]
        first = of_head(0, shape)
        query = jnp.where(first, dq[0, mine, :], dq[1, mine, :]) * (HEAD_DIM**-0.5)
        key = jnp.where(first, dk[0, mine, :], dk[1, mine, :])
        for at, v in ((0, query), (1, key)):
            turned = v * c - swapped(v) * s
            grads[mine, at * LANES : (at + 1) * LANES] = turned.astype(BF)
        value = jnp.where(first, dv[0, mine, :], dv[1, mine, :])
        grads[mine, 2 * LANES :] = value.astype(BF)

    def give(here, there):
        railed[there, :] = grads[here, :]

    send_rows(subs, offsets, give)


def attend_forward(subs, offsets, qkv, cosine, sine, q_mask, k_mask):
    return call(
        functools.partial(forward_kernel, subs),
        [
            LIKE((2, SEQ, LANES), BF),
            LIKE((2, SEQ, LANES), BF),
            LIKE((SEQ, LANES), BF),
            LIKE((SEQ, LANES), BF),
            LIKE((SEQ, LANES), F32),
            LIKE((SEQ, LANES), BF),
        ],
        [IN_SMEM] + [IN_VMEM] * 5,
        [IN_VMEM] * 6,
        8 * SEQ * SEQ * LANES,
        12 * 2**20,
    )(offsets, qkv, cosine, sine, q_mask, k_mask)


def attend_backward(subs, offsets, qe, ke, vs, out32, dout, cosine, sine):
    return call(
        functools.partial(backward_kernel, subs),
        [LIKE((SEQ, 3 * LANES), BF)] * 2,
        [IN_SMEM] + [IN_VMEM] * 7,
        [IN_VMEM] * 2,
        20 * SEQ * SEQ * LANES,
        12 * 2**20,
        scratch=[
            pltpu.VMEM((2, SEQ, LANES), BF),
            pltpu.VMEM((2, SEQ, LANES), F32),
            pltpu.VMEM((2, SEQ, LANES), F32),
            pltpu.VMEM((2, SEQ, LANES), F32),
        ],
    )(offsets, qe, ke, vs, out32, dout, cosine, sine)


def project_kernel(x, gain, w, h, out):
    h[...] = norm_rows(x[...].astype(F32), gain[...]).astype(BF)
    out[...] = matmul(h[...], w[...])


def norm_project(x, gain, w):
    rows, width = x.shape
    step, columns = 256, w.shape[1]
    return call(
        project_kernel,
        [LIKE((rows, width), BF), LIKE((rows, columns), F32)],
        [
            pl.BlockSpec((step, width), lambda i: (i, 0)),
            pl.BlockSpec((1, width), lambda i: (0, 0)),
            pl.BlockSpec((width, columns), lambda i: (0, 0)),
        ],
        [
            pl.BlockSpec((step, width), lambda i: (i, 0)),
            pl.BlockSpec((step, columns), lambda i: (i, 0)),
        ],
        2 * rows * width * columns,
        4 * rows * width,
        grid=(rows // step,),
    )(x, gain, w)


def hidden_kernel(subs, spots, h, w, dm, mixed, dgu, *refs):
    rails = len(subs)
    sent, kept, held = refs[:rails], refs[rails : 2 * rails], refs[2 * rails]
    hidden = dm.shape[1]
    gu = matmul(h[...], w[...])
    gate, up = gu[:, :hidden], gu[:, hidden:]
    sig = 1.0 / (1.0 + jnp.exp(-gate))
    silu = gate * sig
    mixed[...] = (silu * up).astype(BF)
    grad = dm[...]
    dgu[:, :hidden] = (grad * up * (sig + silu * (1.0 - sig))).astype(BF)
    dgu[:, hidden:] = (grad * silu).astype(BF)
    held[...] = times_t(dgu[...], w[...]).astype(BF)
    rows = sum(subs)
    core = spots[0]
    chips = SEQ // (2 * rows)
    start = 0
    for r, sub in enumerate(subs):
        there = pl.ds(pl.multiple_of(spots[1 + r * chips + pl.program_id(0)], 16), sub)
        near = pl.ds(pl.multiple_of(core * rows + start, 16), sub)
        far = pl.ds(pl.multiple_of((1 - core) * rows + start, 16), sub)
        kept[r][there, :] = held[near, :]
        sent[r][there, :] = held[far, :]
        start += sub


def hidden_rows(subs, spots, h, w, dm):
    rows, width = h.shape
    hidden = dm.shape[1]
    step = 2 * sum(subs)
    chips = rows // step
    rails = [LIKE((chips * sub, width), BF) for sub in subs]
    made = call(
        functools.partial(hidden_kernel, subs),
        [LIKE((rows, hidden), BF), LIKE((rows, 2 * hidden), BF)] + rails + rails,
        [
            IN_SMEM,
            pl.BlockSpec((step, width), lambda i: (i, 0)),
            pl.BlockSpec((width, 2 * hidden), lambda i: (0, 0)),
            pl.BlockSpec((step, hidden), lambda i: (i, 0)),
        ],
        [
            pl.BlockSpec((step, hidden), lambda i: (i, 0)),
            pl.BlockSpec((step, 2 * hidden), lambda i: (i, 0)),
        ]
        + [IN_VMEM] * (2 * len(subs)),
        8 * rows * width * hidden,
        6 * rows * width,
        grid=(chips,),
        scratch=[pltpu.VMEM((step, width), BF)],
    )(spots, h, w, dm)
    return made[0], made[1], made[2 : 2 + len(subs)], made[2 + len(subs) :]


def cut_kernel(first, each, blocks, *refs):
    out = refs[-1]
    for p in range(out.shape[0]):
        at = 0
        for w in refs[:-1]:
            for j in range(blocks):
                out[p, :, at : at + each] = w[:, first(j, p) : first(j, p) + each]
                at += each


def cut_columns(weights, size, first, each, blocks):
    rows = weights[0].shape[0]
    columns = each * blocks * len(weights)
    return call(
        functools.partial(cut_kernel, first, each, blocks),
        LIKE((size, rows, columns), BF),
        [IN_VMEM] * len(weights),
        IN_VMEM,
        0,
        4 * size * rows * columns,
    )(*weights)


def join_kernel(first, each, blocks, v, *outs):
    for p in range(v.shape[0]):
        at = 0
        for out in outs:
            for j in range(blocks):
                out[:, first(j, p) : first(j, p) + each] = v[p, :, at : at + each].astype(F32)
                at += each


def join_columns(v, parts, first, each, blocks):
    size, rows, _ = v.shape
    return call(
        functools.partial(join_kernel, first, each, blocks),
        [LIKE((rows, size * each * blocks), F32)] * parts,
        [IN_VMEM],
        [IN_VMEM] * parts,
        0,
        6 * v.size,
    )(v)


class Team:
    def __init__(self, rows, count):
        self.rows, self.count = rows, count
        self.size = SEQ // rows
        self.teams = count // self.size
        self.groups = [[t * self.size + p for p in range(self.size)] for t in range(self.teams)]
        axes = [2 << k for k in range(self.size.bit_length() - 2)]
        self.rails = [tuple(axes[r:] + axes[:r]) for r in range(len(axes))]
        share = rows // (8 * 16) * 16
        self.subs = [2 * share] + [3 * share] * (len(axes) - 1)
        self.subs[-1] += rows - sum(self.subs)

    def flip(self, mask):
        pairs = [(i, i ^ mask) for i in range(self.count)]
        return lambda v: lax.ppermute(v, "fsdp", pairs)

    def ahead(self, teams):
        step = teams * self.size
        pairs = [(i, (i + step) % self.count) for i in range(self.count)]
        return lambda v: lax.ppermute(v, "fsdp", pairs)

    def stay(self, v):
        return v

    def exchange(self, v):
        return lax.all_to_all(v, "fsdp", 0, 0, tiled=True, axis_index_groups=self.groups)

    def gather(self, v):
        return lax.all_gather(v, "fsdp", axis=0, tiled=True, axis_index_groups=self.groups)

    def reduce(self, v):
        return lax.psum_scatter(
            v, "fsdp", scatter_dimension=0, tiled=True, axis_index_groups=self.groups
        )

    def spots(self, place):
        away = 2 * jnp.arange(self.size // 2, dtype=jnp.int32) ^ place
        out = []
        for rail, sub in zip(self.rails, self.subs):
            at = jnp.zeros_like(away)
            for k, mask in enumerate(rail):
                at = at + jnp.where(away & mask != 0, sub << k, 0)
            out.append(at)
        return jnp.stack(out).astype(jnp.int32)

    def offsets(self, place):
        starts = jnp.cumsum(jnp.array([0] + self.subs[:-1], jnp.int32)) * (self.size // 2)
        chip = self.spots(place) + starts[:, None]
        other = (jnp.arange(2, dtype=jnp.int32) ^ place) & 1
        return (chip[:, :, None] + other * (SEQ // 2)).reshape(-1).astype(jnp.int32)

    def cut(self, v):
        out, start = [], 0
        for sub in self.subs:
            each = sub * self.size // 2
            out.append(v[start : start + each])
            start += each
        return out

    def one(self, v, move):
        [got] = yield [(v, move)]
        return got

    def scatter(self, sent, kept):
        got = yield [(s, self.flip(1)) for s in sent]
        held = [k.astype(F32) + g.astype(F32) for k, g in zip(kept, got)]
        for step in reversed(range(len(self.rails[0]))):
            upper = [h[h.shape[0] // 2 :].astype(BF) for h in held]
            got = yield [(u, self.flip(rail[step])) for u, rail in zip(upper, self.rails)]
            held = [h[: h.shape[0] // 2] + g.astype(F32) for h, g in zip(held, got)]
        return jnp.concatenate(held)

    def spread(self, block, chunks, mine):
        got, start = [[] for _ in range(self.teams)], 0
        for chunk in chunks:
            each = block.shape[0] * chunk // 16
            part = block[start : start + each]
            start += each
            new = yield [(part, self.ahead(s)) for s in range(1, self.teams)]
            for s, piece in enumerate(new):
                got[s + 1].append(piece)
        held = jnp.zeros((self.teams,) + block.shape, block.dtype)
        held = lax.dynamic_update_index_in_dim(held, block, mine, 0)
        for s in range(1, self.teams):
            at, start = (mine - s) % self.teams, 0
            for piece in got[s]:
                held = lax.dynamic_update_slice(held, piece[None], (at, start, 0))
                start += piece.shape[0]
        return held.reshape((-1,) + block.shape[1:])

    def columns(self, cut, chunks, mine):
        [block] = yield [(cut, self.exchange)]
        return (yield from self.spread(block.reshape(-1, block.shape[2]), chunks, mine))

    def add(self, left, right, chunks, mine):
        width = left.shape[1] // self.teams

        def product(team):
            return t_times(lax.dynamic_slice_in_dim(left, team * width, width, 1), right)

        sent = [product((mine + s) % self.teams).astype(BF) for s in range(1, self.teams)]
        got, start, total = [[] for _ in sent], 0, None
        for chunk in chunks:
            each = width * chunk // 16
            moves = [(v[start : start + each], self.ahead(s + 1)) for s, v in enumerate(sent)]
            if start == 0:
                new = yield moves
            else:
                *new, total = yield moves + [(total, self.stay)]
            start += each
            if total is None:
                total = product(mine)
            for s, piece in enumerate(new):
                got[s].append(piece)
        for pieces in got:
            total = total + jnp.concatenate(pieces).astype(F32)
        return total

    def owners(self, left, right, chunks, mine):
        total = yield from self.add(left, right, chunks, mine)
        [got] = yield [(total.astype(BF).reshape(self.size, -1, total.shape[1]), self.exchange)]
        return got


class Transfer:
    def __init__(self, steps):
        self.steps, self.value, self.over, self.got = steps, None, False, None
        self.moves = next(steps)

    def take(self):
        got, self.got = self.got, None
        try:
            self.moves = self.steps.send(got)
        except StopIteration as end:
            self.value, self.over, self.moves = end.value, True, []


class Clock:
    def __init__(self, token):
        self.token = token

    def start(self, *transfers):
        given = [v for t in transfers for v, _ in t.moves]
        given = list(barrier(self.token, *given)[1:])
        for t in transfers:
            t.got = [move(given.pop(0)) for _, move in t.moves]

    def wait(self, transfers, *values):
        tied = list(barrier(self.token, *values, *[g for t in transfers for g in t.got]))
        self.token, values, rest = tied[0], tied[1 : 1 + len(values)], tied[1 + len(values) :]
        for t in transfers:
            t.got = [rest.pop(0) for _ in t.got]
        for t in transfers:
            t.take()
        return values


def local(
    tokens,
    segments,
    positions,
    gain_attn,
    w_query,
    w_key,
    w_value,
    w_out,
    gain_mlp,
    w_gate,
    w_up,
    w_down,
    cotangent,
):
    rows, width = tokens.shape
    count = lax.axis_size("fsdp")
    team = Team(rows, count)
    size, teams = team.size, team.teams
    index = lax.axis_index("fsdp")
    mine = index // size
    place = index % size
    own = w_query.shape[0]
    whole_heads = own % HEAD_DIM == 0
    ff_own = w_down.shape[0]
    if whole_heads:
        head_cut = (lambda j, p: (j * size + p) * HEAD_DIM, HEAD_DIM, 2)
    else:
        head_cut = (lambda j, p: p * LANES, LANES, 1)
    ff_cut = (lambda j, p: (j * size + p) * ff_own, ff_own, teams)

    def everywhere(v):
        return lax.all_to_all(v, "fsdp", 0, 0, tiled=True)

    def across(move, *args):
        return Transfer(move(*args, mine))

    clock = Clock(positions)
    start, wait = clock.start, clock.wait

    get_x = Transfer(team.one(tokens, team.gather))
    start(get_x)
    small = jnp.concatenate([v.astype(F32) for v in (gain_attn, gain_mlp, segments, positions)])
    small = jnp.broadcast_to(small[None], (count, small.shape[0]))
    small = Transfer(team.one(small, everywhere))
    get_qkv = across(team.columns, cut_columns([w_query, w_key, w_value], size, *head_cut), [8, 8])
    get_down = across(team.spread, w_down, [4, 4, 4, 4])
    moving = [get_qkv]
    if whole_heads:
        get_out = across(team.spread, w_out, [16])
        moving.append(get_out)
    start(*moving)
    wait(moving)
    out_rows = (
        get_out.value
        if whole_heads
        else lax.dynamic_slice_in_dim(
            lax.all_gather(w_out, "fsdp", axis=0, tiled=True), place * LANES, LANES
        )
    )
    get_dy = Transfer(team.one(cotangent, team.gather))
    start(get_qkv, small, get_dy)
    wait([get_qkv, small])
    start(get_qkv)
    small = small.value
    gain_one = small[:, :own].reshape(1, -1)
    gain_two = small[:, own : 2 * own].reshape(1, -1)
    small = lax.dynamic_slice_in_dim(small, mine * size, size, 0)
    docs = small[:, 2 * own : 2 * own + rows].reshape(SEQ, 1)
    places = small[:, 2 * own + rows :].reshape(SEQ, 1)
    freqs = THETA ** (-jnp.arange(HALF, dtype=F32) * 2.0 / HEAD_DIM)
    angles = places * freqs[None, :]
    cosine, sine = jnp.cos(angles), jnp.sin(angles)
    cosine = jnp.concatenate([cosine] * 4, axis=1)
    sine = jnp.concatenate([-sine, sine] * 2, axis=1)
    lane = jnp.arange(LANES)[None, :] % HEAD_DIM
    number = lane.astype(F32)
    q_mask = jnp.where((lane < DOCS) & (docs != number), HIDE, 0.0).astype(BF)
    tail = (lane >= HALF) & (lane < HALF + 3)
    k_mask = jnp.where(((lane < DOCS) & (docs == number)) | tail, 1.0, 0.0).astype(BF)
    offsets = team.offsets(place)
    spots = jnp.concatenate([place[None] % 2, team.spots(place).reshape(-1)]).astype(jnp.int32)
    subs = tuple(team.subs)
    cut_gu = cut_columns([w_gate, w_up], size, *ff_cut)
    get_gu = across(team.columns, cut_gu, [4, 4, 4, 4])
    cosine, sine, q_mask, k_mask = wait([get_qkv, get_x], cosine, sine, q_mask, k_mask)

    x_all, w_qkv = get_x.value, get_qkv.value
    start(get_gu, get_down)
    h1, qkv = norm_project(x_all, gain_one, w_qkv)
    qe, ke, vs, out, out32, railed = attend_forward(
        subs, offsets, qkv, cosine, sine, q_mask, k_mask
    )
    [railed] = wait([get_down, get_gu], railed)

    def products(left, times):
        cut = team.cut(left[: SEQ // 2]), team.cut(left[SEQ // 2 :])
        return [times(v).astype(BF) for v in cut[1]], [times(v) for v in cut[0]]

    add_out = Transfer(team.scatter(*products(railed, lambda v: matmul(v, out_rows))))
    start(add_out, get_down)
    wait([add_out, get_down])
    start(add_out, get_gu)
    wait([add_out, get_gu])
    start(add_out, get_down)
    wait([add_out, get_down])
    start(add_out, get_down)
    wait([add_out, get_down])
    x = tokens.astype(F32)
    x2 = x + add_out.value
    get_h2 = Transfer(team.one(norm_rows(x2, gain_two).astype(BF), team.gather))
    start(get_h2, get_gu)
    wait([get_gu, get_dy])
    start(get_gu)
    dy = get_dy.value
    down_rows = get_down.value
    dm = times_t(dy, down_rows)
    [dm] = wait([get_gu], dm)
    start(get_gu)
    wait([get_gu, get_h2])
    w_gu = get_gu.value
    h2 = get_h2.value
    mixed, dgu, sent, kept = hidden_rows(subs, spots, h2, w_gu, dm)

    add_dh2 = Transfer(team.scatter(sent, kept))
    start(add_dh2)
    send_gu = across(team.owners, h2, dgu, [4, 2, 2, 4, 4])
    wait([add_dh2])
    for _ in range(3):
        start(add_dh2, send_gu)
        wait([add_dh2, send_gu])
    back, gain_two_part = norm_back(x2, gain_two, add_dh2.value)
    dx2 = cotangent.astype(F32) + back
    get_da = Transfer(team.one(dx2.astype(BF), team.gather))
    start(get_da, send_gu)
    send_down = across(team.add, mixed, dy, [4, 8, 4])
    wait([send_gu])
    start(send_gu)
    partial = matmul(mixed, down_rows).astype(BF)
    [partial] = wait([send_gu, get_da], partial)
    da = get_da.value
    dout = times_t(da, out_rows).astype(BF)
    if whole_heads:
        send_out = across(team.add, out, da, [16])
        start(send_out)
        [dout] = wait([send_out], dout)
        grad_out = send_out.value
    else:
        grad_out = lax.psum(
            t_times(out, da), "fsdp", axis_index_groups=[list(t) for t in zip(*team.groups)]
        )
        grad_out = lax.dynamic_slice_in_dim(team.gather(grad_out), index * own, own)
    add_result = Transfer(team.one(partial, team.reduce))
    start(add_result, send_gu, send_down)
    dqkv, railed = attend_backward(subs, offsets, qe, ke, vs, out32, dout, cosine, sine)
    dqkv, railed = wait([send_down, send_gu], dqkv, railed)
    grad_gate, grad_up = join_columns(send_gu.value, 2, *ff_cut)
    add_dh1 = Transfer(team.scatter(*products(railed, lambda v: times_t(v, w_qkv))))
    start(add_dh1, send_down)
    send_qkv = across(team.owners, h1, dqkv, [8, 8])
    wait([add_dh1, send_down])
    start(add_dh1, send_qkv)
    wait([add_dh1, send_qkv])
    start(add_dh1, send_qkv)
    wait([add_dh1, send_qkv])
    start(add_dh1, send_qkv, send_down)
    wait([add_dh1, send_qkv, send_down])
    back, gain_one_part = norm_back(x, gain_one, add_dh1.value)
    grad_tokens = dx2 + back
    gains = jnp.stack([gain_one_part, gain_two_part]).reshape(2, count, own).transpose(1, 0, 2)
    gains = Transfer(team.one(gains, everywhere))
    start(gains)
    wait([gains, add_result])
    gains = jnp.sum(gains.value, axis=0)
    result = (x2 + add_result.value.astype(F32)).astype(BF)
    grad_query, grad_key, grad_value = join_columns(send_qkv.value, 3, *head_cut)
    return (
        result,
        grad_tokens,
        gains[0],
        grad_query,
        grad_key,
        grad_value,
        grad_out,
        gains[1],
        grad_gate,
        grad_up,
        send_down.value,
    )


def solution(mesh):
    flat = P("fsdp")
    wide = P("fsdp", None)
    return jax.shard_map(
        local,
        mesh=mesh,
        in_specs=(wide, flat, flat, flat, wide, wide, wide, wide, flat, wide, wide, wide, wide),
        out_specs=(wide, wide, flat, wide, wide, wide, wide, flat, wide, wide, wide),
        check_vma=False,
    )
```

```python
import functools

import jax
import jax.numpy as jnp
from jax import lax
from jax.experimental import pallas as pl
from jax.experimental.pallas import tpu as pltpu
from jax.sharding import PartitionSpec as P

HEADS = 32
HEAD_DIM = 64
SEQ = 2048
DOCS = 16


EPS = 1e-05
THETA = 130000.0
HIDE = -1e30
BF = jnp.bfloat16
F32 = jnp.float32
LANES = 2 * HEAD_DIM
HALF = HEAD_DIM // 2
BLOCK = 512
MIB = 2**20


def barrier(*values):
    return lax.optimization_barrier(values)


def norm_rows(v, gain):
    scale = lax.rsqrt(jnp.mean(v * v, axis=-1, keepdims=True) + EPS)
    return v * scale * gain


def matmul(left, right):
    return jnp.dot(left, right, preferred_element_type=F32)


def times_t(left, right):
    return lax.dot_general(left, right, (((1,), (1,)), ((), ())), preferred_element_type=F32)


def t_times(left, right):
    return lax.dot_general(left, right, (((0,), (0,)), ((), ())), preferred_element_type=F32)


def call(kernel, out_shape, in_specs, out_specs, vmem=56, grid=(), scratch=()):
    return pl.pallas_call(
        kernel,
        grid=grid,
        out_shape=out_shape,
        in_specs=in_specs,
        out_specs=out_specs,
        scratch_shapes=list(scratch),
        compiler_params=pltpu.CompilerParams(vmem_limit_bytes=vmem * MIB),
        cost_estimate=pl.CostEstimate(flops=2**26, bytes_accessed=2**20, transcendentals=0),
    )


LIKE = jax.ShapeDtypeStruct
IN_SMEM = pl.BlockSpec(memory_space=pltpu.SMEM)
IN_VMEM = pl.BlockSpec(memory_space=pltpu.VMEM)


def per_step(rows, columns):
    return pl.BlockSpec((rows, columns), lambda i: (i, 0))


def same(shape):
    return pl.BlockSpec(shape, lambda i: (0, 0))


def lane_index(shape):
    return lax.broadcasted_iota(jnp.int32, shape, len(shape) - 1)


def of_head(head, shape):
    return lane_index(shape) // HEAD_DIM == head


def swapped(v):
    first = lane_index(v.shape) % HEAD_DIM < HALF
    return jnp.where(first, pltpu.roll(v, LANES - HALF, 1), pltpu.roll(v, HALF, 1))


def parts_of(v):
    high = v.astype(BF)
    rest = v - high.astype(F32)
    mid = rest.astype(BF)
    return high, mid, (rest - mid.astype(F32)).astype(BF)


def in_lanes(columns, first, shape):
    lane = lane_index(shape)
    out = jnp.zeros(shape, BF)
    for c, column in enumerate(columns):
        out = jnp.where(lane == first + c, column, out)
    return out


def each_block(size, give):
    rows = SEQ // size

    def one(b, carry):
        q = (b % (size // 2)) * 2 + b // (size // 2)
        give(pl.ds(pl.multiple_of(b * rows, 128), rows), pl.ds(pl.multiple_of(q * rows, 128), rows))
        return carry

    lax.fori_loop(0, size, one, 0)


def each_piece(size, subs, offsets, give):
    rows = SEQ // size

    def one(b, carry):
        start = 0
        for r, sub in enumerate(subs):
            there = pl.ds(pl.multiple_of(offsets[r * size + b], 16), sub)
            give(pl.ds(pl.multiple_of(b * rows + start, 16), sub), there)
            start += sub
        return carry

    lax.fori_loop(0, size, one, 0)


def forward_kernel(
    size, subs, offsets, qkv, cosine, sine, q_mask, k_mask, qe, ke, vs, out, out32, railed
):
    def place(there, here):
        c, s = cosine[there, :], sine[there, :]
        for at, ends, mask in ((0, qe, q_mask), (1, ke, k_mask)):
            v = qkv[here, at * LANES : (at + 1) * LANES]
            turned = (v * c + swapped(v) * s).astype(BF)
            if at == 0:
                turned = turned * (HEAD_DIM**-0.5)
            hidden = mask[there, :]
            for head in range(2):
                ends[head, there, :] = jnp.where(of_head(head, turned.shape), turned, hidden)
        vs[there, :] = qkv[here, 2 * LANES :].astype(BF)

    each_block(size, place)
    shape = (BLOCK, LANES)
    diagonal = lax.broadcasted_iota(jnp.int32, (BLOCK, BLOCK), 0) >= lane_index((BLOCK, BLOCK))
    for i in range(SEQ // BLOCK):
        mine = slice(i * BLOCK, (i + 1) * BLOCK)
        outs = []
        for head in range(2):
            spare = (1 - head) * HEAD_DIM
            query = qe[head, mine, :]
            scores = []
            for j in range(i + 1):
                s = times_t(query, ke[head, j * BLOCK : (j + 1) * BLOCK, :])
                scores.append(jnp.where(diagonal, s, HIDE) if j == i else s)
            top = functools.reduce(jnp.maximum, scores)
            top = jnp.max(top, axis=1, keepdims=True)
            total = jnp.zeros(shape, F32)
            for j, s in enumerate(scores):
                probs = jnp.exp(s - top).astype(BF)
                value = vs[j * BLOCK : (j + 1) * BLOCK, :]
                value = jnp.where(of_head(head, shape), value, jnp.ones((), BF))
                total += matmul(probs, value)
            weight = total[:, spare : spare + 1]
            outs.append(total / weight)
            logsum = top + jnp.log(weight)
            qe[head, mine, :] = query + in_lanes(parts_of(-logsum), spare + HALF, shape)
        out32[mine, :] = jnp.where(of_head(0, shape), outs[0], outs[1])

    def send(there, here):
        out[here, :] = out32[there, :].astype(BF)

    def rail(there, here):
        railed[here, :] = out32[there, :].astype(BF)

    each_block(size, send)
    each_piece(size, subs, offsets, rail)


def backward_kernel(
    size,
    subs,
    offsets,
    qe,
    ke,
    vs,
    out32,
    dout,
    cosine,
    sine,
    grads,
    railed,
    de,
    dq,
    dk,
    dv,
    turned,
):
    def place(there, here):
        grad = dout[here, :]
        weighted = grad.astype(F32) * out32[there, :]
        for head in range(2):
            own = of_head(head, grad.shape)
            delta = jnp.sum(jnp.where(own, weighted, 0.0), axis=1, keepdims=True)
            extra = in_lanes(parts_of(-delta), (1 - head) * HEAD_DIM, grad.shape)
            de[head, there, :] = jnp.where(own, grad, extra)

    each_block(size, place)
    shape = (BLOCK, LANES)
    diagonal = lax.broadcasted_iota(jnp.int32, (BLOCK, BLOCK), 0) <= lane_index((BLOCK, BLOCK))
    lane = lane_index(shape)
    for head in range(2):
        spare = (1 - head) * HEAD_DIM
        ones = jnp.where((lane >= spare) & (lane < spare + 3), jnp.ones((), BF), jnp.zeros((), BF))
        for j in range(SEQ // BLOCK):
            theirs = slice(j * BLOCK, (j + 1) * BLOCK)
            key = ke[head, theirs, :]
            value = jnp.where(of_head(head, shape), vs[theirs, :], ones)
            dkey = jnp.zeros(shape, F32)
            dvalue = jnp.zeros(shape, F32)
            for i in range(j, SEQ // BLOCK):
                mine = slice(i * BLOCK, (i + 1) * BLOCK)
                query = qe[head, mine, :]
                grad = de[head, mine, :]
                probs = jnp.exp(times_t(key, query))
                if i == j:
                    probs = jnp.where(diagonal, probs, 0.0)
                dscore = (probs * times_t(value, grad)).astype(BF)
                dvalue += matmul(probs.astype(BF), grad)
                dkey += matmul(dscore, query)
                dquery = t_times(dscore, key)
                if j > 0:
                    dquery += dq[head, mine, :]
                dq[head, mine, :] = dquery
            dk[head, theirs, :] = dkey
            dv[head, theirs, :] = dvalue
    for i in range(SEQ // BLOCK):
        mine = slice(i * BLOCK, (i + 1) * BLOCK)
        c, s = cosine[mine, :], sine[mine, :]
        first = of_head(0, shape)
        query = jnp.where(first, dq[0, mine, :], dq[1, mine, :]) * (HEAD_DIM**-0.5)
        key = jnp.where(first, dk[0, mine, :], dk[1, mine, :])
        for at, v in ((0, query), (1, key)):
            back = v * c - swapped(v) * s
            turned[mine, at * LANES : (at + 1) * LANES] = back.astype(BF)
        value = jnp.where(first, dv[0, mine, :], dv[1, mine, :])
        turned[mine, 2 * LANES :] = value.astype(BF)

    def send(there, here):
        grads[here, :] = turned[there, :]

    def rail(there, here):
        railed[here, :] = turned[there, :]

    each_block(size, send)
    each_piece(size, subs, offsets, rail)


def attend_forward(size, subs, offsets, qkv, cosine, sine, q_mask, k_mask):
    return call(
        functools.partial(forward_kernel, size, subs),
        [
            LIKE((2, SEQ, LANES), BF),
            LIKE((2, SEQ, LANES), BF),
            LIKE((SEQ, LANES), BF),
            LIKE((SEQ, LANES), BF),
            LIKE((SEQ, LANES), F32),
            LIKE((SEQ, LANES), BF),
        ],
        [IN_SMEM] + [IN_VMEM] * 5,
        [IN_VMEM] * 6,
    )(offsets, qkv, cosine, sine, q_mask, k_mask)


def attend_backward(size, subs, offsets, qe, ke, vs, out32, dout, cosine, sine):
    return call(
        functools.partial(backward_kernel, size, subs),
        [LIKE((SEQ, 3 * LANES), BF)] * 2,
        [IN_SMEM] + [IN_VMEM] * 7,
        [IN_VMEM] * 2,
        scratch=[
            pltpu.VMEM((2, SEQ, LANES), BF),
            pltpu.VMEM((2, SEQ, LANES), F32),
            pltpu.VMEM((2, SEQ, LANES), F32),
            pltpu.VMEM((2, SEQ, LANES), F32),
            pltpu.VMEM((SEQ, 3 * LANES), BF),
        ],
    )(offsets, qe, ke, vs, out32, dout, cosine, sine)


def project_kernel(x, gain, w, h, out):
    h[...] = norm_rows(x[...].astype(F32), gain[...]).astype(BF)
    out[...] = matmul(h[...], w[...])


def norm_project(x, gain, w):
    rows, width = x.shape
    step, columns = 256, w.shape[1]
    return call(
        project_kernel,
        [LIKE((rows, width), BF), LIKE((rows, columns), F32)],
        [per_step(step, width), same((1, width)), same((width, columns))],
        [per_step(step, width), per_step(step, columns)],
        grid=(rows // step,),
    )(x, gain, w)


def hand_out(subs, spots, product, sent, kept):
    rows = sum(subs)
    chips = SEQ // (2 * rows)
    core, chip = pl.program_id(0) % 2, pl.program_id(0) // 2
    for side, outs in ((spots[0], kept), (1 - spots[0], sent)):

        @pl.when(core == side)
        def _():
            for half in range(2):
                start = half * rows
                for r, sub in enumerate(subs):
                    there = spots[1 + r * chips + half * (chips // 2) + chip]
                    outs[r][pl.ds(pl.multiple_of(there, 16), sub), :] = product[start : start + sub]
                    start += sub


def hidden_kernel(subs, spots, h, w_gate, w_up, dm, mixed, dgate, dup, *outs):
    rails = len(subs)
    gate, up, grad = matmul(h[...], w_gate[...]), matmul(h[...], w_up[...]), dm[...]
    sig = 1.0 / (1.0 + jnp.exp(-gate))
    silu = gate * sig
    mixed[...] = (silu * up).astype(BF)
    dgate[...] = (grad * up * (sig + silu * (1.0 - sig))).astype(BF)
    dup[...] = (grad * silu).astype(BF)
    product = times_t(dgate[...], w_gate[...]) + times_t(dup[...], w_up[...])
    hand_out(subs, spots, product.astype(BF), outs[:rails], outs[rails:])


def hidden_rows(subs, spots, h, w_gate, w_up, dm):
    rows, width = h.shape
    hidden = dm.shape[1]
    step = 2 * sum(subs)
    rails = [LIKE((rows // step * sub, width), BF) for sub in subs]
    made = call(
        functools.partial(hidden_kernel, subs),
        [LIKE((rows, hidden), BF)] * 3 + rails + rails,
        [IN_SMEM, per_step(step, width), same(w_gate.shape), same(w_up.shape), per_step(step, hidden)],
        [per_step(step, hidden)] * 3 + [IN_VMEM] * (2 * len(subs)),
        grid=(rows // step,),
    )(spots, h, w_gate, w_up, dm)
    return *made[:3], made[3 : 3 + len(subs)], made[3 + len(subs) :]


def product_kernel(subs, spots, left, right, *outs):
    product = matmul(left[...], right[...]).astype(BF)
    hand_out(subs, spots, product, outs[: len(subs)], outs[len(subs) :])


def products(subs, spots, left, right):
    rows, depth = left.shape
    width = right.shape[1]
    step = 2 * sum(subs)
    rails = [LIKE((rows // step * sub, width), BF) for sub in subs]
    made = call(
        functools.partial(product_kernel, subs),
        rails + rails,
        [IN_SMEM, per_step(step, depth), same(right.shape)],
        [IN_VMEM] * (2 * len(subs)),
        vmem=24,
        grid=(rows // step,),
    )(spots, left, right)
    return made[: len(subs)], made[len(subs) :]


def fold_kernel(rails, last, *refs):
    held, got, outs = refs[:rails], refs[rails : 2 * rails], refs[2 * rails :]
    for r in range(rails):
        half = held[r].shape[0] // 2
        total = held[r][...].astype(F32) + got[r][...].astype(F32)
        outs[r][...] = total[half:].astype(BF)
        outs[rails + r][...] = total[:half]
        if last:
            outs[2 * rails + r][...] = total[:half].astype(BF)


def fold(held, got, last=False):
    rails, width = len(held), held[0].shape[1]
    step = width // 4

    def block(rows):
        return pl.BlockSpec((rows, step), lambda i: (0, i))

    halves = [v.shape[0] // 2 for v in held]
    kinds = [BF, F32] + [BF] * last
    made = call(
        functools.partial(fold_kernel, rails, last),
        [LIKE((h, width), kind) for kind in kinds for h in halves],
        [block(v.shape[0]) for v in (*held, *got)],
        [block(h) for kind in kinds for h in halves],
        vmem=16,
        grid=(4,),
    )(*held, *got)
    return [made[i : i + rails] for i in range(0, len(made), rails)]


def pair_rows(rails, half, refs):
    lower, came, upper, other = (refs[i * rails : (i + 1) * rails] for i in range(4))
    sub = lower[0].shape[0]
    for r in range(rails):
        for side, a, b in ((half, lower, came), (1 - half, upper, other)):
            at = pl.ds(pl.multiple_of(side * (rails * sub) + r * sub, 16), sub)
            yield at, a[r][...].astype(F32) + b[r][...].astype(F32)


def residual_kernel(rails, half, x, gain, *refs):
    sums, (x2, h) = refs[:-2], refs[-2:]
    for at, total in pair_rows(rails, half[0], sums):
        v = x[at, :].astype(F32) + total
        x2[at, :] = v
        h[at, :] = norm_rows(v, gain[...]).astype(BF)


def residual(half, x, gain, sums):
    return call(
        functools.partial(residual_kernel, len(sums) // 4),
        [LIKE(x.shape, F32), LIKE(x.shape, BF)],
        [IN_SMEM] + [IN_VMEM] * (2 + len(sums)),
        [IN_VMEM] * 2,
        vmem=24,
    )(half, x, gain, *sums)


def norm_back(v, gain, grad):
    scale = lax.rsqrt(jnp.mean(v * v, axis=-1, keepdims=True) + EPS)
    hat = v * scale
    weighted = gain * grad
    back = scale * (weighted - hat * jnp.mean(hat * weighted, axis=-1, keepdims=True))
    return back, jnp.sum(grad * hat, axis=0, keepdims=True)


def pair_back_kernel(rails, half, v, base, gain, *refs):
    sums, (out, rounded, part) = refs[:-3], refs[-3:]
    part[...] = jnp.zeros_like(part)
    for at, total in pair_rows(rails, half[0], sums):
        back, share = norm_back(v[at, :], gain[...], total)
        made = base[at, :].astype(F32) + back
        out[at, :] = made
        rounded[at, :] = made.astype(BF)
        part[...] += 0.5 * share


def pair_back(half, v, base, gain, sums):
    return call(
        functools.partial(pair_back_kernel, len(sums) // 4),
        [LIKE(v.shape, F32), LIKE(v.shape, BF), LIKE((1, v.shape[1]), F32)],
        [IN_SMEM] + [IN_VMEM] * (3 + len(sums)),
        [IN_VMEM] * 3,
        vmem=32,
    )(half, v, base, gain, *sums)


def own_rows(rails, half, refs, rows):
    lower, came = refs[:rails], refs[rails : 2 * rails]
    sub = lower[0].shape[0]
    for r in range(rails):
        at = pl.ds(pl.multiple_of(half * rows + r * sub, 16), sub)
        yield slice(r * sub, (r + 1) * sub), at, lower[r][...] + came[r][...].astype(F32)


def own_back_kernel(rails, half, v, base, gain, *refs):
    sums, (out, part) = refs[:-2], refs[-2:]
    part[...] = jnp.zeros_like(part)
    for mine, at, total in own_rows(rails, half[0], sums, v.shape[0]):
        back, share = norm_back(v[mine, :].astype(F32), gain[...], total)
        out[mine, :] = base[at, :] + back
        part[...] += share


def own_back(half, v, base, gain, sums):
    return call(
        functools.partial(own_back_kernel, len(sums) // 2),
        [LIKE(v.shape, F32), LIKE((1, v.shape[1]), F32)],
        [IN_SMEM] + [IN_VMEM] * (3 + len(sums)),
        [IN_VMEM] * 2,
        vmem=24,
    )(half, v, base, gain, *sums)


def result_kernel(rails, half, base, *refs):
    sums, out = refs[:-1], refs[-1]
    for mine, at, total in own_rows(rails, half[0], sums, out.shape[0]):
        out[mine, :] = (base[at, :] + total).astype(BF)


def own_result(half, base, sums):
    rows, width = base.shape
    return call(
        functools.partial(result_kernel, len(sums) // 2),
        LIKE((rows // 2, width), BF),
        [IN_SMEM] + [IN_VMEM] * (1 + len(sums)),
        IN_VMEM,
        vmem=24,
    )(half, base, *sums)


def cut_kernel(size, first, each, blocks, *refs):
    out = refs[-1]
    for d in range(out.shape[0]):
        p, at = d % size, 0
        for w in refs[:-1]:
            for j in range(blocks):
                out[d, :, at : at + each] = w[:, first(j, p) : first(j, p) + each]
                at += each


def cut_columns(weights, count, size, first, each, blocks):
    rows = weights[0].shape[0]
    columns = each * blocks * len(weights)
    return call(
        functools.partial(cut_kernel, size, first, each, blocks),
        LIKE((count, rows, columns), BF),
        [IN_VMEM] * len(weights),
        IN_VMEM,
        vmem=32,
    )(*weights)


def join_kernel(size, first, each, blocks, v, *outs):
    for p in range(size):
        at = 0
        for out in outs:
            for j in range(blocks):
                total = v[p, :, at : at + each].astype(F32)
                for d in range(p + size, v.shape[0], size):
                    total += v[d, :, at : at + each].astype(F32)
                out[:, first(j, p) : first(j, p) + each] = total
                at += each


def join_columns(v, parts, size, first, each, blocks):
    rows = v.shape[1]
    return call(
        functools.partial(join_kernel, size, first, each, blocks),
        [LIKE((rows, size * each * blocks), F32)] * parts,
        [IN_VMEM],
        [IN_VMEM] * parts,
        vmem=32,
    )(v)


class Team:
    def __init__(self, rows, count):
        self.rows, self.count = rows, count
        self.size = SEQ // rows
        self.teams = count // self.size
        self.groups = [[t * self.size + p for p in range(self.size)] for t in range(self.teams)]
        each = self.size // 2
        self.halves = [[h * each + p for p in range(each)] for h in range(2 * self.teams)]
        axes = [2 << k for k in range(self.size.bit_length() - 2)]
        first, rest = axes[-1:], axes[:-1]
        self.rails = [tuple(first + rest[r:] + rest[:r]) for r in range(len(rest))]
        self.subs = (rows // len(rest),) * len(rest)

    def flip(self, mask):
        pairs = [(i, i ^ mask) for i in range(self.count)]
        return lambda v: lax.ppermute(v, "fsdp", pairs)

    def ahead(self, teams):
        step = teams * self.size
        pairs = [(i, (i + step) % self.count) for i in range(self.count)]
        return lambda v: lax.ppermute(v, "fsdp", pairs)

    def stay(self, v):
        return v

    def everywhere(self, v):
        return lax.all_to_all(v, "fsdp", 0, 0, tiled=True)

    def gather(self, v):
        return lax.all_gather(v, "fsdp", axis=0, tiled=True, axis_index_groups=self.halves)

    def spots(self, place):
        away = 2 * jnp.arange(self.size // 2, dtype=jnp.int32) ^ place
        out = []
        for rail, sub in zip(self.rails, self.subs):
            at = jnp.zeros_like(away)
            for k, mask in enumerate(rail):
                at = at + jnp.where(away & mask != 0, sub << k, 0)
            out.append(at)
        return jnp.stack(out).astype(jnp.int32)

    def offsets(self, place):
        starts = jnp.cumsum(jnp.array((0,) + self.subs[:-1], jnp.int32)) * (self.size // 2)
        chip = self.spots(place) + starts[:, None]
        other = (jnp.arange(2, dtype=jnp.int32) ^ place) & 1
        return (chip[:, :, None] + other * (SEQ // 2)).reshape(-1).astype(jnp.int32)

    def cut(self, v):
        out, start = [], 0
        for sub in self.subs:
            each = sub * self.size // 2
            out.append(v[start : start + each])
            start += each
        return out

    def one(self, v, move):
        [got] = yield [(v, move)]
        return got

    def pair_up(self, v, half):
        [got] = yield [(v, self.flip(self.size // 2))]
        return jnp.where(half == 0, jnp.concatenate([v, got]), jnp.concatenate([got, v]))

    def scatter(self, sent, kept, pair):
        held, got = kept, (yield [(s, self.flip(1)) for s in sent])
        for step in reversed(range(1, len(self.rails[0]))):
            upper, held = fold(held, got)
            got = yield [(u, self.flip(rail[step])) for u, rail in zip(upper, self.rails)]
        upper, held, rounded = fold(held, got, last=True)
        move = self.flip(self.size // 2)
        if not pair:
            got = yield [(u, move) for u in upper]
            return [*held, *got]
        got = yield [(u, move) for u in (*upper, *rounded)]
        return [*held, *got[: len(held)], *upper, *got[len(held) :]]

    def spread(self, block, chunks, mine):
        got, start = [[] for _ in range(self.teams)], 0
        for chunk in chunks:
            each = block.shape[0] * chunk // 16
            part = block[start : start + each]
            start += each
            new = yield [(part, self.ahead(s)) for s in range(1, self.teams)]
            for s, piece in enumerate(new):
                got[s + 1].append(piece)
        held = jnp.zeros((self.teams,) + block.shape, block.dtype)
        held = lax.dynamic_update_index_in_dim(held, block, mine, 0)
        for s in range(1, self.teams):
            at, start = (mine - s) % self.teams, 0
            for piece in got[s]:
                held = lax.dynamic_update_slice(held, piece[None], (at, start, 0))
                start += piece.shape[0]
        return held.reshape((-1,) + block.shape[1:])

    def columns(self, cut):
        [got] = yield [(cut, self.everywhere)]
        return got.reshape(-1, got.shape[2])

    def owners(self, made):
        [got] = yield [(made.reshape(self.count, -1, made.shape[1]), self.everywhere)]
        return got

    def add(self, left, right, chunks, mine):
        width = left.shape[1] // self.teams

        def product(team):
            return t_times(lax.dynamic_slice_in_dim(left, team * width, width, 1), right)

        sent = [product((mine + s) % self.teams).astype(BF) for s in range(1, self.teams)]
        got, start = [[] for _ in sent], 0
        for chunk in chunks:
            each = width * chunk // 16
            moves = [(v[start : start + each], self.ahead(s + 1)) for s, v in enumerate(sent)]
            start += each
            if start == width:
                *new, total = yield moves + [(product(mine), self.stay)]
            else:
                new = yield moves
            for s, piece in enumerate(new):
                got[s].append(piece)
        for pieces in got:
            total = total + jnp.concatenate(pieces).astype(F32)
        return total


class Transfer:
    def __init__(self, steps):
        self.steps, self.value, self.over, self.got = steps, None, False, None
        self.moves = next(steps)

    def take(self):
        got, self.got = self.got, None
        try:
            self.moves = self.steps.send(got)
        except StopIteration as end:
            self.value, self.over, self.moves = end.value, True, []


class Clock:
    def __init__(self, token):
        self.token = token

    def start(self, *transfers):
        given = [v for t in transfers for v, _ in t.moves]
        given = list(barrier(self.token, *given)[1:])
        for t in transfers:
            t.got = [move(given.pop(0)) for _, move in t.moves]

    def beside(self, transfer, *values):
        tied = list(barrier(*values, *[v for v, _ in transfer.moves]))
        values, rest = tied[: len(values)], tied[len(values) :]
        transfer.moves = [(v, move) for v, (_, move) in zip(rest, transfer.moves)]
        return values

    def wait(self, transfers, *values):
        tied = list(barrier(self.token, *values, *[g for t in transfers for g in t.got]))
        self.token, values, rest = tied[0], tied[1 : 1 + len(values)], tied[1 + len(values) :]
        for t in transfers:
            t.got = [rest.pop(0) for _ in t.got]
        for t in transfers:
            t.take()
        return values


def local(
    tokens,
    segments,
    positions,
    gain_attn,
    w_query,
    w_key,
    w_value,
    w_out,
    gain_mlp,
    w_gate,
    w_up,
    w_down,
    cotangent,
):
    rows, width = tokens.shape
    count = lax.axis_size("fsdp")
    team = Team(rows, count)
    size, teams = team.size, team.teams
    index = lax.axis_index("fsdp")
    mine = index // size
    place = index % size
    own = w_query.shape[0]
    whole_heads = own % HEAD_DIM == 0
    ff_own = w_down.shape[0]
    if whole_heads:
        head_cut = (lambda j, p: (j * size + p) * HEAD_DIM, HEAD_DIM, 2)
    else:
        head_cut = (lambda j, p: p * LANES, LANES, 1)
    ff_cut = (lambda j, p: (j * size + p) * ff_own, ff_own, teams)

    def across(move, *args):
        return Transfer(move(*args, mine))

    clock = Clock(positions)
    start, wait = clock.start, clock.wait
    half = place // (size // 2)
    subs = team.subs

    pair_x = Transfer(team.pair_up(tokens, half))
    pair_dy = Transfer(team.pair_up(cotangent, half))
    start(pair_x)
    cut_qkv = cut_columns([w_query, w_key, w_value], count, size, *head_cut)
    [cut_qkv] = wait([pair_x], cut_qkv)
    x_pair = pair_x.value
    get_qkv = Transfer(team.columns(cut_qkv))
    get_x = Transfer(team.one(x_pair, team.gather))
    start(get_x, get_qkv, pair_dy)
    cut_gate = cut_columns([w_gate], count, size, *ff_cut)
    cut_up = cut_columns([w_up], count, size, *ff_cut)
    small = jnp.concatenate([v.astype(F32) for v in (gain_attn, gain_mlp, segments, positions)])
    small = jnp.broadcast_to(small[None], (count, small.shape[0]))
    small = Transfer(team.one(small, team.everywhere))
    cut_gate, cut_up = wait([pair_dy, get_qkv], cut_gate, cut_up)
    dy_pair = pair_dy.value
    get_dy = Transfer(team.one(dy_pair, team.gather))
    get_gate = Transfer(team.columns(cut_gate))
    get_up = Transfer(team.columns(cut_up))
    get_down = across(team.spread, w_down, [16])
    start(get_gate, small, get_dy)
    moving = []
    if whole_heads:
        get_out = across(team.spread, w_out, [16])
        start(get_out)
        moving.append(get_out)
    wait([small])
    small = small.value
    gain_one = small[:, :own].reshape(1, -1)
    gain_two = small[:, own : 2 * own].reshape(1, -1)
    small = lax.dynamic_slice_in_dim(small, mine * size, size, 0)
    docs = small[:, 2 * own : 2 * own + rows].reshape(SEQ, 1)
    places = small[:, 2 * own + rows :].reshape(SEQ, 1)
    freqs = THETA ** (-jnp.arange(HALF, dtype=F32) * 2.0 / HEAD_DIM)
    angles = places * freqs[None, :]
    cosine, sine = jnp.cos(angles), jnp.sin(angles)
    cosine = jnp.concatenate([cosine] * 4, axis=1)
    sine = jnp.concatenate([-sine, sine] * 2, axis=1)
    lane = jnp.arange(LANES)[None, :] % HEAD_DIM
    number = lane.astype(F32)
    q_mask = jnp.where((lane < DOCS) & (docs != number), HIDE, 0.0).astype(BF)
    tail = (lane >= HALF) & (lane < HALF + 3)
    k_mask = jnp.where(((lane < DOCS) & (docs == number)) | tail, 1.0, 0.0).astype(BF)
    offsets = team.offsets(place)
    spots = jnp.concatenate([place[None] % 2, team.spots(place).reshape(-1)]).astype(jnp.int32)
    here = half[None].astype(jnp.int32)
    cosine, sine, q_mask, k_mask, gain_one, gain_two, offsets, spots = wait(
        moving, cosine, sine, q_mask, k_mask, gain_one, gain_two, offsets, spots
    )
    w_qkv = get_qkv.value
    if whole_heads:
        out_rows = get_out.value
    else:
        out_rows = lax.dynamic_slice_in_dim(
            lax.all_gather(w_out, "fsdp", axis=0, tiled=True), place * LANES, LANES
        )
    [w_qkv] = wait([get_x], w_qkv)
    h1, qkv = norm_project(get_x.value, gain_one, w_qkv)
    qe, ke, vs, out, out32, railed = attend_forward(
        size, subs, offsets, qkv, cosine, sine, q_mask, k_mask
    )
    [railed] = wait([], railed)

    def rail_products(left, times):
        cut = team.cut(left[: SEQ // 2]), team.cut(left[SEQ // 2 :])
        return [times(v).astype(BF) for v in cut[1]], [times(v).astype(BF) for v in cut[0]]

    sent, kept = rail_products(railed, lambda v: matmul(v, out_rows))
    sent = wait([], *sent)
    add_out = Transfer(team.scatter(sent, kept, True))
    start(add_out)
    wait([add_out, get_gate])
    start(add_out, get_down)
    wait([add_out])
    start(add_out)
    wait([add_out, get_down])
    start(add_out)
    wait([add_out])
    x2, h2 = residual(here, x_pair, gain_two, add_out.value)
    get_h2 = Transfer(team.one(h2, team.gather))
    start(get_h2, get_up)
    wait([get_dy])
    dy, down_rows = get_dy.value, get_down.value
    dm = times_t(dy, down_rows)
    [dm] = wait([get_h2, get_up], dm)
    h2 = get_h2.value
    mixed, dgate, dup, sent, kept = hidden_rows(
        subs, spots, h2, get_gate.value, get_up.value, dm
    )

    add_dh2 = Transfer(team.scatter(sent, kept, True))
    start(add_dh2)
    send_down = across(team.add, mixed, dy, [16])
    wait([add_dh2])
    start(add_dh2, send_down)
    grad_gate = t_times(h2, dgate).astype(BF)
    [grad_gate] = wait([add_dh2], grad_gate)
    start(add_dh2)
    result_parts = products(subs, spots, mixed, down_rows)
    result_parts = [wait([], *part) for part in result_parts]
    wait([add_dh2, send_down])
    add_result = Transfer(team.scatter(*result_parts, False))
    start(add_dh2, add_result)
    wait([add_result])
    start(add_result)
    grad_up = t_times(h2, dup).astype(BF)
    [grad_up] = wait([add_dh2, add_result], grad_up)
    dx2, da, gain_two_part = pair_back(here, x2, dy_pair, gain_two, add_dh2.value)
    get_da = Transfer(team.one(da, team.gather))
    send_gate = Transfer(team.owners(grad_gate))
    send_up = Transfer(team.owners(grad_up))
    start(get_da, send_gate)
    wait([get_da, send_gate])
    da = get_da.value
    start(send_up, add_result)
    dout = times_t(da, out_rows).astype(BF)
    dqkv, railed = attend_backward(size, subs, offsets, qe, ke, vs, out32, dout, cosine, sine)
    sent, kept = rail_products(railed, lambda v: times_t(v, w_qkv))
    dqkv, *sent = wait([add_result], dqkv, *sent)
    add_dh1 = Transfer(team.scatter(sent, kept, False))
    start(add_dh1)
    grad_qkv = t_times(h1, dqkv).astype(BF)
    [grad_qkv] = wait([add_dh1, send_up], grad_qkv)
    send_qkv = Transfer(team.owners(grad_qkv))
    start(add_dh1, add_result, send_qkv)
    grad_gate = join_columns(send_gate.value, 1, size, *ff_cut)[0]
    [grad_gate] = wait([add_dh1, add_result], grad_gate)
    start(add_dh1)
    if whole_heads:
        send_out = across(team.add, out, da, [16])
        start(send_out)
    else:
        grad_out = lax.psum(
            t_times(out, da), "fsdp", axis_index_groups=[list(t) for t in zip(*team.groups)]
        )
        grad_out = lax.all_gather(
            grad_out, "fsdp", axis=0, tiled=True, axis_index_groups=team.groups
        )
        grad_out = lax.dynamic_slice_in_dim(grad_out, index * own, own)
    grad_up = join_columns(send_up.value, 1, size, *ff_cut)[0]
    result = own_result(here, x2, add_result.value)
    grad_up, result = wait([add_dh1], grad_up, result)
    start(add_dh1)
    if whole_heads:
        wait([add_dh1, send_qkv, send_out])
        grad_out = send_out.value
    else:
        wait([add_dh1, send_qkv])
    grad_tokens, gain_one_part = own_back(here, tokens, dx2, gain_one, add_dh1.value)
    gains = jnp.stack([gain_one_part, gain_two_part]).reshape(2, count, own).transpose(1, 0, 2)
    gains = Transfer(team.one(gains, team.everywhere))
    start(gains)
    wait([gains])
    grad_query, grad_key, grad_value = join_columns(send_qkv.value, 3, size, *head_cut)
    gains = jnp.sum(gains.value, axis=0)
    return (
        result,
        grad_tokens,
        gains[0],
        grad_query,
        grad_key,
        grad_value,
        grad_out,
        gains[1],
        grad_gate,
        grad_up,
        send_down.value,
    )


def solution(mesh):
    flat = P("fsdp")
    wide = P("fsdp", None)
    return jax.shard_map(
        local,
        mesh=mesh,
        in_specs=(wide, flat, flat, flat, wide, wide, wide, wide, flat, wide, wide, wide, wide),
        out_specs=(wide, wide, flat, wide, wide, wide, wide, flat, wide, wide, wide),
        check_vma=False,
    )
```

```python
import functools

import jax
import jax.numpy as jnp
from jax import lax
from jax.experimental import pallas as pl
from jax.experimental.pallas import tpu as pltpu
from jax.sharding import PartitionSpec as P

HEADS = 32
HEAD_DIM = 64
SEQ = 2048
DOCS = 16


EPS = 1e-05
THETA = 130000.0
HIDE = -1e30
BF = jnp.bfloat16
F32 = jnp.float32
LANES = 2 * HEAD_DIM
HALF = HEAD_DIM // 2
BLOCK = 512
STEP = 1024
MIB = 2**20


def barrier(*values):
    return lax.optimization_barrier(values)


def norm_rows(v, gain):
    scale = lax.rsqrt(jnp.mean(v * v, axis=-1, keepdims=True) + EPS)
    return v * scale * gain


def matmul(left, right):
    return jnp.dot(left, right, preferred_element_type=F32)


def times_t(left, right):
    return lax.dot_general(left, right, (((1,), (1,)), ((), ())), preferred_element_type=F32)


def t_times(left, right):
    return lax.dot_general(left, right, (((0,), (0,)), ((), ())), preferred_element_type=F32)


def call(kernel, out_shape, in_specs, out_specs, vmem=56, grid=(), scratch=()):
    return pl.pallas_call(
        kernel,
        grid=grid,
        out_shape=out_shape,
        in_specs=in_specs,
        out_specs=out_specs,
        scratch_shapes=list(scratch),
        compiler_params=pltpu.CompilerParams(vmem_limit_bytes=vmem * MIB),
        cost_estimate=pl.CostEstimate(flops=2**26, bytes_accessed=2**20, transcendentals=0),
    )


LIKE = jax.ShapeDtypeStruct
IN_SMEM = pl.BlockSpec(memory_space=pltpu.SMEM)
IN_VMEM = pl.BlockSpec(memory_space=pltpu.VMEM)


def per_step(rows, columns):
    return pl.BlockSpec((rows, columns), lambda i: (i, 0))


def same(shape):
    return pl.BlockSpec(shape, lambda i: (0, 0))


def lane_index(shape):
    return lax.broadcasted_iota(jnp.int32, shape, len(shape) - 1)


def of_head(head, shape):
    return lane_index(shape) // HEAD_DIM == head


def swapped(v):
    first = lane_index(v.shape) % HEAD_DIM < HALF
    return jnp.where(first, pltpu.roll(v, LANES - HALF, 1), pltpu.roll(v, HALF, 1))


def parts_of(v):
    high = v.astype(BF)
    rest = v - high.astype(F32)
    mid = rest.astype(BF)
    return high, mid, (rest - mid.astype(F32)).astype(BF)


def in_lanes(columns, first, shape):
    lane = lane_index(shape)
    out = jnp.zeros(shape, BF)
    for c, column in enumerate(columns):
        out = jnp.where(lane == first + c, column, out)
    return out


def each_block(size, give):
    rows = SEQ // size

    def one(b, carry):
        q = (b % (size // 2)) * 2 + b // (size // 2)
        give(pl.ds(pl.multiple_of(b * rows, 128), rows), pl.ds(pl.multiple_of(q * rows, 128), rows))
        return carry

    lax.fori_loop(0, size, one, 0)


def each_piece(size, subs, offsets, give):
    rows = SEQ // size

    def one(b, carry):
        start = 0
        for r, sub in enumerate(subs):
            there = pl.ds(pl.multiple_of(offsets[r * size + b], 16), sub)
            give(pl.ds(pl.multiple_of(b * rows + start, 16), sub), there)
            start += sub
        return carry

    lax.fori_loop(0, size, one, 0)


def forward_kernel(
    size, subs, offsets, qkv, cosine, sine, q_mask, k_mask, qe, ke, vs, out, out32, railed
):
    def place(there, here):
        c, s = cosine[there, :], sine[there, :]
        for at, ends, mask in ((0, qe, q_mask), (1, ke, k_mask)):
            v = qkv[here, at * LANES : (at + 1) * LANES]
            turned = (v * c + swapped(v) * s).astype(BF)
            if at == 0:
                turned = turned * (HEAD_DIM**-0.5)
            hidden = mask[there, :]
            for head in range(2):
                ends[head, there, :] = jnp.where(of_head(head, turned.shape), turned, hidden)
        vs[there, :] = qkv[here, 2 * LANES :].astype(BF)

    each_block(size, place)
    shape = (BLOCK, LANES)
    diagonal = lax.broadcasted_iota(jnp.int32, (BLOCK, BLOCK), 0) >= lane_index((BLOCK, BLOCK))
    for i in range(SEQ // BLOCK):
        mine = slice(i * BLOCK, (i + 1) * BLOCK)
        outs = []
        for head in range(2):
            spare = (1 - head) * HEAD_DIM
            query = qe[head, mine, :]
            scores = []
            for j in range(i + 1):
                s = times_t(query, ke[head, j * BLOCK : (j + 1) * BLOCK, :])
                scores.append(jnp.where(diagonal, s, HIDE) if j == i else s)
            top = functools.reduce(jnp.maximum, scores)
            top = jnp.max(top, axis=1, keepdims=True)
            total = jnp.zeros(shape, F32)
            for j, s in enumerate(scores):
                probs = jnp.exp(s - top).astype(BF)
                value = vs[j * BLOCK : (j + 1) * BLOCK, :]
                value = jnp.where(of_head(head, shape), value, jnp.ones((), BF))
                total += matmul(probs, value)
            weight = total[:, spare : spare + 1]
            outs.append(total / weight)
            logsum = top + jnp.log(weight)
            qe[head, mine, :] = query + in_lanes(parts_of(-logsum), spare + HALF, shape)
        out32[mine, :] = jnp.where(of_head(0, shape), outs[0], outs[1])

    def send(there, here):
        out[here, :] = out32[there, :].astype(BF)

    def rail(there, here):
        railed[here, :] = out32[there, :].astype(BF)

    each_block(size, send)
    each_piece(size, subs, offsets, rail)


def backward_kernel(
    size,
    subs,
    offsets,
    qe,
    ke,
    vs,
    out32,
    dout,
    cosine,
    sine,
    grads,
    railed,
    de,
    dq,
    dk,
    dv,
    turned,
):
    def place(there, here):
        grad = dout[here, :]
        weighted = grad.astype(F32) * out32[there, :]
        for head in range(2):
            own = of_head(head, grad.shape)
            delta = jnp.sum(jnp.where(own, weighted, 0.0), axis=1, keepdims=True)
            extra = in_lanes(parts_of(-delta), (1 - head) * HEAD_DIM, grad.shape)
            de[head, there, :] = jnp.where(own, grad, extra)

    each_block(size, place)
    shape = (BLOCK, LANES)
    diagonal = lax.broadcasted_iota(jnp.int32, (BLOCK, BLOCK), 0) <= lane_index((BLOCK, BLOCK))
    lane = lane_index(shape)
    for head in range(2):
        spare = (1 - head) * HEAD_DIM
        ones = jnp.where((lane >= spare) & (lane < spare + 3), jnp.ones((), BF), jnp.zeros((), BF))
        for j in range(SEQ // BLOCK):
            theirs = slice(j * BLOCK, (j + 1) * BLOCK)
            key = ke[head, theirs, :]
            value = jnp.where(of_head(head, shape), vs[theirs, :], ones)
            dkey = jnp.zeros(shape, F32)
            dvalue = jnp.zeros(shape, F32)
            for i in range(j, SEQ // BLOCK):
                mine = slice(i * BLOCK, (i + 1) * BLOCK)
                query = qe[head, mine, :]
                grad = de[head, mine, :]
                probs = jnp.exp(times_t(key, query))
                if i == j:
                    probs = jnp.where(diagonal, probs, 0.0)
                dscore = (probs * times_t(value, grad)).astype(BF)
                dvalue += matmul(probs.astype(BF), grad)
                dkey += matmul(dscore, query)
                dquery = t_times(dscore, key)
                if j > 0:
                    dquery += dq[head, mine, :]
                dq[head, mine, :] = dquery
            dk[head, theirs, :] = dkey
            dv[head, theirs, :] = dvalue
    for i in range(SEQ // BLOCK):
        mine = slice(i * BLOCK, (i + 1) * BLOCK)
        c, s = cosine[mine, :], sine[mine, :]
        first = of_head(0, shape)
        query = jnp.where(first, dq[0, mine, :], dq[1, mine, :]) * (HEAD_DIM**-0.5)
        key = jnp.where(first, dk[0, mine, :], dk[1, mine, :])
        for at, v in ((0, query), (1, key)):
            back = v * c - swapped(v) * s
            turned[mine, at * LANES : (at + 1) * LANES] = back.astype(BF)
        value = jnp.where(first, dv[0, mine, :], dv[1, mine, :])
        turned[mine, 2 * LANES :] = value.astype(BF)

    def send(there, here):
        grads[here, :] = turned[there, :]

    def rail(there, here):
        railed[here, :] = turned[there, :]

    each_block(size, send)
    each_piece(size, subs, offsets, rail)


def attend_forward(size, subs, offsets, qkv, cosine, sine, q_mask, k_mask):
    return call(
        functools.partial(forward_kernel, size, subs),
        [
            LIKE((2, SEQ, LANES), BF),
            LIKE((2, SEQ, LANES), BF),
            LIKE((SEQ, LANES), BF),
            LIKE((SEQ, LANES), BF),
            LIKE((SEQ, LANES), F32),
            LIKE((SEQ, LANES), BF),
        ],
        [IN_SMEM] + [IN_VMEM] * 5,
        [IN_VMEM] * 6,
    )(offsets, qkv, cosine, sine, q_mask, k_mask)


def attend_backward(size, subs, offsets, qe, ke, vs, out32, dout, cosine, sine):
    return call(
        functools.partial(backward_kernel, size, subs),
        [LIKE((SEQ, 3 * LANES), BF)] * 2,
        [IN_SMEM] + [IN_VMEM] * 7,
        [IN_VMEM] * 2,
        scratch=[
            pltpu.VMEM((2, SEQ, LANES), BF),
            pltpu.VMEM((2, SEQ, LANES), F32),
            pltpu.VMEM((2, SEQ, LANES), F32),
            pltpu.VMEM((2, SEQ, LANES), F32),
            pltpu.VMEM((SEQ, 3 * LANES), BF),
        ],
    )(offsets, qe, ke, vs, out32, dout, cosine, sine)


def project_kernel(x, gain, w, h, out):
    h[...] = norm_rows(x[...].astype(F32), gain[...]).astype(BF)
    out[...] = matmul(h[...], w[...])


def norm_project(x, gain, w):
    rows, width = x.shape
    step, columns = STEP, w.shape[1]
    return call(
        project_kernel,
        [LIKE((rows, width), BF), LIKE((rows, columns), F32)],
        [per_step(step, width), same((1, width)), same((width, columns))],
        [per_step(step, width), per_step(step, columns)],
        grid=(rows // step,),
    )(x, gain, w)


def hand_out(subs, spots, product, sent, kept):
    rows = sum(subs)
    chips = SEQ // (2 * rows)
    pairs = product.shape[0] // (2 * rows)
    for j in range(pairs):
        pair = pl.program_id(0) * pairs + j
        core, chip = pair % 2, pair // 2
        for side, outs in ((spots[0], kept), (1 - spots[0], sent)):

            @pl.when(core == side)
            def _():
                for half in range(2):
                    start = (2 * j + half) * rows
                    for r, sub in enumerate(subs):
                        there = spots[1 + r * chips + half * (chips // 2) + chip]
                        there = pl.ds(pl.multiple_of(there, 16), sub)
                        outs[r][there, :] = product[start : start + sub]
                        start += sub


def hidden_kernel(subs, spots, h, w_gate, w_up, dm, mixed, dgate, dup, *outs):
    rails = len(subs)
    gate, up, grad = matmul(h[...], w_gate[...]), matmul(h[...], w_up[...]), dm[...]
    sig = 1.0 / (1.0 + jnp.exp(-gate))
    silu = gate * sig
    mixed[...] = (silu * up).astype(BF)
    dgate[...] = (grad * up * (sig + silu * (1.0 - sig))).astype(BF)
    dup[...] = (grad * silu).astype(BF)
    product = times_t(dgate[...], w_gate[...]) + times_t(dup[...], w_up[...])
    hand_out(subs, spots, product.astype(BF), outs[:rails], outs[rails:])


def hidden_rows(subs, spots, h, w_gate, w_up, dm):
    rows, width = h.shape
    hidden = dm.shape[1]
    step = STEP
    rails = [LIKE((rows // (2 * sum(subs)) * sub, width), BF) for sub in subs]
    made = call(
        functools.partial(hidden_kernel, subs),
        [LIKE((rows, hidden), BF)] * 3 + rails + rails,
        [IN_SMEM, per_step(step, width), same(w_gate.shape), same(w_up.shape), per_step(step, hidden)],
        [per_step(step, hidden)] * 3 + [IN_VMEM] * (2 * len(subs)),
        grid=(rows // step,),
    )(spots, h, w_gate, w_up, dm)
    return *made[:3], made[3 : 3 + len(subs)], made[3 + len(subs) :]


def product_kernel(subs, spots, left, right, *outs):
    product = matmul(left[...], right[...]).astype(BF)
    hand_out(subs, spots, product, outs[: len(subs)], outs[len(subs) :])


def products(subs, spots, left, right):
    rows, depth = left.shape
    width = right.shape[1]
    step = STEP
    rails = [LIKE((rows // (2 * sum(subs)) * sub, width), BF) for sub in subs]
    made = call(
        functools.partial(product_kernel, subs),
        rails + rails,
        [IN_SMEM, per_step(step, depth), same(right.shape)],
        [IN_VMEM] * (2 * len(subs)),
        vmem=24,
        grid=(rows // step,),
    )(spots, left, right)
    return made[: len(subs)], made[len(subs) :]


def fold_kernel(rails, last, *refs):
    held, got, outs = refs[:rails], refs[rails : 2 * rails], refs[2 * rails :]
    for r in range(rails):
        half = held[r].shape[0] // 2
        total = held[r][...].astype(F32) + got[r][...].astype(F32)
        outs[r][...] = total[half:].astype(BF)
        outs[rails + r][...] = total[:half]
        if last:
            outs[2 * rails + r][...] = total[:half].astype(BF)


def fold(held, got, last=False):
    rails, width = len(held), held[0].shape[1]
    step = width // 4

    def block(rows):
        return pl.BlockSpec((rows, step), lambda i: (0, i))

    halves = [v.shape[0] // 2 for v in held]
    kinds = [BF, F32] + [BF] * last
    made = call(
        functools.partial(fold_kernel, rails, last),
        [LIKE((h, width), kind) for kind in kinds for h in halves],
        [block(v.shape[0]) for v in (*held, *got)],
        [block(h) for kind in kinds for h in halves],
        vmem=16,
        grid=(4,),
    )(*held, *got)
    return [made[i : i + rails] for i in range(0, len(made), rails)]


def pair_rows(rails, half, refs):
    lower, came, upper, other = (refs[i * rails : (i + 1) * rails] for i in range(4))
    sub = lower[0].shape[0]
    for r in range(rails):
        for side, a, b in ((half, lower, came), (1 - half, upper, other)):
            at = pl.ds(pl.multiple_of(side * (rails * sub) + r * sub, 16), sub)
            yield at, a[r][...].astype(F32) + b[r][...].astype(F32)


def residual_kernel(rails, half, x, gain, *refs):
    sums, (x2, h) = refs[:-2], refs[-2:]
    for at, total in pair_rows(rails, half[0], sums):
        v = x[at, :].astype(F32) + total
        x2[at, :] = v
        h[at, :] = norm_rows(v, gain[...]).astype(BF)


def residual(half, x, gain, sums):
    return call(
        functools.partial(residual_kernel, len(sums) // 4),
        [LIKE(x.shape, F32), LIKE(x.shape, BF)],
        [IN_SMEM] + [IN_VMEM] * (2 + len(sums)),
        [IN_VMEM] * 2,
        vmem=24,
    )(half, x, gain, *sums)


def norm_back(v, gain, grad):
    scale = lax.rsqrt(jnp.mean(v * v, axis=-1, keepdims=True) + EPS)
    hat = v * scale
    weighted = gain * grad
    return scale * (weighted - hat * jnp.mean(hat * weighted, axis=-1, keepdims=True))


def pair_back_kernel(rails, half, v, base, gain, *refs):
    sums, (out, rounded) = refs[:-2], refs[-2:]
    for at, total in pair_rows(rails, half[0], sums):
        made = base[at, :].astype(F32) + norm_back(v[at, :], gain[...], total)
        out[at, :] = made
        rounded[at, :] = made.astype(BF)


def pair_back(half, v, base, gain, sums):
    return call(
        functools.partial(pair_back_kernel, len(sums) // 4),
        [LIKE(v.shape, F32), LIKE(v.shape, BF)],
        [IN_SMEM] + [IN_VMEM] * (3 + len(sums)),
        [IN_VMEM] * 2,
        vmem=32,
    )(half, v, base, gain, *sums)


def own_rows(rails, half, refs, rows):
    lower, came = refs[:rails], refs[rails : 2 * rails]
    sub = lower[0].shape[0]
    for r in range(rails):
        at = pl.ds(pl.multiple_of(half * rows + r * sub, 16), sub)
        yield slice(r * sub, (r + 1) * sub), at, lower[r][...] + came[r][...].astype(F32)


def own_back_kernel(rails, half, v, base, gain, *refs):
    sums, out = refs[:-1], refs[-1]
    for mine, at, total in own_rows(rails, half[0], sums, v.shape[0]):
        out[mine, :] = base[at, :] + norm_back(v[mine, :].astype(F32), gain[...], total)


def own_back(half, v, base, gain, sums):
    return call(
        functools.partial(own_back_kernel, len(sums) // 2),
        LIKE(v.shape, F32),
        [IN_SMEM] + [IN_VMEM] * (3 + len(sums)),
        IN_VMEM,
        vmem=24,
    )(half, v, base, gain, *sums)


def result_kernel(rails, half, base, *refs):
    sums, out = refs[:-1], refs[-1]
    for mine, at, total in own_rows(rails, half[0], sums, out.shape[0]):
        out[mine, :] = (base[at, :] + total).astype(BF)


def own_result(half, base, sums):
    rows, width = base.shape
    return call(
        functools.partial(result_kernel, len(sums) // 2),
        LIKE((rows // 2, width), BF),
        [IN_SMEM] + [IN_VMEM] * (1 + len(sums)),
        IN_VMEM,
        vmem=24,
    )(half, base, *sums)


def cut_kernel(size, first, each, blocks, *refs):
    out = refs[-1]
    for d in range(out.shape[0]):
        p, at = d % size, 0
        for w in refs[:-1]:
            for j in range(blocks):
                out[d, :, at : at + each] = w[:, first(j, p) : first(j, p) + each]
                at += each


def cut_columns(weights, count, size, first, each, blocks):
    rows = weights[0].shape[0]
    columns = each * blocks * len(weights)
    return call(
        functools.partial(cut_kernel, size, first, each, blocks),
        LIKE((count, rows, columns), BF),
        [IN_VMEM] * len(weights),
        IN_VMEM,
        vmem=32,
    )(*weights)


def join_kernel(size, first, each, blocks, v, *refs):
    parts = (len(refs) - 1) // 2
    weights, outs, share = refs[:parts], refs[parts:-1], refs[-1]
    along = jnp.zeros((v.shape[1], each), F32)
    for p in range(size):
        at = 0
        for w, out in zip(weights, outs):
            for j in range(blocks):
                total = v[p, :, at : at + each].astype(F32)
                for d in range(p + size, v.shape[0], size):
                    total += v[d, :, at : at + each].astype(F32)
                here = slice(first(j, p), first(j, p) + each)
                out[:, here] = total
                along += total * w[:, here].astype(F32)
                at += each
    share[...] = jnp.sum(along, axis=1, keepdims=True)


def join_columns(v, weights, size, first, each, blocks):
    rows = v.shape[1]
    made = call(
        functools.partial(join_kernel, size, first, each, blocks),
        [LIKE((rows, size * each * blocks), F32)] * len(weights) + [LIKE((rows, 1), F32)],
        [IN_VMEM] * (1 + len(weights)),
        [IN_VMEM] * (len(weights) + 1),
        vmem=32,
    )(v, *weights)
    return made


class Team:
    def __init__(self, rows, count):
        self.rows, self.count = rows, count
        self.size = SEQ // rows
        self.teams = count // self.size
        self.groups = [[t * self.size + p for p in range(self.size)] for t in range(self.teams)]
        each = self.size // 2
        self.halves = [[h * each + p for p in range(each)] for h in range(2 * self.teams)]
        axes = [2 << k for k in range(self.size.bit_length() - 2)]
        first, rest = axes[-1:], axes[:-1]
        self.rails = [tuple(first + rest[r:] + rest[:r]) for r in range(len(rest))]
        self.subs = (rows // len(rest),) * len(rest)

    def flip(self, mask):
        pairs = [(i, i ^ mask) for i in range(self.count)]
        return lambda v: lax.ppermute(v, "fsdp", pairs)

    def ahead(self, teams):
        step = teams * self.size
        pairs = [(i, (i + step) % self.count) for i in range(self.count)]
        return lambda v: lax.ppermute(v, "fsdp", pairs)

    def stay(self, v):
        return v

    def everywhere(self, v):
        return lax.all_to_all(v, "fsdp", 0, 0, tiled=True)

    def gather(self, v):
        return lax.all_gather(v, "fsdp", axis=0, tiled=True, axis_index_groups=self.halves)

    def spots(self, place):
        away = 2 * jnp.arange(self.size // 2, dtype=jnp.int32) ^ place
        out = []
        for rail, sub in zip(self.rails, self.subs):
            at = jnp.zeros_like(away)
            for k, mask in enumerate(rail):
                at = at + jnp.where(away & mask != 0, sub << k, 0)
            out.append(at)
        return jnp.stack(out).astype(jnp.int32)

    def offsets(self, place):
        starts = jnp.cumsum(jnp.array((0,) + self.subs[:-1], jnp.int32)) * (self.size // 2)
        chip = self.spots(place) + starts[:, None]
        other = (jnp.arange(2, dtype=jnp.int32) ^ place) & 1
        return (chip[:, :, None] + other * (SEQ // 2)).reshape(-1).astype(jnp.int32)

    def cut(self, v):
        out, start = [], 0
        for sub in self.subs:
            each = sub * self.size // 2
            out.append(v[start : start + each])
            start += each
        return out

    def one(self, v, move):
        [got] = yield [(v, move)]
        return got

    def pair_up(self, v, half):
        [got] = yield [(v, self.flip(self.size // 2))]
        return jnp.where(half == 0, jnp.concatenate([v, got]), jnp.concatenate([got, v]))

    def scatter(self, sent, kept, pair):
        held, got = kept, (yield [(s, self.flip(1)) for s in sent])
        for step in reversed(range(1, len(self.rails[0]))):
            upper, held = fold(held, got)
            got = yield [(u, self.flip(rail[step])) for u, rail in zip(upper, self.rails)]
        upper, held, rounded = fold(held, got, last=True)
        move = self.flip(self.size // 2)
        if not pair:
            got = yield [(u, move) for u in upper]
            return [*held, *got]
        got = yield [(u, move) for u in (*upper, *rounded)]
        return [*held, *got[: len(held)], *upper, *got[len(held) :]]

    def spread(self, block, chunks, mine):
        got, start = [[] for _ in range(self.teams)], 0
        for chunk in chunks:
            each = block.shape[0] * chunk // 16
            part = block[start : start + each]
            start += each
            new = yield [(part, self.ahead(s)) for s in range(1, self.teams)]
            for s, piece in enumerate(new):
                got[s + 1].append(piece)
        held = jnp.zeros((self.teams,) + block.shape, block.dtype)
        held = lax.dynamic_update_index_in_dim(held, block, mine, 0)
        for s in range(1, self.teams):
            at, start = (mine - s) % self.teams, 0
            for piece in got[s]:
                held = lax.dynamic_update_slice(held, piece[None], (at, start, 0))
                start += piece.shape[0]
        return held.reshape((-1,) + block.shape[1:])

    def columns(self, cut):
        [got] = yield [(cut, self.everywhere)]
        return got.reshape(-1, got.shape[2])

    def owners(self, made):
        [got] = yield [(made.reshape(self.count, -1, made.shape[1]), self.everywhere)]
        return got

    def add(self, left, right, chunks, mine):
        width = left.shape[1] // self.teams

        def product(team):
            return t_times(lax.dynamic_slice_in_dim(left, team * width, width, 1), right)

        sent = [product((mine + s) % self.teams).astype(BF) for s in range(1, self.teams)]
        got, start = [[] for _ in sent], 0
        for chunk in chunks:
            each = width * chunk // 16
            moves = [(v[start : start + each], self.ahead(s + 1)) for s, v in enumerate(sent)]
            start += each
            if start == width:
                *new, total = yield moves + [(product(mine), self.stay)]
            else:
                new = yield moves
            for s, piece in enumerate(new):
                got[s].append(piece)
        for pieces in got:
            total = total + jnp.concatenate(pieces).astype(F32)
        return total


class Transfer:
    def __init__(self, steps):
        self.steps, self.value, self.over, self.got = steps, None, False, None
        self.moves = next(steps)

    def take(self):
        got, self.got = self.got, None
        try:
            self.moves = self.steps.send(got)
        except StopIteration as end:
            self.value, self.over, self.moves = end.value, True, []


class Clock:
    def __init__(self, token):
        self.token = token

    def start(self, *transfers):
        for t in transfers:
            t.got = [move(barrier(self.token, v)[1]) for v, move in t.moves]

    def start_together(self, *transfers):
        given = [v for t in transfers for v, _ in t.moves]
        given = list(barrier(self.token, *given)[1:])
        for t in transfers:
            t.got = [move(given.pop(0)) for _, move in t.moves]

    def beside(self, transfer, *values):
        tied = list(barrier(*values, *[v for v, _ in transfer.moves]))
        values, rest = tied[: len(values)], tied[len(values) :]
        transfer.moves = [(v, move) for v, (_, move) in zip(rest, transfer.moves)]
        return values

    def wait(self, transfers, *values):
        tied = list(barrier(self.token, *values, *[g for t in transfers for g in t.got]))
        self.token, values, rest = tied[0], tied[1 : 1 + len(values)], tied[1 + len(values) :]
        for t in transfers:
            t.got = [rest.pop(0) for _ in t.got]
        for t in transfers:
            t.take()
        return values


def local(
    tokens,
    segments,
    positions,
    gain_attn,
    w_query,
    w_key,
    w_value,
    w_out,
    gain_mlp,
    w_gate,
    w_up,
    w_down,
    cotangent,
):
    rows, width = tokens.shape
    count = lax.axis_size("fsdp")
    team = Team(rows, count)
    size, teams = team.size, team.teams
    index = lax.axis_index("fsdp")
    mine = index // size
    place = index % size
    own = w_query.shape[0]
    whole_heads = own % HEAD_DIM == 0
    ff_own = w_down.shape[0]
    if whole_heads:
        head_cut = (lambda j, p: (j * size + p) * HEAD_DIM, HEAD_DIM, 2)
    else:
        head_cut = (lambda j, p: p * LANES, LANES, 1)
    ff_cut = (lambda j, p: (j * size + p) * ff_own, ff_own, teams)

    def across(move, *args):
        return Transfer(move(*args, mine))

    clock = Clock(positions)
    start, wait = clock.start, clock.wait
    half = place // (size // 2)
    subs = team.subs

    pair_x = Transfer(team.pair_up(tokens, half))
    pair_dy = Transfer(team.pair_up(cotangent, half))
    start(pair_x)
    cut_qkv = cut_columns([w_query, w_key, w_value], count, size, *head_cut)
    [cut_qkv] = wait([pair_x], cut_qkv)
    x_pair = pair_x.value
    get_qkv = Transfer(team.columns(cut_qkv))
    get_x = Transfer(team.one(x_pair, team.gather))
    clock.start_together(get_x, get_qkv, pair_dy)
    cut_gate = cut_columns([w_gate], count, size, *ff_cut)
    cut_up = cut_columns([w_up], count, size, *ff_cut)
    small = jnp.concatenate([v.astype(F32) for v in (gain_attn, gain_mlp, segments, positions)])
    small = jnp.broadcast_to(small[None], (count, small.shape[0]))
    small = Transfer(team.one(small, team.everywhere))
    cut_gate, cut_up = wait([pair_dy, get_qkv], cut_gate, cut_up)
    dy_pair = pair_dy.value
    get_dy = Transfer(team.one(dy_pair, team.gather))
    get_gate = Transfer(team.columns(cut_gate))
    get_up = Transfer(team.columns(cut_up))
    get_down = across(team.spread, w_down, [16])
    start(get_gate, small, get_dy)
    moving = []
    if whole_heads:
        get_out = across(team.spread, w_out, [16])
        start(get_out)
        moving.append(get_out)
    wait([small])
    small = small.value
    gain_one = small[:, :own].reshape(1, -1)
    gain_two = small[:, own : 2 * own].reshape(1, -1)
    small = lax.dynamic_slice_in_dim(small, mine * size, size, 0)
    docs = small[:, 2 * own : 2 * own + rows].reshape(SEQ, 1)
    places = small[:, 2 * own + rows :].reshape(SEQ, 1)
    freqs = THETA ** (-jnp.arange(HALF, dtype=F32) * 2.0 / HEAD_DIM)
    angles = places * freqs[None, :]
    cosine, sine = jnp.cos(angles), jnp.sin(angles)
    cosine = jnp.concatenate([cosine] * 4, axis=1)
    sine = jnp.concatenate([-sine, sine] * 2, axis=1)
    lane = jnp.arange(LANES)[None, :] % HEAD_DIM
    number = lane.astype(F32)
    q_mask = jnp.where((lane < DOCS) & (docs != number), HIDE, 0.0).astype(BF)
    tail = (lane >= HALF) & (lane < HALF + 3)
    k_mask = jnp.where(((lane < DOCS) & (docs == number)) | tail, 1.0, 0.0).astype(BF)
    offsets = team.offsets(place)
    spots = jnp.concatenate([place[None] % 2, team.spots(place).reshape(-1)]).astype(jnp.int32)
    here = half[None].astype(jnp.int32)
    cosine, sine, q_mask, k_mask, gain_one, gain_two, offsets, spots = wait(
        moving, cosine, sine, q_mask, k_mask, gain_one, gain_two, offsets, spots
    )
    w_qkv = get_qkv.value
    if whole_heads:
        out_rows = get_out.value
    else:
        out_rows = lax.dynamic_slice_in_dim(
            lax.all_gather(w_out, "fsdp", axis=0, tiled=True), place * LANES, LANES
        )
    [w_qkv] = wait([get_x], w_qkv)
    h1, qkv = norm_project(get_x.value, gain_one, w_qkv)
    qe, ke, vs, out, out32, railed = attend_forward(
        size, subs, offsets, qkv, cosine, sine, q_mask, k_mask
    )
    [railed] = wait([], railed)

    def rail_products(left, times):
        cut = team.cut(left[: SEQ // 2]), team.cut(left[SEQ // 2 :])
        return [times(v).astype(BF) for v in cut[1]], [times(v).astype(BF) for v in cut[0]]

    sent, kept = rail_products(railed, lambda v: matmul(v, out_rows))
    sent = wait([], *sent)
    add_out = Transfer(team.scatter(sent, kept, True))
    start(add_out)
    wait([add_out, get_gate])
    start(add_out, get_down)
    wait([add_out])
    start(add_out)
    wait([add_out, get_down])
    start(add_out)
    wait([add_out])
    x2, h2 = residual(here, x_pair, gain_two, add_out.value)
    get_h2 = Transfer(team.one(h2, team.gather))
    start(get_h2, get_up)
    wait([get_dy])
    dy, down_rows = get_dy.value, get_down.value
    dm = times_t(dy, down_rows)
    [dm] = wait([get_h2, get_up], dm)
    h2 = get_h2.value
    mixed, dgate, dup, sent, kept = hidden_rows(
        subs, spots, h2, get_gate.value, get_up.value, dm
    )

    add_dh2 = Transfer(team.scatter(sent, kept, True))
    start(add_dh2)
    send_down = across(team.add, mixed, dy, [16])
    wait([add_dh2])
    start(add_dh2, send_down)
    grad_gate = t_times(h2, dgate).astype(BF)
    [grad_gate] = wait([add_dh2], grad_gate)
    start(add_dh2)
    result_parts = products(subs, spots, mixed, down_rows)
    result_parts = [wait([], *part) for part in result_parts]
    wait([add_dh2, send_down])
    add_result = Transfer(team.scatter(*result_parts, False))
    start(add_dh2, add_result)
    wait([add_result])
    start(add_result)
    grad_up = t_times(h2, dup).astype(BF)
    [grad_up] = wait([add_dh2, add_result], grad_up)
    dx2, da = pair_back(here, x2, dy_pair, gain_two, add_dh2.value)
    get_da = Transfer(team.one(da, team.gather))
    send_gate = Transfer(team.owners(grad_gate))
    send_up = Transfer(team.owners(grad_up))
    start(get_da, send_gate)
    wait([get_da, send_gate])
    da = get_da.value
    start(send_up, add_result)
    dout = times_t(da, out_rows).astype(BF)
    dqkv, railed = attend_backward(size, subs, offsets, qe, ke, vs, out32, dout, cosine, sine)
    sent, kept = rail_products(railed, lambda v: times_t(v, w_qkv))
    dqkv, *sent = wait([add_result], dqkv, *sent)
    add_dh1 = Transfer(team.scatter(sent, kept, False))
    start(add_dh1)
    grad_qkv = t_times(h1, dqkv).astype(BF)
    [grad_qkv] = wait([add_dh1, send_up], grad_qkv)
    send_qkv = Transfer(team.owners(grad_qkv))
    start(add_dh1, add_result, send_qkv)
    grad_gate, share_gate = join_columns(send_gate.value, [w_gate], size, *ff_cut)
    [grad_gate] = wait([add_dh1, add_result], grad_gate)
    start(add_dh1)
    if whole_heads:
        send_out = across(team.add, out, da, [16])
        start(send_out)
    else:
        grad_out = lax.psum(
            t_times(out, da), "fsdp", axis_index_groups=[list(t) for t in zip(*team.groups)]
        )
        grad_out = lax.all_gather(
            grad_out, "fsdp", axis=0, tiled=True, axis_index_groups=team.groups
        )
        grad_out = lax.dynamic_slice_in_dim(grad_out, index * own, own)
    grad_up, share_up = join_columns(send_up.value, [w_up], size, *ff_cut)
    grad_gain_mlp = (share_gate + share_up)[:, 0] / gain_mlp.astype(F32)
    result = own_result(here, x2, add_result.value)
    grad_up, result = wait([add_dh1], grad_up, result)
    start(add_dh1)
    if whole_heads:
        wait([add_dh1, send_qkv, send_out])
        grad_out = send_out.value
    else:
        wait([add_dh1, send_qkv])
    grad_tokens = own_back(here, tokens, dx2, gain_one, add_dh1.value)
    grad_query, grad_key, grad_value, share = join_columns(
        send_qkv.value, [w_query, w_key, w_value], size, *head_cut
    )
    grad_gain_attn = share[:, 0] / gain_attn.astype(F32)
    return (
        result,
        grad_tokens,
        grad_gain_attn,
        grad_query,
        grad_key,
        grad_value,
        grad_out,
        grad_gain_mlp,
        grad_gate,
        grad_up,
        send_down.value,
    )


def solution(mesh):
    flat = P("fsdp")
    wide = P("fsdp", None)
    return jax.shard_map(
        local,
        mesh=mesh,
        in_specs=(wide, flat, flat, flat, wide, wide, wide, wide, flat, wide, wide, wide, wide),
        out_specs=(wide, wide, flat, wide, wide, wide, wide, flat, wide, wide, wide),
        check_vma=False,
    )
```

```python
import functools

import jax
import jax.numpy as jnp
from jax import lax
from jax.experimental import pallas as pl
from jax.experimental.pallas import tpu as pltpu
from jax.sharding import PartitionSpec as P

HEADS = 32
HEAD_DIM = 64
SEQ = 2048
DOCS = 16


EPS = 1e-05
THETA = 130000.0
HIDE = -1e30
BF = jnp.bfloat16
F32 = jnp.float32
LANES = 2 * HEAD_DIM
HALF = HEAD_DIM // 2
BLOCK = 512
STEP = 1024
MIB = 2**20


def barrier(*values):
    return lax.optimization_barrier(values)


def norm_rows(v, gain):
    scale = lax.rsqrt(jnp.mean(v * v, axis=-1, keepdims=True) + EPS)
    return v * scale * gain


def matmul(left, right):
    return jnp.dot(left, right, preferred_element_type=F32)


def times_t(left, right):
    return lax.dot_general(left, right, (((1,), (1,)), ((), ())), preferred_element_type=F32)


def t_times(left, right):
    return lax.dot_general(left, right, (((0,), (0,)), ((), ())), preferred_element_type=F32)


def call(kernel, out_shape, in_specs, out_specs, vmem=56, grid=(), scratch=()):
    return pl.pallas_call(
        kernel,
        grid=grid,
        out_shape=out_shape,
        in_specs=in_specs,
        out_specs=out_specs,
        scratch_shapes=list(scratch),
        compiler_params=pltpu.CompilerParams(vmem_limit_bytes=vmem * MIB),
        cost_estimate=pl.CostEstimate(flops=2**26, bytes_accessed=2**20, transcendentals=0),
    )


LIKE = jax.ShapeDtypeStruct
IN_SMEM = pl.BlockSpec(memory_space=pltpu.SMEM)
IN_VMEM = pl.BlockSpec(memory_space=pltpu.VMEM)


def per_step(rows, columns):
    return pl.BlockSpec((rows, columns), lambda i: (i, 0))


def same(shape):
    return pl.BlockSpec(shape, lambda i: (0, 0))


def lane_index(shape):
    return lax.broadcasted_iota(jnp.int32, shape, len(shape) - 1)


def of_head(head, shape):
    return lane_index(shape) // HEAD_DIM == head


def swapped(v):
    first = lane_index(v.shape) % HEAD_DIM < HALF
    return jnp.where(first, pltpu.roll(v, LANES - HALF, 1), pltpu.roll(v, HALF, 1))


def parts_of(v):
    high = v.astype(BF)
    rest = v - high.astype(F32)
    mid = rest.astype(BF)
    return high, mid, (rest - mid.astype(F32)).astype(BF)


def in_lanes(columns, first, shape):
    lane = lane_index(shape)
    out = jnp.zeros(shape, BF)
    for c, column in enumerate(columns):
        out = jnp.where(lane == first + c, column, out)
    return out


def each_block(size, give):
    rows = SEQ // size

    def one(b, carry):
        q = (b % (size // 2)) * 2 + b // (size // 2)
        give(pl.ds(pl.multiple_of(b * rows, 128), rows), pl.ds(pl.multiple_of(q * rows, 128), rows))
        return carry

    lax.fori_loop(0, size, one, 0)


def each_piece(size, subs, offsets, give):
    rows = SEQ // size

    def one(b, carry):
        start = 0
        for r, sub in enumerate(subs):
            there = pl.ds(pl.multiple_of(offsets[r * size + b], 16), sub)
            give(pl.ds(pl.multiple_of(b * rows + start, 16), sub), there)
            start += sub
        return carry

    lax.fori_loop(0, size, one, 0)


def forward_kernel(
    size, subs, offsets, qkv, cosine, sine, q_mask, k_mask, qe, ke, vs, out, out32, railed
):
    def place(there, here):
        c, s = cosine[there, :], sine[there, :]
        for at, ends, mask in ((0, qe, q_mask), (1, ke, k_mask)):
            v = qkv[here, at * LANES : (at + 1) * LANES]
            turned = (v * c + swapped(v) * s).astype(BF)
            if at == 0:
                turned = turned * (HEAD_DIM**-0.5)
            hidden = mask[there, :]
            for head in range(2):
                ends[head, there, :] = jnp.where(of_head(head, turned.shape), turned, hidden)
        vs[there, :] = qkv[here, 2 * LANES :].astype(BF)

    each_block(size, place)
    shape = (BLOCK, LANES)
    diagonal = lax.broadcasted_iota(jnp.int32, (BLOCK, BLOCK), 0) >= lane_index((BLOCK, BLOCK))
    for i in range(SEQ // BLOCK):
        mine = slice(i * BLOCK, (i + 1) * BLOCK)
        outs = []
        for head in range(2):
            spare = (1 - head) * HEAD_DIM
            query = qe[head, mine, :]
            scores = []
            for j in range(i + 1):
                s = times_t(query, ke[head, j * BLOCK : (j + 1) * BLOCK, :])
                scores.append(jnp.where(diagonal, s, HIDE) if j == i else s)
            top = functools.reduce(jnp.maximum, scores)
            top = jnp.max(top, axis=1, keepdims=True)
            total = jnp.zeros(shape, F32)
            for j, s in enumerate(scores):
                probs = jnp.exp(s - top).astype(BF)
                value = vs[j * BLOCK : (j + 1) * BLOCK, :]
                value = jnp.where(of_head(head, shape), value, jnp.ones((), BF))
                total += matmul(probs, value)
            weight = total[:, spare : spare + 1]
            outs.append(total / weight)
            logsum = top + jnp.log(weight)
            qe[head, mine, :] = query + in_lanes(parts_of(-logsum), spare + HALF, shape)
        out32[mine, :] = jnp.where(of_head(0, shape), outs[0], outs[1])

    def send(there, here):
        out[here, :] = out32[there, :].astype(BF)

    def rail(there, here):
        railed[here, :] = out32[there, :].astype(BF)

    each_block(size, send)
    each_piece(size, subs, offsets, rail)


def backward_kernel(
    size,
    subs,
    offsets,
    qe,
    ke,
    vs,
    out32,
    dout,
    cosine,
    sine,
    grads,
    railed,
    de,
    dq,
    dk,
    dv,
    turned,
):
    def place(there, here):
        grad = dout[here, :]
        weighted = grad.astype(F32) * out32[there, :]
        for head in range(2):
            own = of_head(head, grad.shape)
            delta = jnp.sum(jnp.where(own, weighted, 0.0), axis=1, keepdims=True)
            extra = in_lanes(parts_of(-delta), (1 - head) * HEAD_DIM, grad.shape)
            de[head, there, :] = jnp.where(own, grad, extra)

    each_block(size, place)
    shape = (BLOCK, LANES)
    diagonal = lax.broadcasted_iota(jnp.int32, (BLOCK, BLOCK), 0) <= lane_index((BLOCK, BLOCK))
    lane = lane_index(shape)
    for head in range(2):
        spare = (1 - head) * HEAD_DIM
        ones = jnp.where((lane >= spare) & (lane < spare + 3), jnp.ones((), BF), jnp.zeros((), BF))
        for j in range(SEQ // BLOCK):
            theirs = slice(j * BLOCK, (j + 1) * BLOCK)
            key = ke[head, theirs, :]
            value = jnp.where(of_head(head, shape), vs[theirs, :], ones)
            dkey = jnp.zeros(shape, F32)
            dvalue = jnp.zeros(shape, F32)
            for i in range(j, SEQ // BLOCK):
                mine = slice(i * BLOCK, (i + 1) * BLOCK)
                query = qe[head, mine, :]
                grad = de[head, mine, :]
                probs = jnp.exp(times_t(key, query))
                if i == j:
                    probs = jnp.where(diagonal, probs, 0.0)
                dscore = (probs * times_t(value, grad)).astype(BF)
                dvalue += matmul(probs.astype(BF), grad)
                dkey += matmul(dscore, query)
                dquery = t_times(dscore, key)
                if j > 0:
                    dquery += dq[head, mine, :]
                dq[head, mine, :] = dquery
            dk[head, theirs, :] = dkey
            dv[head, theirs, :] = dvalue
    for i in range(SEQ // BLOCK):
        mine = slice(i * BLOCK, (i + 1) * BLOCK)
        c, s = cosine[mine, :], sine[mine, :]
        first = of_head(0, shape)
        query = jnp.where(first, dq[0, mine, :], dq[1, mine, :]) * (HEAD_DIM**-0.5)
        key = jnp.where(first, dk[0, mine, :], dk[1, mine, :])
        for at, v in ((0, query), (1, key)):
            back = v * c - swapped(v) * s
            turned[mine, at * LANES : (at + 1) * LANES] = back.astype(BF)
        value = jnp.where(first, dv[0, mine, :], dv[1, mine, :])
        turned[mine, 2 * LANES :] = value.astype(BF)

    def send(there, here):
        grads[here, :] = turned[there, :]

    def rail(there, here):
        railed[here, :] = turned[there, :]

    each_block(size, send)
    each_piece(size, subs, offsets, rail)


def attend_forward(size, subs, offsets, qkv, cosine, sine, q_mask, k_mask):
    return call(
        functools.partial(forward_kernel, size, subs),
        [
            LIKE((2, SEQ, LANES), BF),
            LIKE((2, SEQ, LANES), BF),
            LIKE((SEQ, LANES), BF),
            LIKE((SEQ, LANES), BF),
            LIKE((SEQ, LANES), F32),
            LIKE((SEQ, LANES), BF),
        ],
        [IN_SMEM] + [IN_VMEM] * 5,
        [IN_VMEM] * 6,
    )(offsets, qkv, cosine, sine, q_mask, k_mask)


def attend_backward(size, subs, offsets, qe, ke, vs, out32, dout, cosine, sine):
    return call(
        functools.partial(backward_kernel, size, subs),
        [LIKE((SEQ, 3 * LANES), BF)] * 2,
        [IN_SMEM] + [IN_VMEM] * 7,
        [IN_VMEM] * 2,
        scratch=[
            pltpu.VMEM((2, SEQ, LANES), BF),
            pltpu.VMEM((2, SEQ, LANES), F32),
            pltpu.VMEM((2, SEQ, LANES), F32),
            pltpu.VMEM((2, SEQ, LANES), F32),
            pltpu.VMEM((SEQ, 3 * LANES), BF),
        ],
    )(offsets, qe, ke, vs, out32, dout, cosine, sine)


def project_kernel(x, gain, w, h, out):
    h[...] = norm_rows(x[...].astype(F32), gain[...]).astype(BF)
    out[...] = matmul(h[...], w[...])


def norm_project(x, gain, w):
    rows, width = x.shape
    step, columns = STEP, w.shape[1]
    return call(
        project_kernel,
        [LIKE((rows, width), BF), LIKE((rows, columns), F32)],
        [per_step(step, width), same((1, width)), same((width, columns))],
        [per_step(step, width), per_step(step, columns)],
        grid=(rows // step,),
    )(x, gain, w)


def hand_out(subs, spots, product, sent, kept):
    rows = sum(subs)
    chips = SEQ // (2 * rows)
    pairs = product.shape[0] // (2 * rows)
    for j in range(pairs):
        pair = pl.program_id(0) * pairs + j
        core, chip = pair % 2, pair // 2
        for side, outs in ((spots[0], kept), (1 - spots[0], sent)):

            @pl.when(core == side)
            def _():
                for half in range(2):
                    start = (2 * j + half) * rows
                    for r, sub in enumerate(subs):
                        there = spots[1 + r * chips + half * (chips // 2) + chip]
                        there = pl.ds(pl.multiple_of(there, 16), sub)
                        outs[r][there, :] = product[start : start + sub]
                        start += sub


def hidden_kernel(subs, spots, h, w_gate, w_up, dm, mixed, dgate, dup, *outs):
    rails = len(subs)
    gate, up, grad = matmul(h[...], w_gate[...]), matmul(h[...], w_up[...]), dm[...]
    sig = 1.0 / (1.0 + jnp.exp(-gate))
    silu = gate * sig
    mixed[...] = (silu * up).astype(BF)
    dgate[...] = (grad * up * (sig + silu * (1.0 - sig))).astype(BF)
    dup[...] = (grad * silu).astype(BF)
    product = times_t(dgate[...], w_gate[...]) + times_t(dup[...], w_up[...])
    hand_out(subs, spots, product.astype(BF), outs[:rails], outs[rails:])


def hidden_rows(subs, spots, h, w_gate, w_up, dm):
    rows, width = h.shape
    hidden = dm.shape[1]
    step = STEP
    rails = [LIKE((rows // (2 * sum(subs)) * sub, width), BF) for sub in subs]
    made = call(
        functools.partial(hidden_kernel, subs),
        [LIKE((rows, hidden), BF)] * 3 + rails + rails,
        [IN_SMEM, per_step(step, width), same(w_gate.shape), same(w_up.shape), per_step(step, hidden)],
        [per_step(step, hidden)] * 3 + [IN_VMEM] * (2 * len(subs)),
        grid=(rows // step,),
    )(spots, h, w_gate, w_up, dm)
    return *made[:3], made[3 : 3 + len(subs)], made[3 + len(subs) :]


def product_kernel(subs, spots, left, right, *outs):
    product = matmul(left[...], right[...]).astype(BF)
    hand_out(subs, spots, product, outs[: len(subs)], outs[len(subs) :])


def products(subs, spots, left, right):
    rows, depth = left.shape
    width = right.shape[1]
    step = STEP
    rails = [LIKE((rows // (2 * sum(subs)) * sub, width), BF) for sub in subs]
    made = call(
        functools.partial(product_kernel, subs),
        rails + rails,
        [IN_SMEM, per_step(step, depth), same(right.shape)],
        [IN_VMEM] * (2 * len(subs)),
        vmem=24,
        grid=(rows // step,),
    )(spots, left, right)
    return made[: len(subs)], made[len(subs) :]


def fold_kernel(rails, last, *refs):
    held, got, outs = refs[:rails], refs[rails : 2 * rails], refs[2 * rails :]
    for r in range(rails):
        half = held[r].shape[0] // 2
        total = held[r][...].astype(F32) + got[r][...].astype(F32)
        outs[r][...] = total[half:].astype(BF)
        outs[rails + r][...] = total[:half]
        if last:
            outs[2 * rails + r][...] = total[:half].astype(BF)


def fold(held, got, last=False):
    rails, width = len(held), held[0].shape[1]
    step = width // 4

    def block(rows):
        return pl.BlockSpec((rows, step), lambda i: (0, i))

    halves = [v.shape[0] // 2 for v in held]
    kinds = [BF, F32] + [BF] * last
    made = call(
        functools.partial(fold_kernel, rails, last),
        [LIKE((h, width), kind) for kind in kinds for h in halves],
        [block(v.shape[0]) for v in (*held, *got)],
        [block(h) for kind in kinds for h in halves],
        vmem=16,
        grid=(4,),
    )(*held, *got)
    return [made[i : i + rails] for i in range(0, len(made), rails)]


def pair_rows(rails, half, refs):
    lower, came, upper, other = (refs[i * rails : (i + 1) * rails] for i in range(4))
    sub = lower[0].shape[0]
    for r in range(rails):
        for side, a, b in ((half, lower, came), (1 - half, upper, other)):
            at = pl.ds(pl.multiple_of(side * (rails * sub) + r * sub, 16), sub)
            yield at, a[r][...].astype(F32) + b[r][...].astype(F32)


def residual_kernel(rails, half, x, gain, *refs):
    sums, (x2, h) = refs[:-2], refs[-2:]
    for at, total in pair_rows(rails, half[0], sums):
        v = x[at, :].astype(F32) + total
        x2[at, :] = v
        h[at, :] = norm_rows(v, gain[...]).astype(BF)


def residual(half, x, gain, sums):
    return call(
        functools.partial(residual_kernel, len(sums) // 4),
        [LIKE(x.shape, F32), LIKE(x.shape, BF)],
        [IN_SMEM] + [IN_VMEM] * (2 + len(sums)),
        [IN_VMEM] * 2,
        vmem=24,
    )(half, x, gain, *sums)


def norm_back(v, gain, grad):
    scale = lax.rsqrt(jnp.mean(v * v, axis=-1, keepdims=True) + EPS)
    hat = v * scale
    weighted = gain * grad
    return scale * (weighted - hat * jnp.mean(hat * weighted, axis=-1, keepdims=True))


def pair_back_kernel(rails, half, v, base, gain, *refs):
    sums, (out, rounded) = refs[:-2], refs[-2:]
    for at, total in pair_rows(rails, half[0], sums):
        made = base[at, :].astype(F32) + norm_back(v[at, :], gain[...], total)
        out[at, :] = made
        rounded[at, :] = made.astype(BF)


def pair_back(half, v, base, gain, sums):
    return call(
        functools.partial(pair_back_kernel, len(sums) // 4),
        [LIKE(v.shape, F32), LIKE(v.shape, BF)],
        [IN_SMEM] + [IN_VMEM] * (3 + len(sums)),
        [IN_VMEM] * 2,
        vmem=32,
    )(half, v, base, gain, *sums)


def own_rows(rails, half, refs, rows):
    lower, came = refs[:rails], refs[rails : 2 * rails]
    sub = lower[0].shape[0]
    for r in range(rails):
        at = pl.ds(pl.multiple_of(half * rows + r * sub, 16), sub)
        yield slice(r * sub, (r + 1) * sub), at, lower[r][...] + came[r][...].astype(F32)


def own_back_kernel(rails, half, v, base, gain, *refs):
    sums, out = refs[:-1], refs[-1]
    for mine, at, total in own_rows(rails, half[0], sums, v.shape[0]):
        out[mine, :] = base[at, :] + norm_back(v[mine, :].astype(F32), gain[...], total)


def own_back(half, v, base, gain, sums):
    return call(
        functools.partial(own_back_kernel, len(sums) // 2),
        LIKE(v.shape, F32),
        [IN_SMEM] + [IN_VMEM] * (3 + len(sums)),
        IN_VMEM,
        vmem=24,
    )(half, v, base, gain, *sums)


def result_kernel(rails, half, base, *refs):
    sums, out = refs[:-1], refs[-1]
    for mine, at, total in own_rows(rails, half[0], sums, out.shape[0]):
        out[mine, :] = (base[at, :] + total).astype(BF)


def own_result(half, base, sums):
    rows, width = base.shape
    return call(
        functools.partial(result_kernel, len(sums) // 2),
        LIKE((rows // 2, width), BF),
        [IN_SMEM] + [IN_VMEM] * (1 + len(sums)),
        IN_VMEM,
        vmem=24,
    )(half, base, *sums)


def cut_kernel(size, first, each, blocks, *refs):
    out = refs[-1]
    for d in range(out.shape[0]):
        p, at = d % size, 0
        for w in refs[:-1]:
            for j in range(blocks):
                out[d, :, at : at + each] = w[:, first(j, p) : first(j, p) + each]
                at += each


def cut_columns(weights, count, size, first, each, blocks):
    rows = weights[0].shape[0]
    columns = each * blocks * len(weights)
    return call(
        functools.partial(cut_kernel, size, first, each, blocks),
        LIKE((count, rows, columns), BF),
        [IN_VMEM] * len(weights),
        IN_VMEM,
        vmem=32,
    )(*weights)


def join_kernel(size, first, each, blocks, v, *refs):
    parts = (len(refs) - 1) // 2
    weights, outs, share = refs[:parts], refs[parts:-1], refs[-1]
    along = jnp.zeros((v.shape[1], each), F32)
    for p in range(size):
        at = 0
        for w, out in zip(weights, outs):
            for j in range(blocks):
                total = v[p, :, at : at + each].astype(F32)
                for d in range(p + size, v.shape[0], size):
                    total += v[d, :, at : at + each].astype(F32)
                here = slice(first(j, p), first(j, p) + each)
                out[:, here] = total
                along += total * w[:, here].astype(F32)
                at += each
    share[...] = jnp.sum(along, axis=1, keepdims=True)


def join_columns(v, weights, size, first, each, blocks):
    rows = v.shape[1]
    made = call(
        functools.partial(join_kernel, size, first, each, blocks),
        [LIKE((rows, size * each * blocks), F32)] * len(weights) + [LIKE((rows, 1), F32)],
        [IN_VMEM] * (1 + len(weights)),
        [IN_VMEM] * (len(weights) + 1),
        vmem=32,
    )(v, *weights)
    return made


class Team:
    def __init__(self, rows, count):
        self.rows, self.count = rows, count
        self.size = SEQ // rows
        self.teams = count // self.size
        self.groups = [[t * self.size + p for p in range(self.size)] for t in range(self.teams)]
        each = self.size // 2
        self.halves = [[h * each + p for p in range(each)] for h in range(2 * self.teams)]
        axes = [2 << k for k in range(self.size.bit_length() - 2)]
        first, rest = axes[-1:], axes[:-1]
        self.rails = [tuple(first + rest[r:] + rest[:r]) for r in range(len(rest))]
        self.subs = (rows // len(rest),) * len(rest)

    def flip(self, mask):
        pairs = [(i, i ^ mask) for i in range(self.count)]
        return lambda v: lax.ppermute(v, "fsdp", pairs)

    def ahead(self, teams):
        step = teams * self.size
        pairs = [(i, (i + step) % self.count) for i in range(self.count)]
        return lambda v: lax.ppermute(v, "fsdp", pairs)

    def stay(self, v):
        return v

    def everywhere(self, v):
        return lax.all_to_all(v, "fsdp", 0, 0, tiled=True)

    def gather(self, v):
        return lax.all_gather(v, "fsdp", axis=0, tiled=True, axis_index_groups=self.halves)

    def spots(self, place):
        away = 2 * jnp.arange(self.size // 2, dtype=jnp.int32) ^ place
        out = []
        for rail, sub in zip(self.rails, self.subs):
            at = jnp.zeros_like(away)
            for k, mask in enumerate(rail):
                at = at + jnp.where(away & mask != 0, sub << k, 0)
            out.append(at)
        return jnp.stack(out).astype(jnp.int32)

    def offsets(self, place):
        starts = jnp.cumsum(jnp.array((0,) + self.subs[:-1], jnp.int32)) * (self.size // 2)
        chip = self.spots(place) + starts[:, None]
        other = (jnp.arange(2, dtype=jnp.int32) ^ place) & 1
        return (chip[:, :, None] + other * (SEQ // 2)).reshape(-1).astype(jnp.int32)

    def cut(self, v):
        out, start = [], 0
        for sub in self.subs:
            each = sub * self.size // 2
            out.append(v[start : start + each])
            start += each
        return out

    def one(self, v, move):
        [got] = yield [(v, move)]
        return got

    def pair_up(self, v, half):
        [got] = yield [(v, self.flip(self.size // 2))]
        return jnp.where(half == 0, jnp.concatenate([v, got]), jnp.concatenate([got, v]))

    def scatter(self, sent, kept, pair):
        held, got = kept, (yield [(s, self.flip(1)) for s in sent])
        for step in reversed(range(1, len(self.rails[0]))):
            upper, held = fold(held, got)
            got = yield [(u, self.flip(rail[step])) for u, rail in zip(upper, self.rails)]
        upper, held, rounded = fold(held, got, last=True)
        move = self.flip(self.size // 2)
        if not pair:
            got = yield [(u, move) for u in upper]
            return [*held, *got]
        got = yield [(u, move) for u in (*upper, *rounded)]
        return [*held, *got[: len(held)], *upper, *got[len(held) :]]

    def spread(self, block, chunks, mine):
        got, start = [[] for _ in range(self.teams)], 0
        for chunk in chunks:
            each = block.shape[0] * chunk // 16
            part = block[start : start + each]
            start += each
            new = yield [(part, self.ahead(s)) for s in range(1, self.teams)]
            for s, piece in enumerate(new):
                got[s + 1].append(piece)
        held = jnp.zeros((self.teams,) + block.shape, block.dtype)
        held = lax.dynamic_update_index_in_dim(held, block, mine, 0)
        for s in range(1, self.teams):
            at, start = (mine - s) % self.teams, 0
            for piece in got[s]:
                held = lax.dynamic_update_slice(held, piece[None], (at, start, 0))
                start += piece.shape[0]
        return held.reshape((-1,) + block.shape[1:])

    def columns(self, cut):
        [got] = yield [(cut, self.everywhere)]
        return got.reshape(-1, got.shape[2])

    def owners(self, made):
        [got] = yield [(made.reshape(self.count, -1, made.shape[1]), self.everywhere)]
        return got

    def add(self, left, right, chunks, mine):
        width = left.shape[1] // self.teams

        def product(team):
            return t_times(lax.dynamic_slice_in_dim(left, team * width, width, 1), right)

        sent = [product((mine + s) % self.teams).astype(BF) for s in range(1, self.teams)]
        got, start = [[] for _ in sent], 0
        for chunk in chunks:
            each = width * chunk // 16
            moves = [(v[start : start + each], self.ahead(s + 1)) for s, v in enumerate(sent)]
            start += each
            if start == width:
                *new, total = yield moves + [(product(mine), self.stay)]
            else:
                new = yield moves
            for s, piece in enumerate(new):
                got[s].append(piece)
        for pieces in got:
            total = total + jnp.concatenate(pieces).astype(F32)
        return total


class Transfer:
    def __init__(self, steps):
        self.steps, self.value, self.over, self.got = steps, None, False, None
        self.moves = next(steps)

    def take(self):
        got, self.got = self.got, None
        try:
            self.moves = self.steps.send(got)
        except StopIteration as end:
            self.value, self.over, self.moves = end.value, True, []


class Clock:
    def __init__(self, token):
        self.token = token

    def start(self, *transfers):
        for t in transfers:
            t.got = [move(barrier(self.token, v)[1]) for v, move in t.moves]

    def start_together(self, *transfers):
        given = [v for t in transfers for v, _ in t.moves]
        given = list(barrier(self.token, *given)[1:])
        for t in transfers:
            t.got = [move(given.pop(0)) for _, move in t.moves]

    def beside(self, transfer, *values):
        tied = list(barrier(*values, *[v for v, _ in transfer.moves]))
        values, rest = tied[: len(values)], tied[len(values) :]
        transfer.moves = [(v, move) for v, (_, move) in zip(rest, transfer.moves)]
        return values

    def ready(self, transfer, transfers):
        made = self.wait(transfers, *[v for v, _ in transfer.moves])
        transfer.moves = [(v, move) for v, (_, move) in zip(made, transfer.moves)]

    def wait(self, transfers, *values):
        tied = list(barrier(self.token, *values, *[g for t in transfers for g in t.got]))
        self.token, values, rest = tied[0], tied[1 : 1 + len(values)], tied[1 + len(values) :]
        for t in transfers:
            t.got = [rest.pop(0) for _ in t.got]
        for t in transfers:
            t.take()
        return values


def local(
    tokens,
    segments,
    positions,
    gain_attn,
    w_query,
    w_key,
    w_value,
    w_out,
    gain_mlp,
    w_gate,
    w_up,
    w_down,
    cotangent,
):
    rows, width = tokens.shape
    count = lax.axis_size("fsdp")
    team = Team(rows, count)
    size, teams = team.size, team.teams
    index = lax.axis_index("fsdp")
    mine = index // size
    place = index % size
    own = w_query.shape[0]
    whole_heads = own % HEAD_DIM == 0
    ff_own = w_down.shape[0]
    if whole_heads:
        head_cut = (lambda j, p: (j * size + p) * HEAD_DIM, HEAD_DIM, 2)
    else:
        head_cut = (lambda j, p: p * LANES, LANES, 1)
    ff_cut = (lambda j, p: (j * size + p) * ff_own, ff_own, teams)

    def across(move, *args):
        return Transfer(move(*args, mine))

    clock = Clock(positions)
    start, wait = clock.start, clock.wait
    half = place // (size // 2)
    subs = team.subs

    pair_x = Transfer(team.pair_up(tokens, half))
    pair_dy = Transfer(team.pair_up(cotangent, half))
    start(pair_x)
    cut_qkv = cut_columns([w_query, w_key, w_value], count, size, *head_cut)
    [cut_qkv] = wait([pair_x], cut_qkv)
    x_pair = pair_x.value
    get_qkv = Transfer(team.columns(cut_qkv))
    get_x = Transfer(team.one(x_pair, team.gather))
    clock.start_together(get_x, get_qkv, pair_dy)
    cut_gate = cut_columns([w_gate], count, size, *ff_cut)
    cut_up = cut_columns([w_up], count, size, *ff_cut)
    small = jnp.concatenate([v.astype(F32) for v in (gain_attn, gain_mlp, segments, positions)])
    small = jnp.broadcast_to(small[None], (count, small.shape[0]))
    small = Transfer(team.one(small, team.everywhere))
    cut_gate, cut_up = wait([pair_dy, get_qkv], cut_gate, cut_up)
    dy_pair = pair_dy.value
    get_dy = Transfer(team.one(dy_pair, team.gather))
    get_gate = Transfer(team.columns(cut_gate))
    get_up = Transfer(team.columns(cut_up))
    get_down = across(team.spread, w_down, [16])
    start(get_gate, small, get_dy)
    moving = []
    if whole_heads:
        get_out = across(team.spread, w_out, [16])
        start(get_out)
        moving.append(get_out)
    wait([small])
    small = small.value
    gain_one = small[:, :own].reshape(1, -1)
    gain_two = small[:, own : 2 * own].reshape(1, -1)
    small = lax.dynamic_slice_in_dim(small, mine * size, size, 0)
    docs = small[:, 2 * own : 2 * own + rows].reshape(SEQ, 1)
    places = small[:, 2 * own + rows :].reshape(SEQ, 1)
    freqs = THETA ** (-jnp.arange(HALF, dtype=F32) * 2.0 / HEAD_DIM)
    angles = places * freqs[None, :]
    cosine, sine = jnp.cos(angles), jnp.sin(angles)
    cosine = jnp.concatenate([cosine] * 4, axis=1)
    sine = jnp.concatenate([-sine, sine] * 2, axis=1)
    lane = jnp.arange(LANES)[None, :] % HEAD_DIM
    number = lane.astype(F32)
    q_mask = jnp.where((lane < DOCS) & (docs != number), HIDE, 0.0).astype(BF)
    tail = (lane >= HALF) & (lane < HALF + 3)
    k_mask = jnp.where(((lane < DOCS) & (docs == number)) | tail, 1.0, 0.0).astype(BF)
    offsets = team.offsets(place)
    spots = jnp.concatenate([place[None] % 2, team.spots(place).reshape(-1)]).astype(jnp.int32)
    here = half[None].astype(jnp.int32)
    cosine, sine, q_mask, k_mask, gain_one, gain_two, offsets, spots = wait(
        moving, cosine, sine, q_mask, k_mask, gain_one, gain_two, offsets, spots
    )
    w_qkv = get_qkv.value
    if whole_heads:
        out_rows = get_out.value
    else:
        out_rows = lax.dynamic_slice_in_dim(
            lax.all_gather(w_out, "fsdp", axis=0, tiled=True), place * LANES, LANES
        )
    [w_qkv] = wait([get_x], w_qkv)
    h1, qkv = norm_project(get_x.value, gain_one, w_qkv)
    qe, ke, vs, out, out32, railed = attend_forward(
        size, subs, offsets, qkv, cosine, sine, q_mask, k_mask
    )
    [railed] = wait([], railed)

    def rail_products(left, times):
        cut = team.cut(left[: SEQ // 2]), team.cut(left[SEQ // 2 :])
        return [times(v).astype(BF) for v in cut[1]], [times(v).astype(BF) for v in cut[0]]

    sent, kept = rail_products(railed, lambda v: matmul(v, out_rows))
    sent = wait([], *sent)
    add_out = Transfer(team.scatter(sent, kept, True))
    start(add_out)
    wait([add_out, get_gate])
    start(add_out, get_down)
    wait([add_out])
    start(add_out)
    wait([add_out, get_down])
    start(add_out)
    wait([add_out])
    x2, h2 = residual(here, x_pair, gain_two, add_out.value)
    get_h2 = Transfer(team.one(h2, team.gather))
    start(get_h2, get_up)
    wait([get_dy])
    dy, down_rows = get_dy.value, get_down.value
    dm = times_t(dy, down_rows)
    [dm] = wait([get_h2, get_up], dm)
    h2 = get_h2.value
    mixed, dgate, dup, sent, kept = hidden_rows(
        subs, spots, h2, get_gate.value, get_up.value, dm
    )

    add_dh2 = Transfer(team.scatter(sent, kept, True))
    start(add_dh2)
    send_down = across(team.add, mixed, dy, [16])
    wait([add_dh2])
    start(add_dh2, send_down)
    grad_gate = t_times(h2, dgate).astype(BF)
    [grad_gate] = wait([add_dh2], grad_gate)
    start(add_dh2)
    result_parts = products(subs, spots, mixed, down_rows)
    result_parts = [wait([], *part) for part in result_parts]
    wait([add_dh2, send_down])
    add_result = Transfer(team.scatter(*result_parts, False))
    start(add_dh2, add_result)
    wait([add_result])
    start(add_result)
    grad_up = t_times(h2, dup).astype(BF)
    [grad_up] = wait([add_dh2, add_result], grad_up)
    dx2, da = pair_back(here, x2, dy_pair, gain_two, add_dh2.value)
    get_da = Transfer(team.one(da, team.gather))
    send_gate = Transfer(team.owners(grad_gate))
    send_up = Transfer(team.owners(grad_up))
    start(get_da, send_gate)
    clock.ready(add_result, [get_da, send_gate])
    da = get_da.value
    start(send_up, add_result)
    dout = times_t(da, out_rows).astype(BF)
    dqkv, railed = attend_backward(size, subs, offsets, qe, ke, vs, out32, dout, cosine, sine)
    sent, kept = rail_products(railed, lambda v: times_t(v, w_qkv))
    dqkv, *sent = wait([add_result], dqkv, *sent)
    add_dh1 = Transfer(team.scatter(sent, kept, False))
    start(add_dh1)
    grad_qkv = t_times(h1, dqkv).astype(BF)
    [grad_qkv] = wait([add_dh1, send_up], grad_qkv)
    send_qkv = Transfer(team.owners(grad_qkv))
    start(add_dh1, add_result, send_qkv)
    grad_gate, share_gate = join_columns(send_gate.value, [w_gate], size, *ff_cut)
    [grad_gate] = wait([add_dh1, add_result], grad_gate)
    start(add_dh1)
    if whole_heads:
        send_out = across(team.add, out, da, [16])
        start(send_out)
    else:
        grad_out = lax.psum(
            t_times(out, da), "fsdp", axis_index_groups=[list(t) for t in zip(*team.groups)]
        )
        grad_out = lax.all_gather(
            grad_out, "fsdp", axis=0, tiled=True, axis_index_groups=team.groups
        )
        grad_out = lax.dynamic_slice_in_dim(grad_out, index * own, own)
    grad_up, share_up = join_columns(send_up.value, [w_up], size, *ff_cut)
    grad_gain_mlp = (share_gate + share_up)[:, 0] / gain_mlp.astype(F32)
    result = own_result(here, x2, add_result.value)
    grad_up, result = wait([add_dh1, send_qkv], grad_up, result)
    start(add_dh1)
    grads = join_columns(send_qkv.value, [w_query, w_key, w_value], size, *head_cut)
    if whole_heads:
        grads = wait([add_dh1, send_out], *grads)
        grad_out = send_out.value
    else:
        grads = wait([add_dh1], *grads)
    grad_query, grad_key, grad_value, share = grads
    grad_tokens = own_back(here, tokens, dx2, gain_one, add_dh1.value)
    grad_gain_attn = share[:, 0] / gain_attn.astype(F32)
    return (
        result,
        grad_tokens,
        grad_gain_attn,
        grad_query,
        grad_key,
        grad_value,
        grad_out,
        grad_gain_mlp,
        grad_gate,
        grad_up,
        send_down.value,
    )


def solution(mesh):
    flat = P("fsdp")
    wide = P("fsdp", None)
    return jax.shard_map(
        local,
        mesh=mesh,
        in_specs=(wide, flat, flat, flat, wide, wide, wide, wide, flat, wide, wide, wide, wide),
        out_specs=(wide, wide, flat, wide, wide, wide, wide, flat, wide, wide, wide),
        check_vma=False,
    )
```

```python
import functools

import jax
import jax.numpy as jnp
from jax import lax
from jax.experimental import pallas as pl
from jax.experimental.pallas import tpu as pltpu
from jax.sharding import PartitionSpec as P

HEADS = 32
HEAD_DIM = 64
SEQ = 2048
DOCS = 16


EPS = 1e-05
THETA = 130000.0
HIDE = -1e30
BF = jnp.bfloat16
F32 = jnp.float32
LANES = 2 * HEAD_DIM
HALF = HEAD_DIM // 2
BLOCK = 512
STEP = 1024
MIB = 2**20


def barrier(*values):
    return lax.optimization_barrier(values)


def norm_rows(v, gain):
    scale = lax.rsqrt(jnp.mean(v * v, axis=-1, keepdims=True) + EPS)
    return v * scale * gain


def matmul(left, right):
    return jnp.dot(left, right, preferred_element_type=F32)


def times_t(left, right):
    return lax.dot_general(left, right, (((1,), (1,)), ((), ())), preferred_element_type=F32)


def t_times(left, right):
    return lax.dot_general(left, right, (((0,), (0,)), ((), ())), preferred_element_type=F32)


def call(kernel, out_shape, in_specs, out_specs, vmem=56, grid=(), scratch=()):
    return pl.pallas_call(
        kernel,
        grid=grid,
        out_shape=out_shape,
        in_specs=in_specs,
        out_specs=out_specs,
        scratch_shapes=list(scratch),
        compiler_params=pltpu.CompilerParams(vmem_limit_bytes=vmem * MIB),
        cost_estimate=pl.CostEstimate(flops=2**26, bytes_accessed=2**20, transcendentals=0),
    )


LIKE = jax.ShapeDtypeStruct
IN_SMEM = pl.BlockSpec(memory_space=pltpu.SMEM)
IN_VMEM = pl.BlockSpec(memory_space=pltpu.VMEM)


def per_step(rows, columns):
    return pl.BlockSpec((rows, columns), lambda i: (i, 0))


def same(shape):
    return pl.BlockSpec(shape, lambda i: (0, 0))


def lane_index(shape):
    return lax.broadcasted_iota(jnp.int32, shape, len(shape) - 1)


def of_head(head, shape):
    return lane_index(shape) // HEAD_DIM == head


def swapped(v):
    first = lane_index(v.shape) % HEAD_DIM < HALF
    return jnp.where(first, pltpu.roll(v, LANES - HALF, 1), pltpu.roll(v, HALF, 1))


def parts_of(v):
    high = v.astype(BF)
    rest = v - high.astype(F32)
    mid = rest.astype(BF)
    return high, mid, (rest - mid.astype(F32)).astype(BF)


def in_lanes(columns, first, shape):
    lane = lane_index(shape)
    out = jnp.zeros(shape, BF)
    for c, column in enumerate(columns):
        out = jnp.where(lane == first + c, column, out)
    return out


def each_block(size, give):
    rows = SEQ // size

    def one(b, carry):
        q = (b % (size // 2)) * 2 + b // (size // 2)
        give(pl.ds(pl.multiple_of(b * rows, 128), rows), pl.ds(pl.multiple_of(q * rows, 128), rows))
        return carry

    lax.fori_loop(0, size, one, 0)


def each_piece(size, subs, offsets, give):
    rows = SEQ // size

    def one(b, carry):
        start = 0
        for r, sub in enumerate(subs):
            there = pl.ds(pl.multiple_of(offsets[r * size + b], 16), sub)
            give(pl.ds(pl.multiple_of(b * rows + start, 16), sub), there)
            start += sub
        return carry

    lax.fori_loop(0, size, one, 0)


def forward_kernel(
    size, subs, offsets, qkv, cosine, sine, q_mask, k_mask, qe, ke, vs, out, out32, railed
):
    def place(there, here):
        c, s = cosine[there, :], sine[there, :]
        for at, ends, mask in ((0, qe, q_mask), (1, ke, k_mask)):
            v = qkv[here, at * LANES : (at + 1) * LANES]
            turned = (v * c + swapped(v) * s).astype(BF)
            if at == 0:
                turned = turned * (HEAD_DIM**-0.5)
            hidden = mask[there, :]
            for head in range(2):
                ends[head, there, :] = jnp.where(of_head(head, turned.shape), turned, hidden)
        vs[there, :] = qkv[here, 2 * LANES :].astype(BF)

    each_block(size, place)
    shape = (BLOCK, LANES)
    diagonal = lax.broadcasted_iota(jnp.int32, (BLOCK, BLOCK), 0) >= lane_index((BLOCK, BLOCK))
    lane = lane_index(shape)
    for i in range(SEQ // BLOCK):
        mine = slice(i * BLOCK, (i + 1) * BLOCK)

        def one_head(head, carry):
            spare = (1 - head) * HEAD_DIM
            query = qe[head, mine, :]
            scores = []
            for j in range(i + 1):
                s = times_t(query, ke[head, j * BLOCK : (j + 1) * BLOCK, :])
                scores.append(jnp.where(diagonal, s, HIDE) if j == i else s)
            top = functools.reduce(jnp.maximum, scores)
            top = jnp.max(top, axis=1, keepdims=True)
            total = jnp.zeros(shape, F32)
            for j, s in enumerate(scores):
                probs = jnp.exp(s - top).astype(BF)
                value = vs[j * BLOCK : (j + 1) * BLOCK, :]
                value = jnp.where(of_head(head, shape), value, jnp.ones((), BF))
                total += matmul(probs, value)
            weight = jnp.sum(jnp.where(lane == spare, total, 0.0), axis=1, keepdims=True)
            before = jnp.where(head == 0, 0.0, out32[mine, :])
            out32[mine, :] = jnp.where(of_head(head, shape), total / weight, before)
            logsum = top + jnp.log(weight)
            qe[head, mine, :] = query + in_lanes(parts_of(-logsum), spare + HALF, shape)
            return carry

        lax.fori_loop(0, 2, one_head, 0)

    def send(there, here):
        out[here, :] = out32[there, :].astype(BF)

    def rail(there, here):
        railed[here, :] = out32[there, :].astype(BF)

    each_block(size, send)
    each_piece(size, subs, offsets, rail)


def backward_kernel(
    size,
    subs,
    offsets,
    qe,
    ke,
    vs,
    out32,
    dout,
    cosine,
    sine,
    grads,
    railed,
    de,
    dq,
    dk,
    dv,
    turned,
):
    def place(there, here):
        grad = dout[here, :]
        weighted = grad.astype(F32) * out32[there, :]
        for head in range(2):
            own = of_head(head, grad.shape)
            delta = jnp.sum(jnp.where(own, weighted, 0.0), axis=1, keepdims=True)
            extra = in_lanes(parts_of(-delta), (1 - head) * HEAD_DIM, grad.shape)
            de[head, there, :] = jnp.where(own, grad, extra)

    each_block(size, place)
    shape = (BLOCK, LANES)
    diagonal = lax.broadcasted_iota(jnp.int32, (BLOCK, BLOCK), 0) <= lane_index((BLOCK, BLOCK))
    lane = lane_index(shape)
    for head in range(2):
        spare = (1 - head) * HEAD_DIM
        ones = jnp.where((lane >= spare) & (lane < spare + 3), jnp.ones((), BF), jnp.zeros((), BF))
        for j in range(SEQ // BLOCK):
            theirs = slice(j * BLOCK, (j + 1) * BLOCK)
            key = ke[head, theirs, :]
            value = jnp.where(of_head(head, shape), vs[theirs, :], ones)
            dkey = jnp.zeros(shape, F32)
            dvalue = jnp.zeros(shape, F32)
            for i in range(j, SEQ // BLOCK):
                mine = slice(i * BLOCK, (i + 1) * BLOCK)
                query = qe[head, mine, :]
                grad = de[head, mine, :]
                probs = jnp.exp(times_t(key, query))
                if i == j:
                    probs = jnp.where(diagonal, probs, 0.0)
                dscore = (probs * times_t(value, grad)).astype(BF)
                dvalue += matmul(probs.astype(BF), grad)
                dkey += matmul(dscore, query)
                dquery = t_times(dscore, key)
                if j > 0:
                    dquery += dq[head, mine, :]
                dq[head, mine, :] = dquery
            dk[head, theirs, :] = dkey
            dv[head, theirs, :] = dvalue
    for i in range(SEQ // BLOCK):
        mine = slice(i * BLOCK, (i + 1) * BLOCK)
        c, s = cosine[mine, :], sine[mine, :]
        first = of_head(0, shape)
        query = jnp.where(first, dq[0, mine, :], dq[1, mine, :]) * (HEAD_DIM**-0.5)
        key = jnp.where(first, dk[0, mine, :], dk[1, mine, :])
        for at, v in ((0, query), (1, key)):
            back = v * c - swapped(v) * s
            turned[mine, at * LANES : (at + 1) * LANES] = back.astype(BF)
        value = jnp.where(first, dv[0, mine, :], dv[1, mine, :])
        turned[mine, 2 * LANES :] = value.astype(BF)

    def send(there, here):
        grads[here, :] = turned[there, :]

    def rail(there, here):
        railed[here, :] = turned[there, :]

    each_block(size, send)
    each_piece(size, subs, offsets, rail)


def attend_forward(size, subs, offsets, qkv, cosine, sine, q_mask, k_mask):
    return call(
        functools.partial(forward_kernel, size, subs),
        [
            LIKE((2, SEQ, LANES), BF),
            LIKE((2, SEQ, LANES), BF),
            LIKE((SEQ, LANES), BF),
            LIKE((SEQ, LANES), BF),
            LIKE((SEQ, LANES), F32),
            LIKE((SEQ, LANES), BF),
        ],
        [IN_SMEM] + [IN_VMEM] * 5,
        [IN_VMEM] * 6,
        vmem=48,
    )(offsets, qkv, cosine, sine, q_mask, k_mask)


def attend_backward(size, subs, offsets, qe, ke, vs, out32, dout, cosine, sine):
    return call(
        functools.partial(backward_kernel, size, subs),
        [LIKE((SEQ, 3 * LANES), BF)] * 2,
        [IN_SMEM] + [IN_VMEM] * 7,
        [IN_VMEM] * 2,
        scratch=[
            pltpu.VMEM((2, SEQ, LANES), BF),
            pltpu.VMEM((2, SEQ, LANES), F32),
            pltpu.VMEM((2, SEQ, LANES), F32),
            pltpu.VMEM((2, SEQ, LANES), F32),
            pltpu.VMEM((SEQ, 3 * LANES), BF),
        ],
    )(offsets, qe, ke, vs, out32, dout, cosine, sine)


def project_kernel(x, gain, w, h, out):
    h[...] = norm_rows(x[...].astype(F32), gain[...]).astype(BF)
    out[...] = matmul(h[...], w[...])


def norm_project(x, gain, w):
    rows, width = x.shape
    step, columns = STEP, w.shape[1]
    return call(
        project_kernel,
        [LIKE((rows, width), BF), LIKE((rows, columns), F32)],
        [per_step(step, width), same((1, width)), same((width, columns))],
        [per_step(step, width), per_step(step, columns)],
        grid=(rows // step,),
    )(x, gain, w)


def hand_out(subs, spots, product, sent, kept):
    rows = sum(subs)
    chips = SEQ // (2 * rows)
    pairs = product.shape[0] // (2 * rows)
    for j in range(pairs):
        pair = pl.program_id(0) * pairs + j
        core, chip = pair % 2, pair // 2
        for side, outs in ((spots[0], kept), (1 - spots[0], sent)):

            @pl.when(core == side)
            def _():
                for half in range(2):
                    start = (2 * j + half) * rows
                    for r, sub in enumerate(subs):
                        there = spots[1 + r * chips + half * (chips // 2) + chip]
                        there = pl.ds(pl.multiple_of(there, 16), sub)
                        outs[r][there, :] = product[start : start + sub]
                        start += sub


def hidden_kernel(subs, spots, h, w_gate, w_up, dm, mixed, dgate, dup, *outs):
    rails = len(subs)
    gate, up, grad = matmul(h[...], w_gate[...]), matmul(h[...], w_up[...]), dm[...]
    sig = 1.0 / (1.0 + jnp.exp(-gate))
    silu = gate * sig
    mixed[...] = (silu * up).astype(BF)
    dgate[...] = (grad * up * (sig + silu * (1.0 - sig))).astype(BF)
    dup[...] = (grad * silu).astype(BF)
    product = times_t(dgate[...], w_gate[...]) + times_t(dup[...], w_up[...])
    hand_out(subs, spots, product.astype(BF), outs[:rails], outs[rails:])


def hidden_rows(subs, spots, h, w_gate, w_up, dm):
    rows, width = h.shape
    hidden = dm.shape[1]
    step = STEP
    rails = [LIKE((rows // (2 * sum(subs)) * sub, width), BF) for sub in subs]
    made = call(
        functools.partial(hidden_kernel, subs),
        [LIKE((rows, hidden), BF)] * 3 + rails + rails,
        [IN_SMEM, per_step(step, width), same(w_gate.shape), same(w_up.shape), per_step(step, hidden)],
        [per_step(step, hidden)] * 3 + [IN_VMEM] * (2 * len(subs)),
        grid=(rows // step,),
    )(spots, h, w_gate, w_up, dm)
    return *made[:3], made[3 : 3 + len(subs)], made[3 + len(subs) :]


def product_kernel(subs, spots, left, right, *outs):
    product = matmul(left[...], right[...]).astype(BF)
    hand_out(subs, spots, product, outs[: len(subs)], outs[len(subs) :])


def products(subs, spots, left, right):
    rows, depth = left.shape
    width = right.shape[1]
    step = STEP
    rails = [LIKE((rows // (2 * sum(subs)) * sub, width), BF) for sub in subs]
    made = call(
        functools.partial(product_kernel, subs),
        rails + rails,
        [IN_SMEM, per_step(step, depth), same(right.shape)],
        [IN_VMEM] * (2 * len(subs)),
        vmem=24,
        grid=(rows // step,),
    )(spots, left, right)
    return made[: len(subs)], made[len(subs) :]


def fold_kernel(rails, last, *refs):
    held, got, outs = refs[:rails], refs[rails : 2 * rails], refs[2 * rails :]
    for r in range(rails):
        half = held[r].shape[0] // 2
        total = held[r][...].astype(F32) + got[r][...].astype(F32)
        outs[r][...] = total[half:].astype(BF)
        outs[rails + r][...] = total[:half]
        if last:
            outs[2 * rails + r][...] = total[:half].astype(BF)


def fold(held, got, last=False):
    rails, width = len(held), held[0].shape[1]
    step = width // 4

    def block(rows):
        return pl.BlockSpec((rows, step), lambda i: (0, i))

    halves = [v.shape[0] // 2 for v in held]
    kinds = [BF, F32] + [BF] * last
    made = call(
        functools.partial(fold_kernel, rails, last),
        [LIKE((h, width), kind) for kind in kinds for h in halves],
        [block(v.shape[0]) for v in (*held, *got)],
        [block(h) for kind in kinds for h in halves],
        vmem=16,
        grid=(4,),
    )(*held, *got)
    return [made[i : i + rails] for i in range(0, len(made), rails)]


def pair_rows(rails, half, refs):
    lower, came, upper, other = (refs[i * rails : (i + 1) * rails] for i in range(4))
    sub = lower[0].shape[0]
    for r in range(rails):
        for side, a, b in ((half, lower, came), (1 - half, upper, other)):
            at = pl.ds(pl.multiple_of(side * (rails * sub) + r * sub, 16), sub)
            yield at, a[r][...].astype(F32) + b[r][...].astype(F32)


def residual_kernel(rails, half, x, gain, *refs):
    sums, (x2, h) = refs[:-2], refs[-2:]
    for at, total in pair_rows(rails, half[0], sums):
        v = x[at, :].astype(F32) + total
        x2[at, :] = v
        h[at, :] = norm_rows(v, gain[...]).astype(BF)


def residual(half, x, gain, sums):
    return call(
        functools.partial(residual_kernel, len(sums) // 4),
        [LIKE(x.shape, F32), LIKE(x.shape, BF)],
        [IN_SMEM] + [IN_VMEM] * (2 + len(sums)),
        [IN_VMEM] * 2,
        vmem=24,
    )(half, x, gain, *sums)


def norm_back(v, gain, grad):
    scale = lax.rsqrt(jnp.mean(v * v, axis=-1, keepdims=True) + EPS)
    hat = v * scale
    weighted = gain * grad
    return scale * (weighted - hat * jnp.mean(hat * weighted, axis=-1, keepdims=True))


def pair_back_kernel(rails, half, v, base, gain, *refs):
    sums, (out, rounded) = refs[:-2], refs[-2:]
    for at, total in pair_rows(rails, half[0], sums):
        made = base[at, :].astype(F32) + norm_back(v[at, :], gain[...], total)
        out[at, :] = made
        rounded[at, :] = made.astype(BF)


def pair_back(half, v, base, gain, sums):
    return call(
        functools.partial(pair_back_kernel, len(sums) // 4),
        [LIKE(v.shape, F32), LIKE(v.shape, BF)],
        [IN_SMEM] + [IN_VMEM] * (3 + len(sums)),
        [IN_VMEM] * 2,
        vmem=32,
    )(half, v, base, gain, *sums)


def own_rows(rails, half, refs, rows):
    lower, came = refs[:rails], refs[rails : 2 * rails]
    sub = lower[0].shape[0]
    for r in range(rails):
        at = pl.ds(pl.multiple_of(half * rows + r * sub, 16), sub)
        yield slice(r * sub, (r + 1) * sub), at, lower[r][...] + came[r][...].astype(F32)


def own_back_kernel(rails, half, v, base, gain, *refs):
    sums, out = refs[:-1], refs[-1]
    for mine, at, total in own_rows(rails, half[0], sums, v.shape[0]):
        out[mine, :] = base[at, :] + norm_back(v[mine, :].astype(F32), gain[...], total)


def own_back(half, v, base, gain, sums):
    return call(
        functools.partial(own_back_kernel, len(sums) // 2),
        LIKE(v.shape, F32),
        [IN_SMEM] + [IN_VMEM] * (3 + len(sums)),
        IN_VMEM,
        vmem=24,
    )(half, v, base, gain, *sums)


def result_kernel(rails, half, base, *refs):
    sums, out = refs[:-1], refs[-1]
    for mine, at, total in own_rows(rails, half[0], sums, out.shape[0]):
        out[mine, :] = (base[at, :] + total).astype(BF)


def own_result(half, base, sums):
    rows, width = base.shape
    return call(
        functools.partial(result_kernel, len(sums) // 2),
        LIKE((rows // 2, width), BF),
        [IN_SMEM] + [IN_VMEM] * (1 + len(sums)),
        IN_VMEM,
        vmem=24,
    )(half, base, *sums)


def cut_kernel(size, first, each, blocks, *refs):
    out = refs[-1]
    for d in range(out.shape[0]):
        p, at = d % size, 0
        for w in refs[:-1]:
            for j in range(blocks):
                out[d, :, at : at + each] = w[:, first(j, p) : first(j, p) + each]
                at += each


def cut_columns(weights, count, size, first, each, blocks):
    rows = weights[0].shape[0]
    columns = each * blocks * len(weights)
    return call(
        functools.partial(cut_kernel, size, first, each, blocks),
        LIKE((count, rows, columns), BF),
        [IN_VMEM] * len(weights),
        IN_VMEM,
        vmem=32,
    )(*weights)


def join_kernel(size, first, each, blocks, v, *refs):
    parts = (len(refs) - 1) // 2
    weights, outs, share = refs[:parts], refs[parts:-1], refs[-1]
    along = jnp.zeros((v.shape[1], each), F32)
    for p in range(size):
        at = 0
        for w, out in zip(weights, outs):
            for j in range(blocks):
                total = v[p, :, at : at + each].astype(F32)
                for d in range(p + size, v.shape[0], size):
                    total += v[d, :, at : at + each].astype(F32)
                here = slice(first(j, p), first(j, p) + each)
                out[:, here] = total
                along += total * w[:, here].astype(F32)
                at += each
    share[...] = jnp.sum(along, axis=1, keepdims=True)


def join_columns(v, weights, size, first, each, blocks):
    rows = v.shape[1]
    made = call(
        functools.partial(join_kernel, size, first, each, blocks),
        [LIKE((rows, size * each * blocks), F32)] * len(weights) + [LIKE((rows, 1), F32)],
        [IN_VMEM] * (1 + len(weights)),
        [IN_VMEM] * (len(weights) + 1),
        vmem=32,
    )(v, *weights)
    return made


class Team:
    def __init__(self, rows, count):
        self.rows, self.count = rows, count
        self.size = SEQ // rows
        self.teams = count // self.size
        self.groups = [[t * self.size + p for p in range(self.size)] for t in range(self.teams)]
        each = self.size // 2
        self.halves = [[h * each + p for p in range(each)] for h in range(2 * self.teams)]
        axes = [2 << k for k in range(self.size.bit_length() - 2)]
        first, rest = axes[-1:], axes[:-1]
        self.rails = [tuple(first + rest[r:] + rest[:r]) for r in range(len(rest))]
        self.subs = (rows // len(rest),) * len(rest)

    def flip(self, mask):
        pairs = [(i, i ^ mask) for i in range(self.count)]
        return lambda v: lax.ppermute(v, "fsdp", pairs)

    def ahead(self, teams):
        step = teams * self.size
        pairs = [(i, (i + step) % self.count) for i in range(self.count)]
        return lambda v: lax.ppermute(v, "fsdp", pairs)

    def stay(self, v):
        return v

    def everywhere(self, v):
        return lax.all_to_all(v, "fsdp", 0, 0, tiled=True)

    def gather(self, v):
        return lax.all_gather(v, "fsdp", axis=0, tiled=True, axis_index_groups=self.halves)

    def spots(self, place):
        away = 2 * jnp.arange(self.size // 2, dtype=jnp.int32) ^ place
        out = []
        for rail, sub in zip(self.rails, self.subs):
            at = jnp.zeros_like(away)
            for k, mask in enumerate(rail):
                at = at + jnp.where(away & mask != 0, sub << k, 0)
            out.append(at)
        return jnp.stack(out).astype(jnp.int32)

    def offsets(self, place):
        starts = jnp.cumsum(jnp.array((0,) + self.subs[:-1], jnp.int32)) * (self.size // 2)
        chip = self.spots(place) + starts[:, None]
        other = (jnp.arange(2, dtype=jnp.int32) ^ place) & 1
        return (chip[:, :, None] + other * (SEQ // 2)).reshape(-1).astype(jnp.int32)

    def cut(self, v):
        out, start = [], 0
        for sub in self.subs:
            each = sub * self.size // 2
            out.append(v[start : start + each])
            start += each
        return out

    def one(self, v, move):
        [got] = yield [(v, move)]
        return got

    def pair_up(self, v, half):
        [got] = yield [(v, self.flip(self.size // 2))]
        return jnp.where(half == 0, jnp.concatenate([v, got]), jnp.concatenate([got, v]))

    def scatter(self, sent, kept, pair):
        held, got = kept, (yield [(s, self.flip(1)) for s in sent])
        for step in reversed(range(1, len(self.rails[0]))):
            upper, held = fold(held, got)
            got = yield [(u, self.flip(rail[step])) for u, rail in zip(upper, self.rails)]
        upper, held, rounded = fold(held, got, last=True)
        move = self.flip(self.size // 2)
        if not pair:
            got = yield [(u, move) for u in upper]
            return [*held, *got]
        got = yield [(u, move) for u in (*upper, *rounded)]
        return [*held, *got[: len(held)], *upper, *got[len(held) :]]

    def spread(self, block, chunks, mine):
        got, start = [[] for _ in range(self.teams)], 0
        for chunk in chunks:
            each = block.shape[0] * chunk // 16
            part = block[start : start + each]
            start += each
            new = yield [(part, self.ahead(s)) for s in range(1, self.teams)]
            for s, piece in enumerate(new):
                got[s + 1].append(piece)
        held = jnp.zeros((self.teams,) + block.shape, block.dtype)
        held = lax.dynamic_update_index_in_dim(held, block, mine, 0)
        for s in range(1, self.teams):
            at, start = (mine - s) % self.teams, 0
            for piece in got[s]:
                held = lax.dynamic_update_slice(held, piece[None], (at, start, 0))
                start += piece.shape[0]
        return held.reshape((-1,) + block.shape[1:])

    def columns(self, cut):
        [got] = yield [(cut, self.everywhere)]
        return got.reshape(-1, got.shape[2])

    def owners(self, made):
        [got] = yield [(made.reshape(self.count, -1, made.shape[1]), self.everywhere)]
        return got

    def add(self, left, right, chunks, mine):
        width = left.shape[1] // self.teams

        def product(team):
            return t_times(lax.dynamic_slice_in_dim(left, team * width, width, 1), right)

        sent = [product((mine + s) % self.teams).astype(BF) for s in range(1, self.teams)]
        got, start = [[] for _ in sent], 0
        for chunk in chunks:
            each = width * chunk // 16
            moves = [(v[start : start + each], self.ahead(s + 1)) for s, v in enumerate(sent)]
            start += each
            if start == width:
                *new, total = yield moves + [(product(mine), self.stay)]
            else:
                new = yield moves
            for s, piece in enumerate(new):
                got[s].append(piece)
        for pieces in got:
            total = total + jnp.concatenate(pieces).astype(F32)
        return total


class Transfer:
    def __init__(self, steps):
        self.steps, self.value, self.over, self.got = steps, None, False, None
        self.moves = next(steps)

    def take(self):
        got, self.got = self.got, None
        try:
            self.moves = self.steps.send(got)
        except StopIteration as end:
            self.value, self.over, self.moves = end.value, True, []


class Clock:
    def __init__(self, token):
        self.token = token

    def start(self, *transfers):
        for t in transfers:
            t.got = [move(barrier(self.token, v)[1]) for v, move in t.moves]

    def start_together(self, *transfers):
        given = [v for t in transfers for v, _ in t.moves]
        given = list(barrier(self.token, *given)[1:])
        for t in transfers:
            t.got = [move(given.pop(0)) for _, move in t.moves]

    def beside(self, transfer, *values):
        tied = list(barrier(*values, *[v for v, _ in transfer.moves]))
        values, rest = tied[: len(values)], tied[len(values) :]
        transfer.moves = [(v, move) for v, (_, move) in zip(rest, transfer.moves)]
        return values

    def ready(self, transfer, transfers):
        made = self.wait(transfers, *[v for v, _ in transfer.moves])
        transfer.moves = [(v, move) for v, (_, move) in zip(made, transfer.moves)]

    def wait(self, transfers, *values):
        tied = list(barrier(self.token, *values, *[g for t in transfers for g in t.got]))
        self.token, values, rest = tied[0], tied[1 : 1 + len(values)], tied[1 + len(values) :]
        for t in transfers:
            t.got = [rest.pop(0) for _ in t.got]
        for t in transfers:
            t.take()
        return values


def local(
    tokens,
    segments,
    positions,
    gain_attn,
    w_query,
    w_key,
    w_value,
    w_out,
    gain_mlp,
    w_gate,
    w_up,
    w_down,
    cotangent,
):
    rows, width = tokens.shape
    count = lax.axis_size("fsdp")
    team = Team(rows, count)
    size, teams = team.size, team.teams
    index = lax.axis_index("fsdp")
    mine = index // size
    place = index % size
    own = w_query.shape[0]
    whole_heads = own % HEAD_DIM == 0
    ff_own = w_down.shape[0]
    if whole_heads:
        head_cut = (lambda j, p: (j * size + p) * HEAD_DIM, HEAD_DIM, 2)
    else:
        head_cut = (lambda j, p: p * LANES, LANES, 1)
    ff_cut = (lambda j, p: (j * size + p) * ff_own, ff_own, teams)

    def across(move, *args):
        return Transfer(move(*args, mine))

    clock = Clock(positions)
    start, wait = clock.start, clock.wait
    half = place // (size // 2)
    subs = team.subs

    pair_x = Transfer(team.pair_up(tokens, half))
    pair_dy = Transfer(team.pair_up(cotangent, half))
    start(pair_x)
    cut_qkv = cut_columns([w_query, w_key, w_value], count, size, *head_cut)
    [cut_qkv] = wait([pair_x], cut_qkv)
    x_pair = pair_x.value
    get_qkv = Transfer(team.columns(cut_qkv))
    get_x = Transfer(team.one(x_pair, team.gather))
    clock.start_together(get_x, get_qkv, pair_dy)
    cut_gate = cut_columns([w_gate], count, size, *ff_cut)
    cut_up = cut_columns([w_up], count, size, *ff_cut)
    small = jnp.concatenate([v.astype(F32) for v in (gain_attn, gain_mlp, segments, positions)])
    small = jnp.broadcast_to(small[None], (count, small.shape[0]))
    small = Transfer(team.one(small, team.everywhere))
    cut_gate, cut_up = wait([pair_dy, get_qkv], cut_gate, cut_up)
    dy_pair = pair_dy.value
    get_dy = Transfer(team.one(dy_pair, team.gather))
    get_gate = Transfer(team.columns(cut_gate))
    get_up = Transfer(team.columns(cut_up))
    get_down = across(team.spread, w_down, [16])
    start(get_gate, small, get_dy)
    moving = []
    if whole_heads:
        get_out = across(team.spread, w_out, [16])
        start(get_out)
        moving.append(get_out)
    wait([small])
    small = small.value
    gain_one = small[:, :own].reshape(1, -1)
    gain_two = small[:, own : 2 * own].reshape(1, -1)
    small = lax.dynamic_slice_in_dim(small, mine * size, size, 0)
    docs = small[:, 2 * own : 2 * own + rows].reshape(SEQ, 1)
    places = small[:, 2 * own + rows :].reshape(SEQ, 1)
    freqs = THETA ** (-jnp.arange(HALF, dtype=F32) * 2.0 / HEAD_DIM)
    angles = places * freqs[None, :]
    cosine, sine = jnp.cos(angles), jnp.sin(angles)
    cosine = jnp.concatenate([cosine] * 4, axis=1)
    sine = jnp.concatenate([-sine, sine] * 2, axis=1)
    lane = jnp.arange(LANES)[None, :] % HEAD_DIM
    number = lane.astype(F32)
    q_mask = jnp.where((lane < DOCS) & (docs != number), HIDE, 0.0).astype(BF)
    tail = (lane >= HALF) & (lane < HALF + 3)
    k_mask = jnp.where(((lane < DOCS) & (docs == number)) | tail, 1.0, 0.0).astype(BF)
    offsets = team.offsets(place)
    spots = jnp.concatenate([place[None] % 2, team.spots(place).reshape(-1)]).astype(jnp.int32)
    here = half[None].astype(jnp.int32)
    cosine, sine, q_mask, k_mask, gain_one, gain_two, offsets, spots = wait(
        moving, cosine, sine, q_mask, k_mask, gain_one, gain_two, offsets, spots
    )
    w_qkv = get_qkv.value
    if whole_heads:
        out_rows = get_out.value
    else:
        out_rows = lax.dynamic_slice_in_dim(
            lax.all_gather(w_out, "fsdp", axis=0, tiled=True), place * LANES, LANES
        )
    [w_qkv] = wait([get_x], w_qkv)
    h1, qkv = norm_project(get_x.value, gain_one, w_qkv)
    qe, ke, vs, out, out32, railed = attend_forward(
        size, subs, offsets, qkv, cosine, sine, q_mask, k_mask
    )
    [railed] = wait([], railed)

    def rail_products(left, times):
        cut = team.cut(left[: SEQ // 2]), team.cut(left[SEQ // 2 :])
        return [times(v).astype(BF) for v in cut[1]], [times(v).astype(BF) for v in cut[0]]

    sent, kept = rail_products(railed, lambda v: matmul(v, out_rows))
    sent = wait([], *sent)
    add_out = Transfer(team.scatter(sent, kept, True))
    start(add_out)
    wait([add_out, get_gate])
    start(add_out, get_down)
    wait([add_out])
    start(add_out)
    wait([add_out, get_down])
    start(add_out)
    wait([add_out])
    x2, h2 = residual(here, x_pair, gain_two, add_out.value)
    get_h2 = Transfer(team.one(h2, team.gather))
    start(get_h2, get_up)
    wait([get_dy])
    dy, down_rows = get_dy.value, get_down.value
    dm = times_t(dy, down_rows)
    [dm] = wait([get_h2, get_up], dm)
    h2 = get_h2.value
    mixed, dgate, dup, sent, kept = hidden_rows(
        subs, spots, h2, get_gate.value, get_up.value, dm
    )

    add_dh2 = Transfer(team.scatter(sent, kept, True))
    start(add_dh2)
    send_down = across(team.add, mixed, dy, [14, 2])
    wait([add_dh2])
    start(add_dh2, send_down)
    grad_gate = t_times(h2, dgate).astype(BF)
    [grad_gate] = wait([add_dh2], grad_gate)
    start(add_dh2)
    result_parts = products(subs, spots, mixed, down_rows)
    result_parts = [wait([], *part) for part in result_parts]
    wait([add_dh2, send_down])
    add_result = Transfer(team.scatter(*result_parts, False))
    start(add_dh2, add_result)
    wait([add_result])
    start(add_result)
    grad_up = t_times(h2, dup).astype(BF)
    [grad_up] = wait([add_dh2, add_result], grad_up)
    dx2, da = pair_back(here, x2, dy_pair, gain_two, add_dh2.value)
    get_da = Transfer(team.one(da, team.gather))
    send_gate = Transfer(team.owners(grad_gate))
    send_up = Transfer(team.owners(grad_up))
    start(get_da, send_gate, send_down)
    clock.ready(add_result, [get_da, send_gate, send_down])
    da = get_da.value
    start(send_up, add_result)
    dout = times_t(da, out_rows).astype(BF)
    dqkv, railed = attend_backward(size, subs, offsets, qe, ke, vs, out32, dout, cosine, sine)
    sent, kept = rail_products(railed, lambda v: times_t(v, w_qkv))
    dqkv, *sent = wait([add_result], dqkv, *sent)
    add_dh1 = Transfer(team.scatter(sent, kept, False))
    start(add_dh1)
    grad_qkv = t_times(h1, dqkv).astype(BF)
    [grad_qkv] = wait([add_dh1, send_up], grad_qkv)
    send_qkv = Transfer(team.owners(grad_qkv))
    start(add_dh1, add_result, send_qkv)
    grad_gate, share_gate = join_columns(send_gate.value, [w_gate], size, *ff_cut)
    [grad_gate] = wait([add_dh1, add_result], grad_gate)
    start(add_dh1)
    if whole_heads:
        send_out = across(team.add, out, da, [16])
        start(send_out)
    else:
        grad_out = lax.psum(
            t_times(out, da), "fsdp", axis_index_groups=[list(t) for t in zip(*team.groups)]
        )
        grad_out = lax.all_gather(
            grad_out, "fsdp", axis=0, tiled=True, axis_index_groups=team.groups
        )
        grad_out = lax.dynamic_slice_in_dim(grad_out, index * own, own)
    grad_up, share_up = join_columns(send_up.value, [w_up], size, *ff_cut)
    grad_gain_mlp = (share_gate + share_up)[:, 0] / gain_mlp.astype(F32)
    result = own_result(here, x2, add_result.value)
    grad_up, result = wait([add_dh1, send_qkv], grad_up, result)
    start(add_dh1)
    grads = join_columns(send_qkv.value, [w_query, w_key, w_value], size, *head_cut)
    if whole_heads:
        grads = wait([add_dh1, send_out], *grads)
        grad_out = send_out.value
    else:
        grads = wait([add_dh1], *grads)
    grad_query, grad_key, grad_value, share = grads
    grad_tokens = own_back(here, tokens, dx2, gain_one, add_dh1.value)
    grad_gain_attn = share[:, 0] / gain_attn.astype(F32)
    return (
        result,
        grad_tokens,
        grad_gain_attn,
        grad_query,
        grad_key,
        grad_value,
        grad_out,
        grad_gain_mlp,
        grad_gate,
        grad_up,
        send_down.value,
    )


def solution(mesh):
    flat = P("fsdp")
    wide = P("fsdp", None)
    return jax.shard_map(
        local,
        mesh=mesh,
        in_specs=(wide, flat, flat, flat, wide, wide, wide, wide, flat, wide, wide, wide, wide),
        out_specs=(wide, wide, flat, wide, wide, wide, wide, flat, wide, wide, wide),
        check_vma=False,
    )
```
